32 devices in a mesh: rep: 2 (over x), store: 8 (over z, y), tp: 2 (over core).
Axes of the slice: x: 2, y: 2, z: 4, core: 2. Of those that a mesh axis runs over, the one named last changes fastest.
Arguments:
- hidden: bfloat16 [8192, 8192], P(('rep', 'store'), 'tp'), parts along dimension 0, may hold values from -6 to 6
- queries: bfloat16 [8192, 32, 128], P(('rep', 'store'), 'tp'), parts along dimension 0, may hold values from -20 to 20
- kv_weight: bfloat16 [8192, 2, 4, 128], P('tp'), may hold values from -0.0625 to 0.0625
- kv_pool: bfloat16 [640, 4, 2, 128, 128], P(('rep', 'store'), 'tp'), parts along dimension 0, may hold values from -4 to 5
- hit_ids: int32 [32, 16], P(('rep', 'store')), parts along dimension 0, may hold values from 0 to 319, as said below
- hit_counts: int32 [32], P(('rep', 'store')), parts along dimension 0, may hold values from 8 to 16, as said below
- new_lengths: int32 [32], P(('rep', 'store')), parts along dimension 0, may hold values from 1 to 256
- dest_store: int32 [32, 2], P(('rep', 'store')), parts along dimension 0, may hold values from 0 to 7, as said below
Outputs:
- attention: bfloat16 [8192, 32, 128], P(('rep', 'store'), 'tp'), parts along dimension 0
- written: bfloat16 [16, 8, 2, 4, 2, 128, 128], P(('rep', 'store'), None, None, 'tp'), parts along dimension 0
The draws below stay inside these ranges and needn't reach their ends.
There are 2 independent parts, one for each index of `rep`. The reference program is written for one: setup_inputs(seed, part) draws one part's arguments, and reference() takes and returns one part's arrays. A program takes and returns all parts, laid end to end along the dimension named above; an argument that names none is the same for every part. Nothing has to cross between parts.
Inputs may be any that keep to these rules, and one draw needn't show every extreme that they name: `hit_ids`: an id names store id // 40, row id % 40 of that store's pool. Among the first hit_counts entries of the 2 sessions of one store device, at most 8 name one store, and exactly 8 name some store. `hit_counts`: session 0 has 16. `dest_store`: of the 4 new blocks of one store device, at most 2 go to one store, exactly 2 to some store.
All inputs are finite; a program needn't handle non-finite values.
Results may differ from the reference program's by a relative error of at most 0.0048.
Values may be sent and summed in bfloat16 or wider, within the bound.
No kernel may reach another device: no remote copies, remote signals or barrier semaphores. Data moves between devices by JAX's collectives and lax.ppermute only.
A program may use at most 192 MiB of HBM per device.

```python
import math
import jax
import jax.numpy as jnp
from jax import lax

D = 8192
HD = 128
KVH = 4
QH = 32
BLK = 128
NEW = 256
HIT = 16
SES_DEV = 2
WCAP = 2
BLK_DEV = 40
GROUP = 8
NB = 2
SESSIONS = 16
TOKENS = 4096
NBLK = 320
CAP = 8
N_STORE = 8


def pick_stores(key, store_count, most, taken):
    entries = jnp.arange(store_count * most, dtype=jnp.int32) // most
    first_key, second_key = jax.random.split(key)
    chosen = jax.random.randint(first_key, (), 0, store_count)
    shuffle = jax.random.permutation(second_key, store_count * most).astype(jnp.int32)
    ranking = jnp.where(entries == chosen, jnp.arange(store_count * most, dtype=jnp.int32) - store_count * most, shuffle)
    return entries[jnp.argsort(ranking)][:taken]


def draw_queries(key, part):
    key = jax.random.fold_in(key, 11)
    values = jnp.clip(jax.random.normal(key, (TOKENS, QH, HD), jnp.float32), -4.0, 4.0)
    return values.astype(jnp.bfloat16)


def draw_kv_pool(key, part):
    key = jax.random.fold_in(key, 13)
    values = jnp.clip(jax.random.normal(key, (NBLK, KVH, 2, BLK, HD), jnp.float32), -4.0, 4.0)
    return values.astype(jnp.bfloat16)


def draw_hit_ids(key, part):
    key = jax.random.fold_in(key, 5)
    owner_keys = jax.random.split(key, N_STORE)
    stores = jax.vmap(lambda one_key: pick_stores(one_key, N_STORE, CAP, SES_DEV * HIT))(owner_keys)
    pool_rows = jax.random.randint(jax.random.fold_in(key, 1), (N_STORE, SES_DEV * HIT), 0, BLK_DEV)
    return (stores * BLK_DEV + pool_rows).reshape(SESSIONS, HIT).astype(jnp.int32)


def draw_hit_counts(key, part):
    key = jax.random.fold_in(key, 7)
    counts = jax.random.randint(key, (SESSIONS,), max(CAP, HIT // 2), HIT + 1)
    return counts.at[0].set(HIT).astype(jnp.int32)


def draw_dest_store(key, part):
    key = jax.random.fold_in(key, 9)
    device_keys = jax.random.split(key, N_STORE)
    stores = jax.vmap(lambda one_key: pick_stores(one_key, N_STORE, WCAP, SES_DEV * NB))(device_keys)
    return stores.reshape(SESSIONS, NB).astype(jnp.int32)


def set_ends(drawn, key, low, top_value):
    longest = drawn.shape.index(max(drawn.shape))
    spots = []
    for shift in (0, 1):
        where = [jax.random.randint(jax.random.fold_in(key, axis), (), 0, length) for axis, length in enumerate(drawn.shape)]
        where[longest] = (where[longest] + shift) % drawn.shape[longest]
        spots.append(tuple(where))
    return drawn.at[spots[0]].set(low).at[spots[1]].set(top_value)


def block_scale(own_key, shape, shards, least, largest):
    def one(axis_at, blocks):
        heights = jax.random.uniform(jax.random.fold_in(jax.random.fold_in(own_key, 6), axis_at), (blocks,), jnp.float32, least / len(shards), largest / len(shards))
        return jnp.repeat(jnp.exp(heights), shape[axis_at] // blocks).reshape((-1,) + (1,) * (len(shape) - axis_at - 1))

    gain = one(*shards[0])
    for cut in shards[1:]:
        gain = gain * one(*cut)
    return gain


def centred(own_key, shape, scale, reach, cuts=(), kind=jnp.bfloat16):
    values = scale * jax.random.normal(own_key, shape, jnp.float32)
    if cuts:
        values = values * block_scale(own_key, shape, cuts, -0.22, 0.18)
    return jnp.clip(values, -reach, reach).astype(kind)


def setup_inputs(seed: int = 0, part: int = 0) -> dict:
    splits = jax.random.split(jax.random.key(seed), 9)
    own_keys = jax.random.split(jax.random.fold_in(splits[8], part), 9)
    return {
        "hidden": centred(own_keys[0], (TOKENS, D), 1.0, 6.0, ((0, 8), (1, 2))),
        "queries": draw_queries(jax.random.fold_in(jax.random.fold_in(splits[8], part), 71), part),
        "kv_weight": centred(splits[2], (D, 2, KVH, HD), D ** -0.5, 0.0625, ((0, 2),)),
        "kv_pool": draw_kv_pool(jax.random.fold_in(jax.random.fold_in(splits[8], part), 71), part),
        "hit_ids": draw_hit_ids(jax.random.fold_in(jax.random.fold_in(splits[8], part), 71), part),
        "hit_counts": draw_hit_counts(jax.random.fold_in(jax.random.fold_in(splits[8], part), 71), part),
        "new_lengths": set_ends(jax.random.randint(own_keys[6], (SESSIONS,), 1, NEW + 1), jax.random.fold_in(own_keys[6], 1), 1, NEW).astype(jnp.int32),
        "dest_store": draw_dest_store(jax.random.fold_in(jax.random.fold_in(splits[8], part), 71), part),
    }


theta_base = 500000.0

def rotate(keys, positions):
    half = keys.shape[-1] // 2
    steps = jnp.arange(half, dtype=jnp.float32)
    inverse = jnp.exp(steps * (-2.0 * math.log(theta_base) / keys.shape[-1]))
    angles = positions[:, None] * inverse[None, :]
    cosine = jnp.cos(angles)
    sine = jnp.sin(angles)
    first = keys[..., :half]
    second = keys[..., half:]
    return jnp.concatenate([first * cosine - second * sine, second * cosine + first * sine], axis=-1)

def attend(query_rows, pre_keys, pre_vals, new_keys, new_vals, hit_total, length, score_scale):
    keys_all = jnp.concatenate([pre_keys, new_keys], axis=0).astype(jnp.float32)
    vals_all = jnp.concatenate([pre_vals, new_vals], axis=0).astype(jnp.float32)
    scores = jnp.einsum('tgd,kd->gtk', query_rows.astype(jnp.float32), keys_all) * score_scale
    new_count = new_keys.shape[0]
    pre_count = pre_keys.shape[0]
    query_pos = jnp.arange(new_count, dtype=jnp.int32)
    pre_ok = jnp.broadcast_to((jnp.arange(pre_count, dtype=jnp.int32) < hit_total * BLK)[None, :], (new_count, pre_count))
    new_ok = query_pos[None, :] <= query_pos[:, None]
    allowed = jnp.concatenate([pre_ok, new_ok], axis=1)
    scores = jnp.where(allowed[None], scores, -jnp.inf)
    peak = lax.optimization_barrier(jnp.max(scores, axis=-1, keepdims=True))
    weights = jnp.exp(scores - peak)
    totals = lax.optimization_barrier(jnp.sum(weights, axis=-1, keepdims=True))
    rounded = lax.optimization_barrier(weights.astype(jnp.bfloat16))
    mixed = jnp.einsum('gtk,kd->gtd', rounded.astype(jnp.float32), vals_all) / totals
    mixed = jnp.where((query_pos < length)[None, :, None], mixed, 0.0)
    return jnp.transpose(mixed, (1, 0, 2)).astype(jnp.bfloat16)

def reference(hidden, queries, kv_weight, kv_pool, hit_ids, hit_counts, new_lengths, dest_store):
    projected = jnp.einsum('ta,abhd->hbtd', hidden.astype(jnp.float32), kv_weight.astype(jnp.float32))
    token_ids = jnp.arange(TOKENS, dtype=jnp.int32)
    within = token_ids % NEW
    start_pos = jnp.repeat(hit_counts, NEW, total_repeat_length=TOKENS)
    live_len = jnp.repeat(new_lengths, NEW, total_repeat_length=TOKENS)
    places = (start_pos * BLK + within).astype(jnp.float32)
    rotated = rotate(projected[:, 0], places)
    fresh_kv = jnp.stack([rotated, projected[:, 1]], axis=1).astype(jnp.bfloat16)
    fresh_kv = jnp.where((within < live_len)[None, None, :, None], fresh_kv, jnp.zeros((), jnp.bfloat16))
    score_scale = 1.0 / math.sqrt(HD)

    def one_session(session):
        blocks = jnp.take(kv_pool, hit_ids[session], axis=0)
        query_rows = lax.dynamic_slice_in_dim(queries, session * NEW, NEW, 0)
        new_part = lax.dynamic_slice_in_dim(fresh_kv, session * NEW, NEW, 2)
        pieces = []
        for kv_head in range(KVH):
            pieces.append(attend(query_rows[:, kv_head * GROUP:(kv_head + 1) * GROUP], blocks[:, kv_head, 0].reshape(HIT * BLK, HD), blocks[:, kv_head, 1].reshape(HIT * BLK, HD), new_part[kv_head, 0], new_part[kv_head, 1], hit_counts[session], new_lengths[session], score_scale))
        return jnp.concatenate(pieces, axis=1)
    attention = lax.map(one_session, jnp.arange(SESSIONS, dtype=jnp.int32)).reshape(TOKENS, QH, HD)
    per_dev = SES_DEV * NB
    dest = dest_store.reshape(N_STORE, per_dev)
    order_ids = jnp.arange(per_dev, dtype=jnp.int32)
    earlier = (dest[:, None, :] == dest[:, :, None]) & (order_ids[None, None, :] < order_ids[None, :, None])
    dest_rank = lax.optimization_barrier(jnp.sum(earlier.astype(jnp.int32), axis=2))
    blocks_out = fresh_kv.reshape(KVH, 2, N_STORE, per_dev, BLK, HD).transpose(2, 3, 0, 1, 4, 5)
    senders = jnp.broadcast_to(jnp.arange(N_STORE, dtype=jnp.int32)[:, None], dest.shape)
    written = jnp.zeros((N_STORE, N_STORE, WCAP, KVH, 2, BLK, HD), jnp.bfloat16)
    written = written.at[dest, senders, dest_rank].set(blocks_out)
    return (attention, written)
```

```python
import functools
import math

import jax
import jax.numpy as jnp
from jax import lax
from jax.experimental import pallas as pl
from jax.experimental.pallas import tpu as pltpu
from jax.sharding import PartitionSpec as P

WCAP = 2
STEP = 2
LAG = 2
BASE_STEPS = 20
NEW_STEP = 8

theta_base = 500000.0

SPAN = 1 << 16
POOL, FRESH, FROM_Y, FROM_LEFT, FROM_RIGHT = range(5)


def rotate(keys, positions):
    half = keys.shape[-1] // 2
    steps = jnp.arange(half, dtype=jnp.float32)
    inverse = jnp.exp(steps * (-2.0 * math.log(theta_base) / keys.shape[-1]))
    angles = positions[:, None] * inverse[None, :]
    cosine = jnp.cos(angles)
    sine = jnp.sin(angles)
    first = keys[..., :half]
    second = keys[..., half:]
    return jnp.concatenate(
        [first * cosine - second * sine, second * cosine + first * sine], axis=-1
    )


class Plan:
    def __init__(self, store_count, ses_count, hit_len, per_dev, pool_rows):
        self.stores = store_count
        self.ny = 2 if store_count % 2 == 0 else 1
        self.nz = store_count // self.ny
        self.ses = ses_count
        self.hit_len = hit_len
        self.hits = ses_count * hit_len
        self.per_dev = per_dev
        self.pool_rows = pool_rows
        self.cap = 2 * ((self.hits + store_count - 1) // store_count)
        self.width = self.hits + ses_count + per_dev
        ny, nz = self.ny, self.nz
        wait = LAG * STEP
        line = sum(min(self.hits, self.cap * ny * k) for k in range(1, nz))
        line += per_dev * ny * (nz - 1)
        self.line_slots = line + wait * (nz + 1) + NEW_STEP * STEP
        cross = nz * self.cap + per_dev + NEW_STEP * STEP
        self.y_slots = cross
        up = 2 * STEP
        self.line_slots = -(-self.line_slots // up) * up + up
        self.y_slots = -(-self.y_slots // up) * up + up
        self.slots = max(self.line_slots, self.y_slots, BASE_STEPS * STEP + up)

    def y_index(self, column, kind, z, zp):
        return ((column * 2 + kind) * self.nz + z) * self.nz + zp

    def line_index(self, z, kind, zs, ys, zp):
        return (((z * 2 + kind) * self.nz + zs) * self.ny + ys) * self.nz + zp


def schedule_kernel(
    plan, me_ref, meta, table, places, arrivals, total, cnt, rows, ranks, ybase, rbase, lbase
):
    S, ny, nz = plan.stores, plan.ny, plan.nz
    wait = LAG * STEP
    me = me_ref[0]
    my_z = me // ny
    my_y = me - my_z * ny
    stride = plan.cap + 1

    def count_at(kind, dst, src):
        return (kind * S + dst) * S + src

    def row_at(kind, dst, src, rank):
        return count_at(kind, dst, src) * stride + rank

    def clear(i, c):
        cnt[i] = 0
        return c

    lax.fori_loop(0, 2 * S * S, clear, 0)

    def clear_table(i, c):
        for link in range(3):
            table[link * plan.slots + i] = -1
        return c

    lax.fori_loop(0, plan.slots, clear_table, 0)

    def scan(d, c):
        base = d * plan.width
        for t in range(plan.ses):
            used = meta[base + plan.hits + t]
            for j in range(plan.hit_len):
                block = meta[base + t * plan.hit_len + j]
                store = lax.div(block, plan.pool_rows)
                at = count_at(0, d, store)
                rank = cnt[at]
                rows[at * stride + jnp.minimum(rank, plan.cap)] = block - store * plan.pool_rows
                ranks[d * plan.hits + t * plan.hit_len + j] = rank
                cnt[at] = rank + (j < used).astype(jnp.int32)
        for j in range(plan.per_dev):
            dest = meta[base + plan.hits + plan.ses + j]
            at = count_at(1, dest, d)
            rank = cnt[at]
            rows[at * stride + jnp.minimum(rank, plan.cap)] = j
            cnt[at] = rank + 1
        return c

    lax.fori_loop(0, S, scan, 0)

    longest = jnp.int32(0)
    if ny == 2:
        for column in range(2):
            into = my_y if column == 0 else 1 - my_y
            for z in range(nz):
                cur = jnp.int32(0)
                for kind in range(2):
                    if kind == 1:
                        cur = jnp.maximum(cur, NEW_STEP * STEP)
                    for zp in sorted(range(nz), key=lambda q: -abs(q - z)):
                        ybase[plan.y_index(column, kind, z, zp)] = cur
                        n = cnt[count_at(kind, zp * ny + into, z * ny + 1 - into)]
                        cur = cur + n
                        longest = jnp.where(n > 0, jnp.maximum(longest, cur), longest)

    for bases, ahead in ((rbase, 1), (lbase, -1)):
        for z in range(nz - 1) if ahead == 1 else range(nz - 1, 0, -1):
            cur = jnp.int32(0)
            for kind in range(2):
                back = z
                while 0 <= back < nz:
                    for ys in range(ny):
                        targets = range(nz - 1, z, -1) if ahead == 1 else range(0, z)
                        for zp in targets:
                            src = back * ny + (my_y if ys == 0 else 1 - my_y)
                            n = cnt[count_at(kind, zp * ny + my_y, src)]
                            if back != z:
                                before = bases[plan.line_index(z - ahead, kind, back, ys, zp)]
                                ready = before + wait
                            elif ys == 1:
                                ready = ybase[plan.y_index(0, kind, z, zp)] + wait
                            else:
                                ready = jnp.int32(NEW_STEP * STEP if kind == 1 else 0)
                            start = jnp.maximum(cur, ready)
                            bases[plan.line_index(z, kind, back, ys, zp)] = start
                            cur = jnp.where(n > 0, start + n, cur)
                    back -= ahead
            longest = jnp.maximum(longest, cur)
    total[0] = longest

    def own_code(kind, dst, i):
        return (POOL if kind == 0 else FRESH) * SPAN + rows[row_at(kind, dst, me, i)]

    def fill(link, start, n, code_of):
        def put(i, c):
            table[link * plan.slots + start + i] = code_of(i)
            return c

        lax.fori_loop(0, n, put, 0)

    for kind in range(2):
        if ny == 2:
            for zp in range(nz):
                dst = zp * ny + 1 - my_y
                fill(
                    0,
                    ybase[plan.y_index(1, kind, my_z, zp)],
                    cnt[count_at(kind, dst, me)],
                    lambda i, kind=kind, dst=dst: own_code(kind, dst, i),
                )
        for link, bases, ahead, origin in ((1, rbase, 1, FROM_LEFT), (2, lbase, -1, FROM_RIGHT)):
            low = my_z + 1 if ahead == 1 else 0
            high = nz if ahead == 1 else my_z

            def each_target(zp, c, kind=kind, link=link, bases=bases, ahead=ahead, origin=origin):
                dst = zp * ny + my_y
                for ys in range(ny):
                    src = my_z * ny + (my_y if ys == 0 else 1 - my_y)
                    start = bases[plan.line_index(my_z, kind, my_z, ys, zp)]
                    n = cnt[count_at(kind, dst, src)]
                    if ys == 0:
                        fill(link, start, n, lambda i: own_code(kind, dst, i))
                    else:
                        held = ybase[plan.y_index(0, kind, my_z, zp)]
                        fill(link, start, n, lambda i: FROM_Y * SPAN + held + i)

                    def each_back(zs, c):
                        src = zs * ny + (my_y if ys == 0 else 1 - my_y)
                        start = bases[plan.line_index(my_z, kind, zs, ys, zp)]
                        held = bases[plan.line_index(my_z - ahead, kind, zs, ys, zp)]
                        n = cnt[count_at(kind, dst, src)]
                        fill(link, start, n, lambda i: origin * SPAN + held + i)
                        return c

                    if ahead == 1:
                        lax.fori_loop(0, my_z, each_back, 0)
                    else:
                        lax.fori_loop(my_z + 1, nz, each_back, 0)
                return c

            lax.fori_loop(low, high, each_target, 0)

    def place(kind, store, rank):
        zs = store // ny
        ys = jnp.where(store - zs * ny == my_y, 0, 1)
        left = rbase[plan.line_index(jnp.maximum(my_z - 1, 0), kind, zs, ys, my_z)]
        right = lbase[plan.line_index(jnp.minimum(my_z + 1, nz - 1), kind, zs, ys, my_z)]
        code = jnp.where(zs < my_z, FROM_LEFT * SPAN + left, FROM_RIGHT * SPAN + right)
        if ny == 2:
            over = FROM_Y * SPAN + ybase[plan.y_index(0, kind, my_z, my_z)]
            code = jnp.where(zs == my_z, over, code)
        own = own_code(kind, me, jnp.minimum(rank, plan.cap))
        return jnp.where(store == me, own, code + rank)

    def own_hit(i, c):
        block = meta[me * plan.width + i]
        store = lax.div(block, plan.pool_rows)
        places[i] = place(0, store, ranks[me * plan.hits + i])
        return c

    lax.fori_loop(0, plan.hits, own_hit, 0)

    def own_new(i, c):
        sender = i // WCAP
        rank = i - sender * WCAP
        there = rank < cnt[count_at(1, me, sender)]
        arrivals[i] = jnp.where(there, place(1, sender, rank), -1)
        return c

    lax.fori_loop(0, S * WCAP, own_new, 0)


def make_schedule(plan, meta, me):
    smem = pl.BlockSpec(memory_space=pltpu.SMEM)
    S, ny, nz = plan.stores, plan.ny, plan.nz
    stride = plan.cap + 1
    lines = nz * 2 * nz * ny * nz
    return pl.pallas_call(
        functools.partial(schedule_kernel, plan),
        out_shape=(
            jax.ShapeDtypeStruct((3 * plan.slots,), jnp.int32),
            jax.ShapeDtypeStruct((plan.hits,), jnp.int32),
            jax.ShapeDtypeStruct((S * WCAP,), jnp.int32),
            jax.ShapeDtypeStruct((1,), jnp.int32),
        ),
        in_specs=[smem, smem],
        out_specs=(smem, smem, smem, smem),
        scratch_shapes=[
            pltpu.SMEM((2 * S * S,), jnp.int32),
            pltpu.SMEM((2 * S * S * stride,), jnp.int32),
            pltpu.SMEM((S * plan.hits,), jnp.int32),
            pltpu.SMEM((4 * nz * nz,), jnp.int32),
            pltpu.SMEM((lines,), jnp.int32),
            pltpu.SMEM((lines,), jnp.int32),
        ],
        name="schedule",
    )(me.reshape(1), meta)


def for_source(code, sources, act):
    kind = code // SPAN
    slot = code - kind * SPAN
    for source, ref in sources.items():

        @pl.when((code >= 0) & (kind == source))
        def _():
            act(ref.at[slot])


def step_kernel(
    plan, keep, step_ref, table, pool, fresh, in_y, in_r, in_l, *refs
):
    del in_y, in_r, in_l
    got, refs = refs[: 3 if keep else 0], refs[3 if keep else 0 :]
    buf_y, buf_r, buf_l, out_y, out_r, out_l, keep_sem, pick_sem = refs
    step = step_ref[0]
    bufs = (buf_y, buf_r, buf_l)
    if keep:
        for i, (new, buf) in enumerate(zip(got, bufs)):
            at = pl.ds((step - LAG) * STEP, STEP)
            if i == 0:

                @pl.when((step - LAG + 1) * STEP <= plan.y_slots)
                def _():
                    pltpu.make_async_copy(new, buf.at[at], keep_sem.at[i]).start()
            else:
                pltpu.make_async_copy(new, buf.at[at], keep_sem.at[i]).start()
        for i, (new, buf) in enumerate(zip(got, bufs)):
            at = pl.ds((step - LAG) * STEP, STEP)
            if i == 0:

                @pl.when((step - LAG + 1) * STEP <= plan.y_slots)
                def _():
                    pltpu.make_async_copy(new, buf.at[at], keep_sem.at[i]).wait()
            else:
                pltpu.make_async_copy(new, buf.at[at], keep_sem.at[i]).wait()
    sources = {POOL: pool, FRESH: fresh, FROM_Y: buf_y, FROM_LEFT: buf_r, FROM_RIGHT: buf_l}
    outs = (out_y, out_r, out_l)
    for start in (True, False):
        for link in range(3):
            for i in range(STEP):
                code = table[link * plan.slots + step * STEP + i]
                dst = outs[link].at[i]
                sem = pick_sem.at[link, i]
                if start:
                    for_source(
                        code,
                        sources,
                        lambda src, dst=dst, sem=sem: pltpu.make_async_copy(src, dst, sem).start(),
                    )
                else:

                    @pl.when(code >= 0)
                    def _():
                        pltpu.make_async_copy(pool.at[0], dst, sem).wait()


def run_step(plan, step, table, pool, fresh, bufs, got):
    block = pool.shape[1:]
    smem = pl.BlockSpec(memory_space=pltpu.SMEM)
    far = pl.BlockSpec(memory_space=pl.ANY)
    keep = got is not None
    args = [jnp.asarray(step, jnp.int32).reshape(1), table, pool, fresh, *bufs]
    args += list(got) if keep else []
    sent = jax.ShapeDtypeStruct((STEP,) + block, pool.dtype)
    outs = pl.pallas_call(
        functools.partial(step_kernel, plan, keep),
        out_shape=tuple(jax.ShapeDtypeStruct(b.shape, b.dtype) for b in bufs) + (sent,) * 3,
        in_specs=[smem, smem] + [far] * (len(args) - 2),
        out_specs=(far,) * 6,
        input_output_aliases={4: 0, 5: 1, 6: 2},
        scratch_shapes=[pltpu.SemaphoreType.DMA((3,)), pltpu.SemaphoreType.DMA((3, STEP))],
        name="step",
    )(*args)
    return outs[:3], outs[3:]


def send(plan, blocks):
    S, ny, nz = plan.stores, plan.ny, plan.nz
    over = [(s, s ^ 1) for s in range(S)] if ny == 2 else []
    right = [(s, s + ny) for s in range(S - ny)]
    left = [(s + ny, s) for s in range(S - ny)]
    return tuple(
        lax.ppermute(b, "store", perm) if perm else b
        for b, perm in zip(blocks, (over, right, left))
    )


def flush_kernel(plan, step_ref, in_y, in_r, in_l, *refs):
    del in_y, in_r, in_l
    got, bufs, sem = refs[:6], refs[6:9], refs[9]
    step = step_ref[0]
    for start in (True, False):
        for part in range(2):
            for i in range(3):
                first = (step - LAG + part) * STEP
                limit = plan.y_slots if i == 0 else plan.slots

                @pl.when(first + STEP <= limit)
                def _():
                    copy = pltpu.make_async_copy(
                        got[3 * part + i], bufs[i].at[pl.ds(first, STEP)], sem.at[part, i]
                    )
                    copy.start() if start else copy.wait()


def flush(plan, step, bufs, got):
    smem = pl.BlockSpec(memory_space=pltpu.SMEM)
    far = pl.BlockSpec(memory_space=pl.ANY)
    return pl.pallas_call(
        functools.partial(flush_kernel, plan),
        out_shape=tuple(jax.ShapeDtypeStruct(b.shape, b.dtype) for b in bufs),
        in_specs=[smem] + [far] * 9,
        out_specs=(far,) * 3,
        input_output_aliases={1: 0, 2: 1, 3: 2},
        scratch_shapes=[pltpu.SemaphoreType.DMA((2, 3))],
        name="flush",
    )(jnp.asarray(step, jnp.int32).reshape(1), *bufs, *got)


ROWS = 512


def attend_kernel(
    plan,
    group,
    places,
    arrivals,
    hit_counts,
    lengths,
    queries,
    fresh_near,
    fresh,
    pool,
    buf_y,
    buf_r,
    buf_l,
    out,
    written,
    keys,
    vals,
    scores,
    weights,
    mixed,
    top,
    zero,
    kv_sem,
    out_sem,
):
    tokens, heads, dim = queries.shape
    kv_heads = heads // group
    block = fresh_near.shape[3]
    new_len = tokens // plan.ses
    new_blocks = new_len // block
    pre = plan.hit_len * block
    scale = math.log2(math.e) / math.sqrt(dim)
    sources = {POOL: pool, FRESH: fresh, FROM_Y: buf_y, FROM_LEFT: buf_r, FROM_RIGHT: buf_l}
    units = [(s, h) for s in range(plan.ses) for h in range(kv_heads)]

    def fetch(unit, slot):
        s, h = units[unit]

        def one(j, c):
            at = pl.ds(pl.multiple_of(j * block, block), block)

            def go(src):
                pltpu.make_async_copy(src.at[h, 0], keys.at[slot, at], kv_sem.at[slot, 0]).start()
                pltpu.make_async_copy(
                    src.at[h, 1], vals.at[slot, at, pl.ds(0, dim)], kv_sem.at[slot, 1]
                ).start()

            for_source(places[s * plan.hit_len + j], sources, go)
            return c

        lax.fori_loop(0, hit_counts[s], one, 0)

    def await_fetch(unit, slot):
        s, h = units[unit]

        def one(j, c):
            at = pl.ds(pl.multiple_of(j * block, block), block)
            pltpu.make_async_copy(
                pool.at[0, h, 0], keys.at[slot, at], kv_sem.at[slot, 0]
            ).wait()
            pltpu.make_async_copy(
                pool.at[0, h, 1], vals.at[slot, at, pl.ds(0, dim)], kv_sem.at[slot, 1]
            ).wait()
            return c

        lax.fori_loop(0, hit_counts[s], one, 0)

    vals[:, :, :dim] = jnp.zeros(vals.shape[:2] + (dim,), vals.dtype)
    vals[:, :, dim:] = jnp.ones(vals.shape[:2] + (vals.shape[2] - dim,), vals.dtype)
    fetch(0, 0)

    zero[...] = jnp.zeros(zero.shape, zero.dtype)

    def put_written(start):
        def one(i, c):
            dst = written.at[i // WCAP, i % WCAP]
            code = arrivals[i]
            if start:
                for_source(
                    code, sources, lambda src: pltpu.make_async_copy(src, dst, out_sem.at[i]).start()
                )

                @pl.when(code < 0)
                def _():
                    pltpu.make_async_copy(zero, dst, out_sem.at[i]).start()
            else:
                pltpu.make_async_copy(zero, dst, out_sem.at[i]).wait()
            return c

        lax.fori_loop(0, plan.stores * WCAP, one, 0)

    put_written(True)

    for unit, (s, h) in enumerate(units):
        slot = unit % 2
        if unit + 1 < len(units):
            fetch(unit + 1, 1 - slot)
        await_fetch(unit, slot)
        for b in range(new_blocks):
            vals[slot, pl.ds(pre + b * block, block), :dim] = fresh_near[
                s * new_blocks + b, h, 1
            ]
        used = hit_counts[s]
        pairs = used // 2
        odd = used - pairs * 2
        step_tokens = ROWS // group

        def tile(rt, c, slot=slot, s=s, h=h, pairs=pairs, odd=odd, used=used):
            first = s * new_len + rt * step_tokens
            here = pl.ds(first, step_tokens)
            q = queries[here].astype(jnp.float32)[:, h * group : (h + 1) * group, :]
            q = q.reshape(ROWS, dim).astype(jnp.bfloat16)

            def dots(k):
                return lax.dot_general(
                    q, k, (((1,), (1,)), ((), ())), preferred_element_type=jnp.float32
                )

            fresh_scores = []
            for b in range(new_blocks):
                part = dots(fresh_near[s * new_blocks + b, h, 0])
                token = rt * step_tokens + lax.broadcasted_iota(
                    jnp.int32, (ROWS, block), 0
                ) // group
                key = b * block + lax.broadcasted_iota(jnp.int32, (ROWS, block), 1)
                part = jnp.where(key <= token, part, -jnp.inf)
                scores[:, pl.ds(pre + b * block, block)] = part
                fresh_scores.append(part)
            top[...] = functools.reduce(jnp.maximum, fresh_scores)

            def pair(i, c):
                at = pl.ds(pl.multiple_of(i * 2 * block, 2 * block), 2 * block)
                part = dots(keys[slot, at])
                scores[:, at] = part
                top[...] = jnp.maximum(
                    top[...], jnp.maximum(part[:, :block], part[:, block:])
                )
                return c

            lax.fori_loop(0, pairs, pair, 0)

            @pl.when(odd == 1)
            def _():
                at = pl.ds(pl.multiple_of(pairs * 2 * block, block), block)
                part = dots(keys[slot, at])
                scores[:, at] = part
                top[...] = jnp.maximum(top[...], part)
                rest = pl.ds(pl.multiple_of((pairs * 2 + 1) * block, block), block)
                scores[:, rest] = jnp.full((ROWS, block), -jnp.inf, jnp.float32)

            peak = jnp.max(top[...], axis=1, keepdims=True) * scale
            top[...] = jnp.broadcast_to(peak, top.shape)

            def weigh(at):
                high = top[...]
                high = jnp.concatenate([high, high], axis=1)
                weights[:, at] = jnp.exp2(scores[:, at] * scale - high).astype(jnp.bfloat16)

            def weigh_pair(i, c):
                weigh(pl.ds(pl.multiple_of(i * 2 * block, 2 * block), 2 * block))
                return c

            lax.fori_loop(0, pairs + odd, weigh_pair, 0)
            for b in range(0, new_blocks, 2):
                weigh(pl.ds(pre + b * block, 2 * block))

            def blank(i, c):
                at = pl.ds(pl.multiple_of(i * 2 * block, 2 * block), 2 * block)
                weights[:, at] = jnp.zeros((ROWS, 2 * block), jnp.bfloat16)
                return c

            lax.fori_loop(pairs + odd, plan.hit_len // 2, blank, 0)
            both = jnp.dot(weights[...], vals[slot], preferred_element_type=jnp.float32)
            result = both[:, :dim] / both[:, dim:]
            token = rt * step_tokens + lax.broadcasted_iota(jnp.int32, (ROWS, dim), 0) // group
            result = jnp.where(token < lengths[s], result, 0.0)
            mixed[here, h * group : (h + 1) * group, :] = result.reshape(step_tokens, group, dim)
            return c

        lax.fori_loop(0, new_len // step_tokens, tile, 0)
        if h == kv_heads - 1:
            span = pl.ds(s * new_len, new_len)
            out[span] = mixed[span].astype(jnp.bfloat16)
    put_written(False)


def attend(plan, queries, fresh, pool, bufs, places, arrivals, hit_counts, lengths):
    smem = pl.BlockSpec(memory_space=pltpu.SMEM)
    near = pl.BlockSpec(memory_space=pltpu.VMEM)
    far = pl.BlockSpec(memory_space=pl.ANY)
    tokens, heads, dim = queries.shape
    kv_heads = pool.shape[1]
    block = pool.shape[3]
    rows = plan.hit_len * block + tokens // plan.ses
    return pl.pallas_call(
        functools.partial(attend_kernel, plan, heads // kv_heads),
        out_shape=(
            jax.ShapeDtypeStruct(queries.shape, jnp.bfloat16),
            jax.ShapeDtypeStruct((plan.stores, WCAP) + pool.shape[1:], pool.dtype),
        ),
        in_specs=[smem] * 4 + [near, near] + [far] * 5,
        out_specs=(near, far),
        scratch_shapes=[
            pltpu.VMEM((2, plan.hit_len * block, dim), jnp.bfloat16),
            pltpu.VMEM((2, rows, 2 * dim), jnp.bfloat16),
            pltpu.VMEM((ROWS, rows), jnp.float32),
            pltpu.VMEM((ROWS, rows), jnp.bfloat16),
            pltpu.VMEM((tokens, heads, dim), jnp.float32),
            pltpu.VMEM((ROWS, block), jnp.float32),
            pltpu.VMEM(pool.shape[1:], pool.dtype),
            pltpu.SemaphoreType.DMA((2, 2)),
            pltpu.SemaphoreType.DMA((plan.stores * WCAP,)),
        ],
        compiler_params=pltpu.CompilerParams(vmem_limit_bytes=48 * 1024 * 1024),
        cost_estimate=pl.CostEstimate(
            flops=4 * tokens * heads * rows * dim,
            bytes_accessed=16 * 1024 * 1024,
            transcendentals=tokens * heads * rows,
        ),
        name="attend",
    )(places, arrivals, hit_counts, lengths, queries, fresh, fresh, pool, *bufs)


def new_rows(hidden, kv_weight, hit_counts, new_lengths, local_kv, block_len):
    tokens = hidden.shape[0]
    ses_count = hit_counts.shape[0]
    new_len = tokens // ses_count
    dim = kv_weight.shape[3]
    part = jnp.einsum("ta,abhd->hbtd", hidden, kv_weight, preferred_element_type=jnp.float32)
    mine = lax.axis_index("tp")
    tp = lax.axis_size("tp")
    own = lax.dynamic_slice_in_dim(part, mine * local_kv, local_kv, 0)
    projected = own
    for away in range(1, tp):
        other = lax.dynamic_slice_in_dim(part, ((mine + away) % tp) * local_kv, local_kv, 0)
        projected = projected + lax.ppermute(
            other, "tp", [(i, (i + away) % tp) for i in range(tp)]
        )
    within = jnp.arange(tokens) % new_len
    start_pos = jnp.repeat(hit_counts, new_len, total_repeat_length=tokens)
    live_len = jnp.repeat(new_lengths, new_len, total_repeat_length=tokens)
    positions = (start_pos * block_len + within).astype(jnp.float32)
    rotated = rotate(projected[:, 0], positions)
    fresh = jnp.stack([rotated, projected[:, 1]], axis=1).astype(jnp.bfloat16)
    fresh = jnp.where((within < live_len)[None, None, :, None], fresh, jnp.zeros((), jnp.bfloat16))
    fresh = fresh.reshape(local_kv, 2, tokens // block_len, block_len, dim)
    return jnp.transpose(fresh, (2, 0, 1, 3, 4))


def local(hidden, queries, kv_weight, kv_pool, hit_ids, hit_counts, new_lengths, dest_store):
    store_count = lax.axis_size("store")
    ses_count, hit_len = hit_ids.shape
    pool_rows, local_kv, _, block_len, _ = kv_pool.shape
    per_dev = hidden.shape[0] // block_len
    plan = Plan(store_count, ses_count, hit_len, per_dev, pool_rows)
    me = lax.axis_index("store").astype(jnp.int32)

    mine = jnp.concatenate([hit_ids.reshape(-1), hit_counts, dest_store.reshape(-1)])
    meta = lax.all_to_all(
        jnp.broadcast_to(mine[None], (store_count, plan.width)),
        "store",
        split_axis=0,
        concat_axis=0,
        tiled=True,
    )
    table, places, arrivals, total = make_schedule(plan, meta.reshape(-1), me)
    total = lax.pmax(total, ("rep", "store", "tp"))

    fresh = new_rows(hidden, kv_weight, hit_counts, new_lengths, local_kv, block_len)

    block = kv_pool.shape[1:]
    bufs = tuple(
        pl.pallas_call(
            lambda o: None,
            out_shape=jax.ShapeDtypeStruct((n,) + block, kv_pool.dtype),
            out_specs=pl.BlockSpec(memory_space=pl.ANY),
            name="room",
        )()
        for n in (plan.y_slots, plan.slots, plan.slots)
    )
    got = []
    for k in range(BASE_STEPS):
        bufs, blocks = run_step(
            plan,
            k,
            table,
            kv_pool,
            fresh if k >= NEW_STEP else kv_pool,
            bufs,
            got[k - LAG] if k >= LAG else None,
        )
        got.append(send(plan, blocks))

    def more(state):
        return state[0] * STEP < total[0]

    def body(state):
        step, bufs, before, last = state
        bufs, blocks = run_step(plan, step, table, kv_pool, fresh, bufs, before)
        first = send(plan, blocks)
        bufs, blocks = run_step(plan, step + 1, table, kv_pool, fresh, bufs, last)
        second = send(plan, blocks)
        return (step + 2, bufs, first, second)

    step, bufs, before, last = lax.while_loop(
        more, body, (jnp.int32(BASE_STEPS), bufs, got[-2], got[-1])
    )
    bufs = flush(plan, step, bufs, before + last)
    attention, written = attend(
        plan, queries, fresh, kv_pool, bufs, places, arrivals, hit_counts, new_lengths
    )
    return attention, written[None]


def solution(mesh):
    placed = (
        P(("rep", "store"), "tp"),
        P(("rep", "store"), "tp", None),
        P("tp", None, None, None),
        P(("rep", "store"), "tp", None, None, None),
        P(("rep", "store"), None),
        P(("rep", "store")),
        P(("rep", "store")),
        P(("rep", "store"), None),
    )
    return jax.shard_map(
        local,
        mesh=mesh,
        in_specs=placed,
        out_specs=(
            P(("rep", "store"), "tp", None),
            P(("rep", "store"), None, None, "tp", None, None, None),
        ),
        check_vma=False,
    )
```

```python
import functools
import math

import jax
import jax.numpy as jnp
from jax import lax
from jax.experimental import pallas as pl
from jax.experimental.pallas import tpu as pltpu
from jax.sharding import PartitionSpec as P

NY = 2
WCAP = 2
EARLY = 4

theta_base = 500000.0

SPAN = 1 << 16
WIDE = 1 << 5
POOL, FRESH, HOP_IN, ALONG_Z, HOP_OUT = range(5)


def rotate(keys, positions):
    half = keys.shape[-1] // 2
    steps = jnp.arange(half, dtype=jnp.float32)
    inverse = jnp.exp(steps * (-2.0 * math.log(theta_base) / keys.shape[-1]))
    angles = positions[:, None] * inverse[None, :]
    cosine = jnp.cos(angles)
    sine = jnp.sin(angles)
    first = keys[..., :half]
    second = keys[..., half:]
    return jnp.concatenate(
        [first * cosine - second * sine, second * cosine + first * sine], axis=-1
    )


class Plan:
    def __init__(self, reps, store_count, ses_count, hit_len, per_dev, pool_rows):
        self.reps = reps
        self.stores = store_count
        self.nz = store_count // NY
        self.ses = ses_count
        self.hit_len = hit_len
        self.hits = ses_count * hit_len
        self.per_dev = per_dev
        self.pool_rows = pool_rows
        self.cap = 2 * ((self.hits + store_count - 1) // store_count)
        self.width = self.hits + ses_count + per_dev
        nz, cap = self.nz, self.cap
        both = cap + 2 * WCAP
        self.most = (
            (max(2 * cap, EARLY + cap), nz * cap, (nz - 1) * cap),
            (2 * both, nz * cap + 2 * per_dev, (nz - 1) * both),
        )
        wanted = (
            ((10, 16, 15), (13, 26, 9)),
            ((11, 16, 15), (14, 28, 11)),
            ((12, 18, 17), (16, 30, 13)),
            self.most,
        )
        self.long_in = max(m[1] for m in self.most)
        self.long_out = max(m[2] for m in self.most)
        assert max(m[0] for m in self.most) <= WIDE
        self.classes = [
            tuple(
                tuple(min(a, b) for a, b in zip(size, most))
                for size, most in zip(sizes, self.most)
            )
            for sizes in wanted
        ]


def schedule_kernel(
    plan, me_ref, meta, z_out, in_out, out_out, places, arrivals, chosen,
    cnt, rows, ranks, over, hop_out_sum, in_base, out_base
):
    S, nz, cap = plan.stores, plan.nz, plan.cap
    me = me_ref[0]
    rep = me_ref[1]
    my_z = me // NY
    my_y = me - my_z * NY
    stride = cap + 1

    def count_at(kind, group, dst, src):
        return ((group * 2 + kind) * S + dst) * S + src

    def units(phase, group, dst, src):
        n = cnt[count_at(0, group, dst, src)]
        return n if phase == 0 else n + 2 * cnt[count_at(1, group, dst, src)]

    def over_at(phase, group, z, zp, ys):
        return (((group * 2 + phase) * nz + z) * nz + zp) * NY + ys

    def zero(ref, n, value=0):
        def put(i, c):
            ref[i] = jnp.int32(value)
            return c

        lax.fori_loop(0, n, put, 0)

    zero(cnt, plan.reps * 2 * S * S)
    zero(hop_out_sum, plan.reps * 2 * nz * NY)
    zero(z_out, 2 * nz * WIDE, -1)
    zero(in_out, 2 * plan.long_in, -1)
    zero(out_out, 2 * plan.long_out, -1)

    def scan(g, c):
        group = g // S
        d = g - group * S
        base = g * plan.width
        for t in range(plan.ses):
            used = meta[base + plan.hits + t]
            for j in range(plan.hit_len):
                block = meta[base + t * plan.hit_len + j]
                store = lax.div(block, plan.pool_rows)
                at = count_at(0, group, d, store)
                rank = cnt[at]
                rows[at * stride + jnp.minimum(rank, cap)] = block - store * plan.pool_rows
                ranks[g * plan.hits + t * plan.hit_len + j] = rank
                cnt[at] = rank + (j < used).astype(jnp.int32)
        for j in range(plan.per_dev):
            dest = meta[base + plan.hits + plan.ses + j]
            at = count_at(1, group, dest, d)
            rank = cnt[at]
            rows[at * stride + jnp.minimum(rank, cap)] = j
            cnt[at] = rank + 1
        return c

    lax.fori_loop(0, plan.reps * S, scan, 0)

    def balance(i, c):
        group = i // nz
        z = i - group * nz
        c = list(c)
        for phase in range(2):
            longest, most_in = c[2 * phase], c[2 * phase + 1]
            going = [units(phase, group, z * NY + 1 - y, z * NY + y) for y in range(NY)]
            for zp in range(nz):
                a = [
                    [units(phase, group, zp * NY + yd, z * NY + ys) for yd in range(NY)]
                    for ys in range(NY)
                ]
                half = (a[0][0] + a[0][1] + a[1][0] + a[1][1] + 1) // 2
                if phase == 0:
                    excess = [a[y][y] + a[y][1 - y] - half for y in range(NY)]
                    first = [
                        a[y][1 - y] - jnp.minimum(jnp.maximum(excess[y], 0), a[y][1 - y])
                        for y in range(NY)
                    ]
                else:
                    excess = [a[y][y] + a[1 - y][y] - half for y in range(NY)]
                    first = [
                        jnp.minimum(jnp.maximum(excess[1 - y], 0), a[y][1 - y]) for y in range(NY)
                    ]
                away = zp != z
                for y in range(NY):
                    over[over_at(phase, group, z, zp, y)] = first[y]
                    later = a[1 - y][y] - first[1 - y]
                    own = a[y][y] + first[y]
                    start = jnp.maximum(own, EARLY) if phase == 0 else own
                    end = jnp.where(later > 0, start + later, own)
                    longest = jnp.where(away, jnp.maximum(longest, end), longest)
                    going[1 - y] = going[1 - y] + jnp.where(away, later, 0)
                    at = ((group * 2 + phase) * nz + zp) * NY + y
                    hop_out_sum[at] = hop_out_sum[at] + jnp.where(away, first[y], 0)
            c[2 * phase] = longest
            c[2 * phase + 1] = jnp.maximum(most_in, jnp.maximum(going[0], going[1]))
        return tuple(c)

    none = jnp.int32(0)
    need = lax.fori_loop(0, plan.reps * nz, balance, (none,) * 4)
    out_need = []
    for phase in range(2):

        def top(i, c, phase=phase):
            group = i // (nz * NY)
            at = (group * 2 + phase) * nz * NY + i - group * nz * NY
            return jnp.maximum(c, hop_out_sum[at])

        out_need.append(lax.fori_loop(0, plan.reps * nz * NY, top, none))
    needs = ((need[0], need[1], out_need[0]), (need[2], need[3], out_need[1]))
    pick = jnp.int32(len(plan.classes) - 1)
    for k in reversed(range(len(plan.classes) - 1)):
        fits = jnp.bool_(True)
        for phase in range(2):
            for n, size in zip(needs[phase], plan.classes[k][phase]):
                fits = fits & (n <= size)
        pick = jnp.where(fits, jnp.int32(k), pick)
    chosen[0] = pick

    def amount(phase, dst, src):
        return units(phase, rep, dst, src)

    def first_of(phase, z, zp, ys):
        return over[over_at(phase, rep, z, zp, ys)]

    def own_code(phase, dst, i):
        hit_at = count_at(0, rep, dst, me)
        hit = rows[hit_at * stride + jnp.minimum(i, cap)]
        code = POOL * SPAN + hit * 2 + phase
        if phase == 0:
            return code
        new_at = count_at(1, rep, dst, me)
        n = cnt[new_at]
        k = i - cnt[hit_at]
        head = (k >= n).astype(jnp.int32)
        new = rows[new_at * stride + jnp.clip(k - head * n, 0, cap)]
        return jnp.where(k >= 0, FRESH * SPAN + new * 2 + head, code)

    def fill(ref, start, n, code_of):
        def put(i, c):
            ref[start + i] = code_of(i)
            return c

        lax.fori_loop(0, n, put, 0)

    other = my_z * NY + 1 - my_y
    for phase in range(2):
        in_first, out_first = phase * plan.long_in, phase * plan.long_out

        def each(zp, c, phase=phase, in_first=in_first, out_first=out_first):
            mine, theirs, out_mine, out_theirs = c
            away = (zp != my_z).astype(jnp.int32)
            over_there = zp * NY + 1 - my_y
            along = zp * NY + my_y
            first = first_of(phase, my_z, zp, my_y)
            n = (amount(phase, over_there, me) - first) * away
            fill(in_out, in_first + mine, n, lambda i: own_code(phase, over_there, first + i))
            later = (amount(phase, along, other) - first_of(phase, my_z, zp, 1 - my_y)) * away
            row = (phase * nz + zp) * WIDE
            own = amount(phase, along, me)
            fill(z_out, row, first * away, lambda i: own_code(phase, over_there, i))
            fill(z_out, row + first, own * away, lambda i: own_code(phase, along, i))
            start = first + own
            if phase == 0:
                start = jnp.maximum(start, EARLY)
            fill(z_out, row + start, later, lambda i: HOP_IN * SPAN + theirs + i)
            out_n = first_of(phase, zp, my_z, my_y) * away
            fill(
                out_out, out_first + out_mine, out_n, lambda i: ALONG_Z * SPAN + zp * WIDE + i
            )
            out_base[phase * nz + zp] = out_theirs
            out_later = first_of(phase, zp, my_z, 1 - my_y) * away
            return mine + n, theirs + later, out_mine + out_n, out_theirs + out_later

        mine, theirs, _, _ = lax.fori_loop(0, nz, each, (none,) * 4)
        fill(
            in_out,
            in_first + mine,
            amount(phase, other, me),
            lambda i, p=phase: own_code(p, other, i),
        )
        in_base[phase] = theirs

    def place(phase, store, i):
        zs = store // NY
        straight = store - zs * NY == my_y
        first = first_of(phase, zs, my_z, my_y)
        held = first + i
        crossing = first_of(phase, zs, my_z, 1 - my_y)
        start = first + amount(phase, me, zs * NY + my_y)
        if phase == 0:
            start = jnp.maximum(start, EARLY)
        slot = jnp.where(straight, held, start + i - crossing)
        code = ALONG_Z * SPAN + zs * WIDE + slot
        late = jnp.logical_not(straight) & (i < crossing)
        code = jnp.where(late, HOP_OUT * SPAN + out_base[phase * nz + zs] + i, code)
        code = jnp.where(zs == my_z, HOP_IN * SPAN + in_base[phase] + i, code)
        return jnp.where(store == me, own_code(phase, me, i), code)

    here = rep * S + me

    def own_hit(i, c):
        store = lax.div(meta[here * plan.width + i], plan.pool_rows)
        rank = ranks[here * plan.hits + i]
        for phase in range(2):
            places[phase * plan.hits + i] = place(phase, store, rank)
        return c

    lax.fori_loop(0, plan.hits, own_hit, 0)

    def own_new(i, c):
        sender = i // WCAP
        rank = i - sender * WCAP
        n = cnt[count_at(1, rep, me, sender)]
        first = cnt[count_at(0, rep, me, sender)] + rank
        for head in range(2):
            code = place(1, sender, first + head * n)
            arrivals[i * 2 + head] = jnp.where(rank < n, code, -1)
        return c

    lax.fori_loop(0, S * WCAP, own_new, 0)


def make_schedule(plan, meta, me, rep):
    smem = pl.BlockSpec(memory_space=pltpu.SMEM)
    S, nz, reps = plan.stores, plan.nz, plan.reps
    ints = lambda *shape: jax.ShapeDtypeStruct(shape, jnp.int32)
    room = lambda n: pltpu.SMEM((n,), jnp.int32)
    return pl.pallas_call(
        functools.partial(schedule_kernel, plan),
        out_shape=(
            ints(2 * nz * WIDE),
            ints(2 * plan.long_in),
            ints(2 * plan.long_out),
            ints(2 * plan.hits),
            ints(S * WCAP * 2),
            ints(1),
        ),
        in_specs=[smem, smem],
        out_specs=(smem,) * 6,
        scratch_shapes=[
            room(reps * 2 * S * S),
            room(reps * 2 * S * S * (plan.cap + 1)),
            room(reps * S * plan.hits),
            room(reps * 2 * nz * nz * NY),
            room(reps * 2 * nz * NY),
            room(2),
            room(2 * nz),
        ],
        name="schedule",
    )(jnp.stack([me, rep]), meta)


def for_source(code, sources, act):
    kind = code // SPAN
    slot = code - kind * SPAN
    for source, ref in sources.items():
        if source == ALONG_Z:
            z = slot // WIDE
            at = slot - z * WIDE
            ends = [first for first, _ in ref[1:]] + [WIDE]
            for (first, part), end in zip(ref, ends):

                @pl.when((code >= 0) & (kind == source) & (at >= first) & (at < end))
                def _():
                    act(part.at[z, at - first])
        else:

            @pl.when((code >= 0) & (kind == source))
            def _():
                act(ref.at[slot])


def pick_kernel(names, firsts, lines, first, table, *refs):
    ins, (out, sem) = refs[: len(names)], refs[len(names) :]
    sources = {}
    for name, start, ref in zip(names, firsts, ins):
        if name == ALONG_Z:
            sources.setdefault(name, []).append((start, ref))
        else:
            sources[name] = ref
    slots = out.shape[1]
    for start in (True, False):
        for line in range(lines):

            def one(i, c):
                code = table[first + line * WIDE + i]
                dst = out.at[line, i]
                if start:
                    for_source(
                        code, sources, lambda src: pltpu.make_async_copy(src, dst, sem).start()
                    )
                else:

                    @pl.when(code >= 0)
                    def _():
                        pltpu.make_async_copy(dst, dst, sem).wait()

                return c

            lax.fori_loop(0, slots, one, 0)


def pick(table, lines, first, slots, sources, unit, dtype):
    smem = pl.BlockSpec(memory_space=pltpu.SMEM)
    far = pl.BlockSpec(memory_space=pl.ANY)
    names = [s[0] for s in sources]
    firsts = [s[1] for s in sources]
    size = lines * slots * math.prod(unit) * 2
    return pl.pallas_call(
        functools.partial(pick_kernel, names, firsts, lines, first),
        out_shape=jax.ShapeDtypeStruct((lines, slots) + unit, dtype),
        in_specs=[smem] + [far] * len(sources),
        out_specs=pl.BlockSpec(memory_space=pltpu.VMEM),
        scratch_shapes=[pltpu.SemaphoreType.DMA],
        compiler_params=pltpu.CompilerParams(vmem_limit_bytes=32 * 1024 * 1024),
        cost_estimate=pl.CostEstimate(flops=0, bytes_accessed=3 * size, transcendentals=0),
        name="pick",
    )(table, *[s[2] for s in sources])


ROWS = 256


def attend_kernel(plan, head, group, names, firsts, places, hit_counts, lengths, arrivals, *refs):
    last = arrivals is not None
    refs = list(refs)
    queries, fresh_near = refs[:2]
    ins = refs[2 : 2 + len(names)]
    refs = refs[2 + len(names) :]
    if last:
        done, out, written = refs[:3]
        refs = refs[3:]
        held, vals, scores, weights, mixed, zero, kv_sem, out_sem = refs
    else:
        mixed, held, vals, scores, weights, kv_sem = refs
    sources = {}
    for name, start, ref in zip(names, firsts, ins):
        if name == ALONG_Z:
            sources.setdefault(name, []).append((start, ref))
        else:
            sources[name] = ref
    tokens, heads, dim = queries.shape
    block = fresh_near.shape[2]
    new_len = tokens // plan.ses
    new_blocks = new_len // block
    pre = new_blocks * block
    scale = math.log2(math.e) / math.sqrt(dim)

    def fetch(s):
        def one(j, c):
            dst = held.at[s, j]
            for_source(
                places[(head * plan.ses + s) * plan.hit_len + j],
                sources,
                lambda src: pltpu.make_async_copy(src, dst, kv_sem.at[s]).start(),
            )
            return c

        lax.fori_loop(0, hit_counts[s], one, 0)

    def await_fetch(s):
        def one(j, c):
            dst = held.at[s, j]
            pltpu.make_async_copy(dst, dst, kv_sem.at[s]).wait()
            return c

        lax.fori_loop(0, hit_counts[s], one, 0)

    for s in range(plan.ses):
        fetch(s)

    if last:
        zero[...] = jnp.zeros(zero.shape, zero.dtype)

        def put_written(start):
            def one(i, c):
                dst = written.at[i // (2 * WCAP), (i // 2) % WCAP, i % 2]
                code = arrivals[i]
                if start:
                    for_source(
                        code,
                        sources,
                        lambda src: pltpu.make_async_copy(src, dst, out_sem.at[0]).start(),
                    )

                    @pl.when(code < 0)
                    def _():
                        pltpu.make_async_copy(zero, dst, out_sem.at[0]).start()
                else:
                    pltpu.make_async_copy(zero, dst, out_sem.at[0]).wait()
                return c

            lax.fori_loop(0, plan.stores * WCAP * 2, one, 0)

        put_written(True)

    vals[:, dim:] = jnp.ones((vals.shape[0], vals.shape[1] - dim), vals.dtype)
    step_tokens = ROWS // group
    assert ROWS % group == 0 and new_len % step_tokens == 0 and plan.hit_len % 2 == 0

    for s in range(plan.ses):
        await_fetch(s)
        used = hit_counts[s]
        for b in range(new_blocks):
            vals[pl.ds(b * block, block), :dim] = fresh_near[(s * new_blocks + b) * 2 + head, 1]
        for j in range(plan.hit_len):

            @pl.when(j < used)
            def _():
                vals[pl.ds(pre + j * block, block), :dim] = held[s, j, 1]

            @pl.when(j >= used)
            def _():
                vals[pl.ds(pre + j * block, block), :dim] = jnp.zeros((block, dim), vals.dtype)

        def tile(rt, c, pairs, s=s, used=used):
            first = s * new_len + rt * step_tokens
            here = pl.ds(first, step_tokens)
            q = queries[here].astype(jnp.float32)[:, head * group : (head + 1) * group, :]
            q = q.reshape(ROWS, dim).astype(jnp.bfloat16)

            def dots(k):
                return lax.dot_general(
                    q, k, (((1,), (1,)), ((), ())), preferred_element_type=jnp.float32
                )

            token = rt * step_tokens + lax.broadcasted_iota(
                jnp.int32, (step_tokens, group, block), 0
            ).reshape(ROWS, block)
            lane = lax.broadcasted_iota(jnp.int32, (ROWS, block), 1)
            tops = None
            for b in range(new_blocks):
                part = dots(fresh_near[(s * new_blocks + b) * 2 + head, 0])
                part = jnp.where(b * block + lane <= token, part, -jnp.inf)
                scores[:, b * block : (b + 1) * block] = part
                tops = part if tops is None else jnp.maximum(tops, part)
            for i in range(pairs):
                part = dots(
                    jnp.concatenate([held[s, 2 * i, 0], held[s, 2 * i + 1, 0]], axis=0)
                )
                left, right = part[:, :block], part[:, block:]
                if i == pairs - 1:
                    right = jnp.where(used < 2 * pairs, -jnp.inf, right)
                at = pre + 2 * i * block
                scores[:, at : at + block] = left
                scores[:, at + block : at + 2 * block] = right
                tops = jnp.maximum(tops, jnp.maximum(left, right))
            peak = jnp.max(tops, axis=1, keepdims=True) * scale
            width = pre + 2 * pairs * block
            for at in range(0, width, block):
                part = scores[:, at : at + block]
                weights[:, at : at + block] = jnp.exp2(part * scale - peak).astype(jnp.bfloat16)
            both = jnp.dot(
                weights[:, :width], vals[:width, :], preferred_element_type=jnp.float32
            )
            result = both[:, :dim] / both[:, dim:]
            result = jnp.where(token < lengths[s], result, 0.0)
            mixed[here] = result.reshape(step_tokens, group, dim)
            return c

        need = (used + 1) // 2
        for pairs in range(1, plan.hit_len // 2 + 1):
            if pairs < plan.hit_len // 4:
                continue

            @pl.when(need == pairs)
            def _():
                lax.fori_loop(
                    0, new_len // step_tokens, functools.partial(tile, pairs=pairs), 0
                )

        if last:
            span = pl.ds(s * new_len, new_len)
            out[span] = jnp.concatenate([done[span], mixed[span]], axis=1).astype(jnp.bfloat16)
    if last:
        put_written(False)


def attend(plan, head, queries, fresh, sources, places, counts, lengths, arrivals=None, done=None):
    smem = pl.BlockSpec(memory_space=pltpu.SMEM)
    near = pl.BlockSpec(memory_space=pltpu.VMEM)
    far = pl.BlockSpec(memory_space=pl.ANY)
    tokens, heads, dim = queries.shape
    group = heads // 2
    unit = fresh.shape[1:]
    block = unit[1]
    rows = plan.hit_len * block + tokens // plan.ses
    last = done is not None
    names = [x[0] for x in sources]
    firsts = [x[1] for x in sources]
    kernel = functools.partial(attend_kernel, plan, head, group, names, firsts)
    scratch = [
        pltpu.VMEM((plan.ses, plan.hit_len) + unit, jnp.bfloat16),
        pltpu.VMEM((rows, 2 * dim), jnp.bfloat16),
        pltpu.VMEM((ROWS, rows), jnp.float32),
        pltpu.VMEM((ROWS, rows), jnp.bfloat16),
    ]
    partial_out = jax.ShapeDtypeStruct((tokens, group, dim), jnp.float32)
    arrays = [x[2] for x in sources]
    if last:
        call = dict(
            out_shape=(
                jax.ShapeDtypeStruct(queries.shape, jnp.bfloat16),
                jax.ShapeDtypeStruct((plan.stores, WCAP, 2) + unit, jnp.bfloat16),
            ),
            in_specs=[smem] * 4 + [near, near] + [far] * len(sources) + [near],
            out_specs=(near, far),
            scratch_shapes=scratch
            + [
                pltpu.VMEM(partial_out.shape, jnp.float32),
                pltpu.VMEM(unit, jnp.bfloat16),
                pltpu.SemaphoreType.DMA((plan.ses,)),
                pltpu.SemaphoreType.DMA((1,)),
            ],
        )
        args = [places, counts, lengths, arrivals, queries, fresh] + arrays + [done]
        body = kernel
    else:
        call = dict(
            out_shape=partial_out,
            in_specs=[smem] * 3 + [near, near] + [far] * len(sources),
            out_specs=near,
            scratch_shapes=scratch + [pltpu.SemaphoreType.DMA((plan.ses,))],
        )
        args = [places, counts, lengths, queries, fresh] + arrays
        body = lambda p, c, n, *refs: kernel(p, c, n, None, *refs)
    return pl.pallas_call(
        body,
        compiler_params=pltpu.CompilerParams(vmem_limit_bytes=40 * 1024 * 1024),
        cost_estimate=pl.CostEstimate(
            flops=2 * tokens * heads * rows * dim,
            bytes_accessed=8 * 1024 * 1024,
            transcendentals=tokens * group * rows,
        ),
        name="attend",
        **call,
    )(*args)


def new_rows(hidden, kv_weight, hit_counts, new_lengths, local_kv, block_len):
    tokens = hidden.shape[0]
    ses_count = hit_counts.shape[0]
    new_len = tokens // ses_count
    dim = kv_weight.shape[3]
    part = jnp.einsum("ta,abhd->hbtd", hidden, kv_weight, preferred_element_type=jnp.float32)
    mine = lax.axis_index("tp")
    tp = lax.axis_size("tp")
    projected = lax.dynamic_slice_in_dim(part, mine * local_kv, local_kv, 0)
    for away in range(1, tp):
        other = lax.dynamic_slice_in_dim(part, ((mine + away) % tp) * local_kv, local_kv, 0)
        projected = projected + lax.ppermute(
            other, "tp", [(i, (i + away) % tp) for i in range(tp)]
        )
    within = jnp.arange(tokens) % new_len
    start_pos = jnp.repeat(hit_counts, new_len, total_repeat_length=tokens)
    live_len = jnp.repeat(new_lengths, new_len, total_repeat_length=tokens)
    positions = (start_pos * block_len + within).astype(jnp.float32)
    rotated = rotate(projected[:, 0], positions)
    fresh = jnp.stack([rotated, projected[:, 1]], axis=1).astype(jnp.bfloat16)
    fresh = jnp.where((within < live_len)[None, None, :, None], fresh, jnp.zeros((), jnp.bfloat16))
    fresh = fresh.reshape(local_kv, 2, tokens // block_len, block_len, dim)
    fresh = jnp.transpose(fresh, (2, 0, 1, 3, 4))
    return fresh.reshape((-1,) + fresh.shape[2:])


def along_z(plan, units):
    columns = [[z * NY + y for z in range(plan.nz)] for y in range(NY)]
    return lax.all_to_all(
        units, "store", split_axis=0, concat_axis=0, axis_index_groups=columns, tiled=True
    )


def over_y(plan, units):
    return lax.ppermute(units[0], "store", [(s, s ^ 1) for s in range(plan.stores)])


def run(plan, size, args):
    hidden, queries, kv_weight, kv_pool, hit_counts, new_lengths, tables = args
    z_out, in_out, out_out, places, arrivals = tables
    pool_rows, local_kv, _, block_len, dim = kv_pool.shape
    unit = kv_pool.shape[2:]
    pool = kv_pool.reshape((pool_rows * local_kv,) + unit)
    take = functools.partial(pick, unit=unit, dtype=kv_pool.dtype)
    z_second = plan.nz * WIDE
    (c0, in0, out0), (c1, in1, out1) = size

    early = along_z(plan, take(z_out, plan.nz, 0, EARLY, [(POOL, 0, pool)]))
    hop0 = over_y(plan, take(in_out, 1, 0, in0, [(POOL, 0, pool)]))
    late = along_z(
        plan, take(z_out, plan.nz, EARLY, c0 - EARLY, [(POOL, 0, pool), (HOP_IN, 0, hop0)])
    )
    fresh = new_rows(hidden, kv_weight, hit_counts, new_lengths, local_kv, block_len)
    hop1 = over_y(plan, take(in_out, 1, plan.long_in, in1, [(POOL, 0, pool), (FRESH, 0, fresh)]))
    second = along_z(
        plan,
        take(z_out, plan.nz, z_second, c1, [(POOL, 0, pool), (FRESH, 0, fresh), (HOP_IN, 0, hop1)]),
    )
    came0 = [(ALONG_Z, 0, early), (ALONG_Z, EARLY, late)]
    back0 = over_y(plan, take(out_out, 1, 0, out0, came0))
    done = attend(
        plan,
        0,
        queries,
        fresh,
        [(POOL, 0, pool), (HOP_IN, 0, hop0), (HOP_OUT, 0, back0)] + came0,
        places,
        hit_counts,
        new_lengths,
    )
    came1 = [(ALONG_Z, 0, second)]
    back1 = over_y(plan, take(out_out, 1, plan.long_out, out1, came1))
    return attend(
        plan,
        1,
        queries,
        fresh,
        [(POOL, 0, pool), (FRESH, 0, fresh), (HOP_IN, 0, hop1), (HOP_OUT, 0, back1)] + came1,
        places,
        hit_counts,
        new_lengths,
        arrivals,
        done,
    )


def local(hidden, queries, kv_weight, kv_pool, hit_ids, hit_counts, new_lengths, dest_store):
    reps = lax.axis_size("rep")
    store_count = lax.axis_size("store")
    ses_count, hit_len = hit_ids.shape
    pool_rows, local_kv, _, block_len, _ = kv_pool.shape
    per_dev = hidden.shape[0] // block_len
    assert local_kv == 2 and store_count % NY == 0
    plan = Plan(reps, store_count, ses_count, hit_len, per_dev, pool_rows)
    me = lax.axis_index("store").astype(jnp.int32)
    rep = lax.axis_index("rep").astype(jnp.int32)

    mine = jnp.concatenate([hit_ids.reshape(-1), hit_counts, dest_store.reshape(-1)])
    meta = lax.all_to_all(
        jnp.broadcast_to(mine[None], (reps * store_count, plan.width)),
        ("rep", "store"),
        split_axis=0,
        concat_axis=0,
        tiled=True,
    )
    *tables, chosen = make_schedule(plan, meta.reshape(-1), me, rep)
    args = (hidden, queries, kv_weight, kv_pool, hit_counts, new_lengths, tables)
    branches = [functools.partial(run, plan, size) for size in plan.classes]
    attention, written = lax.switch(chosen[0], branches, args)
    return attention, written[None]


def solution(mesh):
    placed = (
        P(("rep", "store"), "tp"),
        P(("rep", "store"), "tp", None),
        P("tp", None, None, None),
        P(("rep", "store"), "tp", None, None, None),
        P(("rep", "store"), None),
        P(("rep", "store")),
        P(("rep", "store")),
        P(("rep", "store"), None),
    )
    return jax.shard_map(
        local,
        mesh=mesh,
        in_specs=placed,
        out_specs=(
            P(("rep", "store"), "tp", None),
            P(("rep", "store"), None, None, "tp", None, None, None),
        ),
        check_vma=False,
    )
```

```python
import functools
import math

import jax
import jax.numpy as jnp
from jax import lax
from jax.experimental import pallas as pl
from jax.experimental.pallas import tpu as pltpu
from jax.sharding import PartitionSpec as P

NY = 2
WCAP = 2
EARLY = 4

theta_base = 500000.0

SPAN = 1 << 16
WIDE = 1 << 5
POOL, FRESH, HOP_IN, ALONG_Z, HOP_OUT = range(5)


def rotate(keys, positions):
    half = keys.shape[-1] // 2
    steps = jnp.arange(half, dtype=jnp.float32)
    inverse = jnp.exp(steps * (-2.0 * math.log(theta_base) / keys.shape[-1]))
    angles = positions[:, None] * inverse[None, :]
    cosine = jnp.cos(angles)
    sine = jnp.sin(angles)
    first = keys[..., :half]
    second = keys[..., half:]
    return jnp.concatenate(
        [first * cosine - second * sine, second * cosine + first * sine], axis=-1
    )


class Plan:
    def __init__(self, reps, store_count, ses_count, hit_len, per_dev, pool_rows):
        self.reps = reps
        self.stores = store_count
        self.nz = store_count // NY
        self.ses = ses_count
        self.hit_len = hit_len
        self.hits = ses_count * hit_len
        self.per_dev = per_dev
        self.pool_rows = pool_rows
        self.cap = 2 * ((self.hits + store_count - 1) // store_count)
        self.width = self.hits + ses_count + per_dev
        nz, cap = self.nz, self.cap
        both = cap + 2 * WCAP
        self.most = (
            (max(2 * cap, EARLY + cap), nz * cap, (nz - 1) * cap),
            (2 * both, nz * cap + 2 * per_dev, (nz - 1) * both),
        )
        wanted = (
            ((10, 16, 15), (13, 26, 9)),
            ((11, 16, 15), (14, 28, 11)),
            ((12, 18, 17), (16, 30, 13)),
            self.most,
        )
        self.long_in = max(m[1] for m in self.most)
        self.long_out = max(m[2] for m in self.most)
        assert max(m[0] for m in self.most) <= WIDE
        self.classes = [
            tuple(
                tuple(min(a, b) for a, b in zip(size, most))
                for size, most in zip(sizes, self.most)
            )
            for sizes in wanted
        ]


def schedule_kernel(
    plan, me_ref, meta, z_out, in_out, out_out, places, arrivals, chosen,
    cnt, rows, ranks, over, hop_out_sum, in_base, out_base
):
    S, nz, cap = plan.stores, plan.nz, plan.cap
    me = me_ref[0]
    rep = me_ref[1]
    my_z = me // NY
    my_y = me - my_z * NY
    stride = cap + 1

    def count_at(kind, group, dst, src):
        return ((group * 2 + kind) * S + dst) * S + src

    def units(phase, group, dst, src):
        n = cnt[count_at(0, group, dst, src)]
        return n if phase == 0 else n + 2 * cnt[count_at(1, group, dst, src)]

    def over_at(phase, group, z, zp, ys):
        return (((group * 2 + phase) * nz + z) * nz + zp) * NY + ys

    def zero(ref, n, value=0):
        def put(i, c):
            ref[i] = jnp.int32(value)
            return c

        lax.fori_loop(0, n, put, 0)

    zero(cnt, plan.reps * 2 * S * S)
    zero(hop_out_sum, plan.reps * 2 * nz * NY)
    zero(z_out, 2 * nz * WIDE, -1)
    zero(in_out, 2 * plan.long_in, -1)
    zero(out_out, 2 * plan.long_out, -1)

    def scan(g, c):
        group = g // S
        d = g - group * S
        base = g * plan.width
        for t in range(plan.ses):
            used = meta[base + plan.hits + t]
            for j in range(plan.hit_len):
                block = meta[base + t * plan.hit_len + j]
                store = lax.div(block, plan.pool_rows)
                at = count_at(0, group, d, store)
                rank = cnt[at]
                rows[at * stride + jnp.minimum(rank, cap)] = block - store * plan.pool_rows
                ranks[g * plan.hits + t * plan.hit_len + j] = rank
                cnt[at] = rank + (j < used).astype(jnp.int32)
        for j in range(plan.per_dev):
            dest = meta[base + plan.hits + plan.ses + j]
            at = count_at(1, group, dest, d)
            rank = cnt[at]
            rows[at * stride + jnp.minimum(rank, cap)] = j
            cnt[at] = rank + 1
        return c

    lax.fori_loop(0, plan.reps * S, scan, 0)

    def balance(i, c):
        group = i // nz
        z = i - group * nz
        c = list(c)
        for phase in range(2):
            longest, most_in = c[2 * phase], c[2 * phase + 1]
            going = [units(phase, group, z * NY + 1 - y, z * NY + y) for y in range(NY)]
            for zp in range(nz):
                a = [
                    [units(phase, group, zp * NY + yd, z * NY + ys) for yd in range(NY)]
                    for ys in range(NY)
                ]
                half = (a[0][0] + a[0][1] + a[1][0] + a[1][1] + 1) // 2
                if phase == 0:
                    excess = [a[y][y] + a[y][1 - y] - half for y in range(NY)]
                    first = [
                        a[y][1 - y] - jnp.minimum(jnp.maximum(excess[y], 0), a[y][1 - y])
                        for y in range(NY)
                    ]
                else:
                    excess = [a[y][y] + a[1 - y][y] - half for y in range(NY)]
                    first = [
                        jnp.minimum(jnp.maximum(excess[1 - y], 0), a[y][1 - y]) for y in range(NY)
                    ]
                away = zp != z
                for y in range(NY):
                    over[over_at(phase, group, z, zp, y)] = first[y]
                    later = a[1 - y][y] - first[1 - y]
                    own = a[y][y] + first[y]
                    start = jnp.maximum(own, EARLY) if phase == 0 else own
                    end = jnp.where(later > 0, start + later, own)
                    longest = jnp.where(away, jnp.maximum(longest, end), longest)
                    going[1 - y] = going[1 - y] + jnp.where(away, later, 0)
                    at = ((group * 2 + phase) * nz + zp) * NY + y
                    hop_out_sum[at] = hop_out_sum[at] + jnp.where(away, first[y], 0)
            c[2 * phase] = longest
            c[2 * phase + 1] = jnp.maximum(most_in, jnp.maximum(going[0], going[1]))
        return tuple(c)

    none = jnp.int32(0)
    need = lax.fori_loop(0, plan.reps * nz, balance, (none,) * 4)
    out_need = []
    for phase in range(2):

        def top(i, c, phase=phase):
            group = i // (nz * NY)
            at = (group * 2 + phase) * nz * NY + i - group * nz * NY
            return jnp.maximum(c, hop_out_sum[at])

        out_need.append(lax.fori_loop(0, plan.reps * nz * NY, top, none))
    needs = ((need[0], need[1], out_need[0]), (need[2], need[3], out_need[1]))
    pick = jnp.int32(len(plan.classes) - 1)
    for k in reversed(range(len(plan.classes) - 1)):
        fits = jnp.bool_(True)
        for phase in range(2):
            for n, size in zip(needs[phase], plan.classes[k][phase]):
                fits = fits & (n <= size)
        pick = jnp.where(fits, jnp.int32(k), pick)
    chosen[0] = pick

    def amount(phase, dst, src):
        return units(phase, rep, dst, src)

    def first_of(phase, z, zp, ys):
        return over[over_at(phase, rep, z, zp, ys)]

    def own_code(phase, dst, i):
        hit_at = count_at(0, rep, dst, me)
        hit = rows[hit_at * stride + jnp.minimum(i, cap)]
        code = POOL * SPAN + hit * 2 + phase
        if phase == 0:
            return code
        new_at = count_at(1, rep, dst, me)
        n = cnt[new_at]
        k = i - cnt[hit_at]
        head = (k >= n).astype(jnp.int32)
        new = rows[new_at * stride + jnp.clip(k - head * n, 0, cap)]
        return jnp.where(k >= 0, FRESH * SPAN + new * 2 + head, code)

    def fill(ref, start, n, code_of):
        def put(i, c):
            ref[start + i] = code_of(i)
            return c

        lax.fori_loop(0, n, put, 0)

    other = my_z * NY + 1 - my_y
    for phase in range(2):
        in_first, out_first = phase * plan.long_in, phase * plan.long_out

        def each(zp, c, phase=phase, in_first=in_first, out_first=out_first):
            mine, theirs, out_mine, out_theirs = c
            away = (zp != my_z).astype(jnp.int32)
            over_there = zp * NY + 1 - my_y
            along = zp * NY + my_y
            first = first_of(phase, my_z, zp, my_y)
            n = (amount(phase, over_there, me) - first) * away
            fill(in_out, in_first + mine, n, lambda i: own_code(phase, over_there, first + i))
            later = (amount(phase, along, other) - first_of(phase, my_z, zp, 1 - my_y)) * away
            row = (phase * nz + zp) * WIDE
            own = amount(phase, along, me)
            fill(z_out, row, first * away, lambda i: own_code(phase, over_there, i))
            fill(z_out, row + first, own * away, lambda i: own_code(phase, along, i))
            start = first + own
            if phase == 0:
                start = jnp.maximum(start, EARLY)
            fill(z_out, row + start, later, lambda i: HOP_IN * SPAN + theirs + i)
            out_n = first_of(phase, zp, my_z, my_y) * away
            fill(
                out_out, out_first + out_mine, out_n, lambda i: ALONG_Z * SPAN + zp * WIDE + i
            )
            out_base[phase * nz + zp] = out_theirs
            out_later = first_of(phase, zp, my_z, 1 - my_y) * away
            return mine + n, theirs + later, out_mine + out_n, out_theirs + out_later

        mine, theirs, _, _ = lax.fori_loop(0, nz, each, (none,) * 4)
        fill(
            in_out,
            in_first + mine,
            amount(phase, other, me),
            lambda i, p=phase: own_code(p, other, i),
        )
        in_base[phase] = theirs

    def place(phase, store, i):
        zs = store // NY
        straight = store - zs * NY == my_y
        first = first_of(phase, zs, my_z, my_y)
        held = first + i
        crossing = first_of(phase, zs, my_z, 1 - my_y)
        start = first + amount(phase, me, zs * NY + my_y)
        if phase == 0:
            start = jnp.maximum(start, EARLY)
        slot = jnp.where(straight, held, start + i - crossing)
        code = ALONG_Z * SPAN + zs * WIDE + slot
        late = jnp.logical_not(straight) & (i < crossing)
        code = jnp.where(late, HOP_OUT * SPAN + out_base[phase * nz + zs] + i, code)
        code = jnp.where(zs == my_z, HOP_IN * SPAN + in_base[phase] + i, code)
        return jnp.where(store == me, own_code(phase, me, i), code)

    here = rep * S + me

    def own_hit(i, c):
        store = lax.div(meta[here * plan.width + i], plan.pool_rows)
        rank = ranks[here * plan.hits + i]
        for phase in range(2):
            places[phase * plan.hits + i] = place(phase, store, rank)
        return c

    lax.fori_loop(0, plan.hits, own_hit, 0)

    def own_new(i, c):
        sender = i // WCAP
        rank = i - sender * WCAP
        n = cnt[count_at(1, rep, me, sender)]
        first = cnt[count_at(0, rep, me, sender)] + rank
        for head in range(2):
            code = place(1, sender, first + head * n)
            arrivals[i * 2 + head] = jnp.where(rank < n, code, -1)
        return c

    lax.fori_loop(0, S * WCAP, own_new, 0)


def make_schedule(plan, meta, me, rep):
    smem = pl.BlockSpec(memory_space=pltpu.SMEM)
    S, nz, reps = plan.stores, plan.nz, plan.reps
    ints = lambda *shape: jax.ShapeDtypeStruct(shape, jnp.int32)
    room = lambda n: pltpu.SMEM((n,), jnp.int32)
    return pl.pallas_call(
        functools.partial(schedule_kernel, plan),
        out_shape=(
            ints(2 * nz * WIDE),
            ints(2 * plan.long_in),
            ints(2 * plan.long_out),
            ints(2 * plan.hits),
            ints(S * WCAP * 2),
            ints(1),
        ),
        in_specs=[smem, smem],
        out_specs=(smem,) * 6,
        scratch_shapes=[
            room(reps * 2 * S * S),
            room(reps * 2 * S * S * (plan.cap + 1)),
            room(reps * S * plan.hits),
            room(reps * 2 * nz * nz * NY),
            room(reps * 2 * nz * NY),
            room(2),
            room(2 * nz),
        ],
        name="schedule",
    )(jnp.stack([me, rep]), meta)


def for_source(code, sources, act):
    kind = code // SPAN
    slot = code - kind * SPAN
    for source, ref in sources.items():
        if source == ALONG_Z:
            z = slot // WIDE
            at = slot - z * WIDE
            ends = [first for first, _ in ref[1:]] + [WIDE]
            for (first, part), end in zip(ref, ends):

                @pl.when((code >= 0) & (kind == source) & (at >= first) & (at < end))
                def _():
                    act(part.at[z, at - first])
        else:

            @pl.when((code >= 0) & (kind == source))
            def _():
                act(ref.at[slot])


def pick_kernel(names, firsts, lines, first, table, *refs):
    ins, (out, sem) = refs[: len(names)], refs[len(names) :]
    sources = {}
    for name, start, ref in zip(names, firsts, ins):
        if name == ALONG_Z:
            sources.setdefault(name, []).append((start, ref))
        else:
            sources[name] = ref
    slots = out.shape[1]
    for start in (True, False):
        for line in range(lines):

            def one(i, c):
                code = table[first + line * WIDE + i]
                dst = out.at[line, i]
                if start:
                    for_source(
                        code, sources, lambda src: pltpu.make_async_copy(src, dst, sem).start()
                    )
                else:

                    @pl.when(code >= 0)
                    def _():
                        pltpu.make_async_copy(dst, dst, sem).wait()

                return c

            lax.fori_loop(0, slots, one, 0)


def pick(table, lines, first, slots, sources, unit, dtype):
    smem = pl.BlockSpec(memory_space=pltpu.SMEM)
    far = pl.BlockSpec(memory_space=pl.ANY)
    names = [s[0] for s in sources]
    firsts = [s[1] for s in sources]
    size = lines * slots * math.prod(unit) * 2
    return pl.pallas_call(
        functools.partial(pick_kernel, names, firsts, lines, first),
        out_shape=jax.ShapeDtypeStruct((lines, slots) + unit, dtype),
        in_specs=[smem] + [far] * len(sources),
        out_specs=pl.BlockSpec(memory_space=pltpu.VMEM),
        scratch_shapes=[pltpu.SemaphoreType.DMA],
        compiler_params=pltpu.CompilerParams(vmem_limit_bytes=32 * 1024 * 1024),
        cost_estimate=pl.CostEstimate(flops=0, bytes_accessed=3 * size, transcendentals=0),
        name="pick",
    )(table, *[s[2] for s in sources])


ROWS = 256


def attend_kernel(
    plan, head, sessions, group, names, firsts, places, hit_counts, lengths, arrivals, *refs
):
    last = arrivals is not None
    refs = list(refs)
    queries, fresh_near = refs[:2]
    ins = refs[2 : 2 + len(names)]
    refs = refs[2 + len(names) :]
    if last:
        done, (out, written) = refs[: plan.ses], refs[plan.ses : plan.ses + 2]
        refs = refs[plan.ses + 2 :]
        held, vals, scores, weights, mixed, zero, kv_sem, out_sem = refs
    else:
        mixed, held, vals, scores, weights, kv_sem = refs
    sources = {}
    for name, start, ref in zip(names, firsts, ins):
        if name == ALONG_Z:
            sources.setdefault(name, []).append((start, ref))
        else:
            sources[name] = ref
    tokens, heads, dim = queries.shape
    block = fresh_near.shape[2]
    new_len = tokens // len(sessions)
    new_blocks = new_len // block
    pre = new_blocks * block
    scale = math.log2(math.e) / math.sqrt(dim)

    def fetch(s):
        def one(j, c):
            dst = held.at[s, j]
            for_source(
                places[(head * plan.ses + s) * plan.hit_len + j],
                sources,
                lambda src: pltpu.make_async_copy(src, dst, kv_sem.at[s]).start(),
            )
            return c

        lax.fori_loop(0, hit_counts[s], one, 0)

    def await_fetch(s):
        def one(j, c):
            dst = held.at[s, j]
            pltpu.make_async_copy(dst, dst, kv_sem.at[s]).wait()
            return c

        lax.fori_loop(0, hit_counts[s], one, 0)

    for s in sessions:
        fetch(s)

    if last:
        zero[...] = jnp.zeros(zero.shape, zero.dtype)

        def put_written(start):
            def one(i, c):
                dst = written.at[i // (2 * WCAP), (i // 2) % WCAP, i % 2]
                code = arrivals[i]
                if start:
                    for_source(
                        code,
                        sources,
                        lambda src: pltpu.make_async_copy(src, dst, out_sem.at[0]).start(),
                    )

                    @pl.when(code < 0)
                    def _():
                        pltpu.make_async_copy(zero, dst, out_sem.at[0]).start()
                else:
                    pltpu.make_async_copy(zero, dst, out_sem.at[0]).wait()
                return c

            lax.fori_loop(0, plan.stores * WCAP * 2, one, 0)

        put_written(True)

    vals[:, dim:] = jnp.ones((vals.shape[0], vals.shape[1] - dim), vals.dtype)
    step_tokens = ROWS // group
    assert ROWS % group == 0 and new_len % step_tokens == 0 and plan.hit_len % 2 == 0

    for at_session, s in enumerate(sessions):
        await_fetch(s)
        used = hit_counts[s]
        for b in range(new_blocks):
            vals[pl.ds(b * block, block), :dim] = fresh_near[(s * new_blocks + b) * 2 + head, 1]
        for j in range(plan.hit_len):

            @pl.when(j < used)
            def _():
                vals[pl.ds(pre + j * block, block), :dim] = held[s, j, 1]

            @pl.when(j >= used)
            def _():
                vals[pl.ds(pre + j * block, block), :dim] = jnp.zeros((block, dim), vals.dtype)

        def tile(rt, c, pairs, s=s, used=used, at_session=at_session):
            first = at_session * new_len + rt * step_tokens
            here = pl.ds(first, step_tokens)
            q = queries[here].astype(jnp.float32)[:, head * group : (head + 1) * group, :]
            q = q.reshape(ROWS, dim).astype(jnp.bfloat16)

            def dots(k):
                return lax.dot_general(
                    q, k, (((1,), (1,)), ((), ())), preferred_element_type=jnp.float32
                )

            token = rt * step_tokens + lax.broadcasted_iota(
                jnp.int32, (step_tokens, group, block), 0
            ).reshape(ROWS, block)
            lane = lax.broadcasted_iota(jnp.int32, (ROWS, block), 1)
            tops = None
            for b in range(new_blocks):
                part = dots(fresh_near[(s * new_blocks + b) * 2 + head, 0])
                part = jnp.where(b * block + lane <= token, part, -jnp.inf)
                scores[:, b * block : (b + 1) * block] = part
                tops = part if tops is None else jnp.maximum(tops, part)
            for i in range(pairs):
                part = dots(
                    jnp.concatenate([held[s, 2 * i, 0], held[s, 2 * i + 1, 0]], axis=0)
                )
                left, right = part[:, :block], part[:, block:]
                if i == pairs - 1:
                    right = jnp.where(used < 2 * pairs, -jnp.inf, right)
                at = pre + 2 * i * block
                scores[:, at : at + block] = left
                scores[:, at + block : at + 2 * block] = right
                tops = jnp.maximum(tops, jnp.maximum(left, right))
            peak = jnp.max(tops, axis=1, keepdims=True) * scale
            width = pre + 2 * pairs * block
            for at in range(0, width, block):
                part = scores[:, at : at + block]
                weights[:, at : at + block] = jnp.exp2(part * scale - peak).astype(jnp.bfloat16)
            both = jnp.dot(
                weights[:, :width], vals[:width, :], preferred_element_type=jnp.float32
            )
            result = both[:, :dim] / both[:, dim:]
            result = jnp.where(token < lengths[s], result, 0.0)
            mixed[here] = result.reshape(step_tokens, group, dim)
            return c

        need = (used + 1) // 2
        for pairs in range(1, plan.hit_len // 2 + 1):
            if pairs < plan.hit_len // 4:
                continue

            @pl.when(need == pairs)
            def _():
                lax.fori_loop(
                    0, new_len // step_tokens, functools.partial(tile, pairs=pairs), 0
                )

        if last:
            span = pl.ds(s * new_len, new_len)
            out[span] = jnp.concatenate([done[s][...], mixed[span]], axis=1).astype(jnp.bfloat16)
    if last:
        put_written(False)


def attend(
    plan, head, sessions, queries, fresh, sources, places, counts, lengths, arrivals=None, done=None
):
    smem = pl.BlockSpec(memory_space=pltpu.SMEM)
    near = pl.BlockSpec(memory_space=pltpu.VMEM)
    far = pl.BlockSpec(memory_space=pl.ANY)
    tokens, heads, dim = queries.shape
    group = heads // 2
    unit = fresh.shape[1:]
    block = unit[1]
    new_len = tokens // plan.ses
    rows = plan.hit_len * block + new_len
    last = done is not None
    names = [x[0] for x in sources]
    firsts = [x[1] for x in sources]
    kernel = functools.partial(attend_kernel, plan, head, sessions, group, names, firsts)
    scratch = [
        pltpu.VMEM((plan.ses, plan.hit_len) + unit, jnp.bfloat16),
        pltpu.VMEM((rows, 2 * dim), jnp.bfloat16),
        pltpu.VMEM((ROWS, rows), jnp.float32),
        pltpu.VMEM((ROWS, rows), jnp.bfloat16),
    ]
    mine = len(sessions) * new_len
    partial_out = jax.ShapeDtypeStruct((mine, group, dim), jnp.float32)
    arrays = [x[2] for x in sources]
    if last:
        call = dict(
            out_shape=(
                jax.ShapeDtypeStruct(queries.shape, jnp.bfloat16),
                jax.ShapeDtypeStruct((plan.stores, WCAP, 2) + unit, jnp.bfloat16),
            ),
            in_specs=[smem] * 4 + [near, near] + [far] * len(sources) + [near] * plan.ses,
            out_specs=(near, far),
            scratch_shapes=scratch
            + [
                pltpu.VMEM(partial_out.shape, jnp.float32),
                pltpu.VMEM(unit, jnp.bfloat16),
                pltpu.SemaphoreType.DMA((plan.ses,)),
                pltpu.SemaphoreType.DMA((1,)),
            ],
        )
        args = [places, counts, lengths, arrivals, queries, fresh] + arrays + list(done)
        body = kernel
    else:
        assert len(sessions) == 1
        part = pl.BlockSpec((new_len, heads, dim), lambda i: (sessions[0], 0, 0))
        call = dict(
            grid=(1,),
            out_shape=partial_out,
            in_specs=[smem] * 3 + [part, near] + [far] * len(sources),
            out_specs=near,
            scratch_shapes=scratch + [pltpu.SemaphoreType.DMA((plan.ses,))],
        )
        args = [places, counts, lengths, queries, fresh] + arrays
        body = lambda p, c, n, *refs: kernel(p, c, n, None, *refs)
    return pl.pallas_call(
        body,
        compiler_params=pltpu.CompilerParams(vmem_limit_bytes=40 * 1024 * 1024),
        cost_estimate=pl.CostEstimate(
            flops=4 * mine * group * rows * dim,
            bytes_accessed=8 * 1024 * 1024,
            transcendentals=mine * group * rows,
        ),
        name="attend",
        **call,
    )(*args)


def project(hidden, kv_weight, local_kv):
    part = jnp.einsum("ta,abhd->hbtd", hidden, kv_weight, preferred_element_type=jnp.float32)
    mine = lax.axis_index("tp")
    tp = lax.axis_size("tp")
    projected = lax.dynamic_slice_in_dim(part, mine * local_kv, local_kv, 0)
    for away in range(1, tp):
        other = lax.dynamic_slice_in_dim(part, ((mine + away) % tp) * local_kv, local_kv, 0)
        projected = projected + lax.ppermute(
            other, "tp", [(i, (i + away) % tp) for i in range(tp)]
        )
    return projected


def new_rows(projected, hit_counts, new_lengths, block_len):
    local_kv, _, tokens, dim = projected.shape
    ses_count = hit_counts.shape[0]
    new_len = tokens // ses_count
    within = jnp.arange(tokens) % new_len
    start_pos = jnp.repeat(hit_counts, new_len, total_repeat_length=tokens)
    live_len = jnp.repeat(new_lengths, new_len, total_repeat_length=tokens)
    positions = (start_pos * block_len + within).astype(jnp.float32)
    rotated = rotate(projected[:, 0], positions)
    fresh = jnp.stack([rotated, projected[:, 1]], axis=1).astype(jnp.bfloat16)
    fresh = jnp.where((within < live_len)[None, None, :, None], fresh, jnp.zeros((), jnp.bfloat16))
    fresh = fresh.reshape(local_kv, 2, tokens // block_len, block_len, dim)
    fresh = jnp.transpose(fresh, (2, 0, 1, 3, 4))
    return fresh.reshape((-1,) + fresh.shape[2:])


def along_z(plan, units):
    columns = [[z * NY + y for z in range(plan.nz)] for y in range(NY)]
    return lax.all_to_all(
        units, "store", split_axis=0, concat_axis=0, axis_index_groups=columns, tiled=True
    )


def over_y(plan, units):
    return lax.ppermute(units[0], "store", [(s, s ^ 1) for s in range(plan.stores)])


def run(plan, size, args):
    projected, queries, kv_pool, hit_counts, new_lengths, tables = args
    z_out, in_out, out_out, places, arrivals = tables
    pool_rows, local_kv, _, block_len, dim = kv_pool.shape
    unit = kv_pool.shape[2:]
    pool = kv_pool.reshape((pool_rows * local_kv,) + unit)
    take = functools.partial(pick, unit=unit, dtype=kv_pool.dtype)
    z_second = plan.nz * WIDE
    (c0, in0, out0), (c1, in1, out1) = size

    early = along_z(plan, take(z_out, plan.nz, 0, EARLY, [(POOL, 0, pool)]))
    hop0 = over_y(plan, take(in_out, 1, 0, in0, [(POOL, 0, pool)]))
    late = along_z(
        plan, take(z_out, plan.nz, EARLY, c0 - EARLY, [(POOL, 0, pool), (HOP_IN, 0, hop0)])
    )
    fresh = new_rows(projected, hit_counts, new_lengths, block_len)
    hop1 = over_y(plan, take(in_out, 1, plan.long_in, in1, [(POOL, 0, pool), (FRESH, 0, fresh)]))
    second = along_z(
        plan,
        take(z_out, plan.nz, z_second, c1, [(POOL, 0, pool), (FRESH, 0, fresh), (HOP_IN, 0, hop1)]),
    )
    came0 = [(ALONG_Z, 0, early), (ALONG_Z, EARLY, late)]
    back0 = over_y(plan, take(out_out, 1, 0, out0, came0))
    sources0 = [(POOL, 0, pool), (HOP_IN, 0, hop0), (HOP_OUT, 0, back0)] + came0
    done = [
        attend(plan, 0, [s], queries, fresh, sources0, places, hit_counts, new_lengths)
        for s in range(plan.ses)
    ]
    *first, second = lax.optimization_barrier((*done[:-1], second))
    done[:-1] = first
    came1 = [(ALONG_Z, 0, second)]
    back1 = over_y(plan, take(out_out, 1, plan.long_out, out1, came1))
    return attend(
        plan,
        1,
        list(range(plan.ses)),
        queries,
        fresh,
        [(POOL, 0, pool), (FRESH, 0, fresh), (HOP_IN, 0, hop1), (HOP_OUT, 0, back1)] + came1,
        places,
        hit_counts,
        new_lengths,
        arrivals,
        done,
    )


def local(hidden, queries, kv_weight, kv_pool, hit_ids, hit_counts, new_lengths, dest_store):
    reps = lax.axis_size("rep")
    store_count = lax.axis_size("store")
    ses_count, hit_len = hit_ids.shape
    pool_rows, local_kv, _, block_len, _ = kv_pool.shape
    per_dev = hidden.shape[0] // block_len
    assert local_kv == 2 and store_count % NY == 0
    plan = Plan(reps, store_count, ses_count, hit_len, per_dev, pool_rows)
    me = lax.axis_index("store").astype(jnp.int32)
    rep = lax.axis_index("rep").astype(jnp.int32)

    mine = jnp.concatenate([hit_ids.reshape(-1), hit_counts, dest_store.reshape(-1)])
    meta = lax.all_to_all(
        jnp.broadcast_to(mine[None], (reps * store_count, plan.width)),
        ("rep", "store"),
        split_axis=0,
        concat_axis=0,
        tiled=True,
    )
    projected = project(hidden, kv_weight, local_kv)
    *tables, chosen = make_schedule(plan, meta.reshape(-1), me, rep)
    args = (projected, queries, kv_pool, hit_counts, new_lengths, tables)
    branches = [functools.partial(run, plan, size) for size in plan.classes]
    attention, written = lax.switch(chosen[0], branches, args)
    return attention, written[None]


def solution(mesh):
    placed = (
        P(("rep", "store"), "tp"),
        P(("rep", "store"), "tp", None),
        P("tp", None, None, None),
        P(("rep", "store"), "tp", None, None, None),
        P(("rep", "store"), None),
        P(("rep", "store")),
        P(("rep", "store")),
        P(("rep", "store"), None),
    )
    return jax.shard_map(
        local,
        mesh=mesh,
        in_specs=placed,
        out_specs=(
            P(("rep", "store"), "tp", None),
            P(("rep", "store"), None, None, "tp", None, None, None),
        ),
        check_vma=False,
    )
```

```python
import functools
import math

import jax
import jax.numpy as jnp
from jax import lax
from jax.experimental import pallas as pl
from jax.experimental.pallas import tpu as pltpu
from jax.sharding import PartitionSpec as P

NY = 2
WCAP = 2
EARLY = 5

theta_base = 500000.0

SPAN_BITS, WIDE_BITS = 16, 5
SPAN = 1 << SPAN_BITS
WIDE = 1 << WIDE_BITS
POOL, FRESH, HOP_IN, HOP_NEW, ALONG_Z, HOP_OUT = range(6)


def rotate(keys, positions):
    half = keys.shape[-1] // 2
    steps = jnp.arange(half, dtype=jnp.float32)
    inverse = jnp.exp(steps * (-2.0 * math.log(theta_base) / keys.shape[-1]))
    angles = positions[:, None] * inverse[None, :]
    cosine = jnp.cos(angles)
    sine = jnp.sin(angles)
    first = keys[..., :half]
    second = keys[..., half:]
    return jnp.concatenate(
        [first * cosine - second * sine, second * cosine + first * sine], axis=-1
    )


class Plan:
    def __init__(self, reps, store_count, ses_count, hit_len, per_dev, pool_rows):
        self.reps = reps
        self.stores = store_count
        self.nz = store_count // NY
        self.ses = ses_count
        self.hit_len = hit_len
        self.hits = ses_count * hit_len
        self.per_dev = per_dev
        self.pool_rows = pool_rows
        self.cap = 2 * ((self.hits + store_count - 1) // store_count)
        self.width = self.hits + ses_count + per_dev
        nz, cap = self.nz, self.cap
        both = cap + 2 * WCAP
        self.most = (
            (max(2 * cap, EARLY + cap), nz * cap, (nz - 1) * cap),
            (2 * both, nz * cap, (nz - 1) * both),
        )
        wanted = (
            ((10, 16, 15), (13, 20, 9)),
            ((11, 16, 15), (14, 22, 11)),
            ((12, 18, 17), (16, 24, 13)),
            self.most,
        )
        self.long_in = max(m[1] for m in self.most)
        self.long_out = max(m[2] for m in self.most)
        self.new_units = 2 * per_dev
        assert max(m[0] for m in self.most) <= WIDE
        self.factor = -(-SPAN // pool_rows)
        ids = range(store_count * pool_rows)
        assert all((i * self.factor) >> SPAN_BITS == i // pool_rows for i in ids)
        self.classes = [
            tuple(
                tuple(min(a, b) for a, b in zip(size, most))
                for size, most in zip(sizes, self.most)
            )
            for sizes in wanted
        ]


def schedule_kernel(
    plan, me_ref, meta, z_out, in_out, new_out, out_out, places, arrivals, chosen,
    cnt, rows, ranks, over, hop_out_sum, in_base, new_base, out_base
):
    S, nz, cap = plan.stores, plan.nz, plan.cap
    me = me_ref[0]
    rep = me_ref[1]
    my_z = me >> 1
    my_y = me & 1
    stride = cap + 1

    def count_at(kind, group, dst, src):
        return ((group * 2 + kind) * S + dst) * S + src

    def units(phase, group, dst, src):
        n = cnt[count_at(0, group, dst, src)]
        return n if phase == 0 else n + 2 * cnt[count_at(1, group, dst, src)]

    def over_at(phase, group, z, zp, ys):
        return (((group * 2 + phase) * nz + z) * nz + zp) * NY + ys

    def store_of(block):
        return (block * plan.factor) >> SPAN_BITS

    def zero(ref, n, value=0):
        def put(i, c):
            for k in range(8):
                ref[i * 8 + k] = jnp.int32(value)
            return c

        lax.fori_loop(0, n // 8, put, 0)
        for k in range(n - n % 8, n):
            ref[k] = jnp.int32(value)

    zero(cnt, plan.reps * 2 * S * S)
    zero(hop_out_sum, plan.reps * 2 * nz * NY)
    zero(z_out, 2 * nz * WIDE, -1)
    zero(in_out, 2 * plan.long_in, -1)
    zero(new_out, plan.new_units, -1)
    zero(out_out, 2 * plan.long_out, -1)

    def scan(group, d):
        g = group * S + d
        base = g * plan.width
        for t in range(plan.ses):
            used = meta[base + plan.hits + t]
            for j in range(plan.hit_len):
                block = meta[base + t * plan.hit_len + j]
                store = store_of(block)
                at = count_at(0, group, d, store)
                rank = cnt[at]
                rows[at * stride + jnp.minimum(rank, cap)] = block - store * plan.pool_rows
                ranks[g * plan.hits + t * plan.hit_len + j] = rank
                cnt[at] = rank + (j < used).astype(jnp.int32)
        for j in range(plan.per_dev):
            dest = meta[base + plan.hits + plan.ses + j]
            at = count_at(1, group, dest, d)
            rank = cnt[at]
            rows[at * stride + jnp.minimum(rank, cap)] = j
            cnt[at] = rank + 1

    def scan_group(group, c):
        def one(d, c):
            scan(group, d)
            return c

        return lax.fori_loop(0, S, one, c)

    lax.fori_loop(0, plan.reps, scan_group, 0)

    def balance(group, z, c):
        c = list(c)
        for phase in range(2):
            longest, most_in = c[2 * phase], c[2 * phase + 1]
            going = [units(0, group, z * NY + 1 - y, z * NY + y) for y in range(NY)]
            for zp in range(nz):
                a = [
                    [units(phase, group, zp * NY + yd, z * NY + ys) for yd in range(NY)]
                    for ys in range(NY)
                ]
                half = (a[0][0] + a[0][1] + a[1][0] + a[1][1] + 1) >> 1
                if phase == 0:
                    excess = [a[y][y] + a[y][1 - y] - half for y in range(NY)]
                    first = [
                        a[y][1 - y] - jnp.minimum(jnp.maximum(excess[y], 0), a[y][1 - y])
                        for y in range(NY)
                    ]
                else:
                    excess = [a[y][y] + a[1 - y][y] - half for y in range(NY)]
                    first = [
                        jnp.minimum(jnp.maximum(excess[1 - y], 0), a[y][1 - y]) for y in range(NY)
                    ]
                away = zp != z
                for y in range(NY):
                    over[over_at(phase, group, z, zp, y)] = first[y]
                    later = a[1 - y][y] - first[1 - y]
                    own = a[y][y] + first[y]
                    start = jnp.maximum(own, EARLY) if phase == 0 else own
                    end = jnp.where(later > 0, start + later, own)
                    longest = jnp.where(away, jnp.maximum(longest, end), longest)
                    hop = later
                    if phase == 1:
                        hits = units(0, group, zp * NY + y, z * NY + 1 - y)
                        hop = jnp.maximum(hits - first[1 - y], 0)
                    going[1 - y] = going[1 - y] + jnp.where(away, hop, 0)
                    at = ((group * 2 + phase) * nz + zp) * NY + y
                    hop_out_sum[at] = hop_out_sum[at] + jnp.where(away, first[y], 0)
            c[2 * phase] = longest
            c[2 * phase + 1] = jnp.maximum(most_in, jnp.maximum(going[0], going[1]))
        return tuple(c)

    none = jnp.int32(0)
    need = lax.fori_loop(
        0,
        plan.reps,
        lambda group, c: lax.fori_loop(0, nz, functools.partial(balance, group), c),
        (none,) * 4,
    )
    out_need = []
    for phase in range(2):

        def top(group, c, phase=phase):
            for i in range(nz * NY):
                c = jnp.maximum(c, hop_out_sum[(group * 2 + phase) * nz * NY + i])
            return c

        out_need.append(lax.fori_loop(0, plan.reps, top, none))
    needs = ((need[0], need[1], out_need[0]), (need[2], need[3], out_need[1]))
    pick = jnp.int32(len(plan.classes) - 1)
    for k in reversed(range(len(plan.classes) - 1)):
        fits = jnp.bool_(True)
        for phase in range(2):
            for n, size in zip(needs[phase], plan.classes[k][phase]):
                fits = fits & (n <= size)
        pick = jnp.where(fits, jnp.int32(k), pick)
    chosen[0] = pick

    def amount(phase, dst, src):
        return units(phase, rep, dst, src)

    def first_of(phase, z, zp, ys):
        return over[over_at(phase, rep, z, zp, ys)]

    def own_code(phase, dst, i):
        hit_at = count_at(0, rep, dst, me)
        hit = rows[hit_at * stride + jnp.minimum(i, cap)]
        code = POOL * SPAN + hit * 2 + phase
        if phase == 0:
            return code
        new_at = count_at(1, rep, dst, me)
        n = cnt[new_at]
        k = i - cnt[hit_at]
        head = (k >= n).astype(jnp.int32)
        new = rows[new_at * stride + jnp.clip(k - head * n, 0, cap)]
        return jnp.where(k >= 0, FRESH * SPAN + new * 2 + head, code)

    def fill(ref, start, n, code_of):
        def put(i, c):
            ref[start + i] = code_of(i)
            return c

        lax.fori_loop(0, n, put, 0)

    other = my_z * NY + 1 - my_y
    for phase in range(2):
        in_first, out_first = phase * plan.long_in, phase * plan.long_out

        def each(zp, c, phase=phase, in_first=in_first, out_first=out_first):
            mine, theirs, new_mine, new_theirs, out_mine, out_theirs = c
            away = (zp != my_z).astype(jnp.int32)
            over_there = zp * NY + 1 - my_y
            along = zp * NY + my_y
            first = first_of(phase, my_z, zp, my_y)
            hits = amount(0, over_there, me)
            n = jnp.maximum(hits - first, 0) * away
            fill(in_out, in_first + mine, n, lambda i: own_code(phase, over_there, first + i))
            their_first = first_of(phase, my_z, zp, 1 - my_y)
            their_hits = amount(0, along, other)
            later = jnp.maximum(their_hits - their_first, 0) * away
            new_n, new_later = 0, 0
            if phase == 1:
                skip = jnp.maximum(first, hits)
                new_n = (amount(1, over_there, me) - skip) * away
                fill(new_out, new_mine, new_n, lambda i: own_code(1, over_there, skip + i))
                new_later = amount(1, along, other) - jnp.maximum(their_first, their_hits)
                new_later = new_later * away
            row = (phase * nz + zp) * WIDE
            own = amount(phase, along, me)
            fill(z_out, row, first * away, lambda i: own_code(phase, over_there, i))
            fill(z_out, row + first, own * away, lambda i: own_code(phase, along, i))
            start = first + own
            if phase == 0:
                start = jnp.maximum(start, EARLY)
            fill(z_out, row + start, later, lambda i: HOP_IN * SPAN + theirs + i)
            if phase == 1:
                fill(
                    z_out,
                    row + start + later,
                    new_later,
                    lambda i: HOP_NEW * SPAN + new_theirs + i,
                )
            out_n = first_of(phase, zp, my_z, my_y) * away
            fill(
                out_out, out_first + out_mine, out_n, lambda i: ALONG_Z * SPAN + zp * WIDE + i
            )
            out_base[phase * nz + zp] = out_theirs
            out_later = first_of(phase, zp, my_z, 1 - my_y) * away
            return (
                mine + n,
                theirs + later,
                new_mine + new_n,
                new_theirs + new_later,
                out_mine + out_n,
                out_theirs + out_later,
            )

        mine, theirs, new_mine, new_theirs, _, _ = lax.fori_loop(0, nz, each, (none,) * 6)
        hits = amount(0, other, me)
        fill(in_out, in_first + mine, hits, lambda i, p=phase: own_code(p, other, i))
        in_base[phase] = theirs
        if phase == 1:
            fill(new_out, new_mine, amount(1, other, me) - hits, lambda i: own_code(1, other, hits + i))
            new_base[0] = new_theirs

    def place(phase, store, i):
        zs = store >> 1
        straight = (store & 1) == my_y
        first = first_of(phase, zs, my_z, my_y)
        held = first + i
        crossing = first_of(phase, zs, my_z, 1 - my_y)
        start = first + amount(phase, me, zs * NY + my_y)
        if phase == 0:
            start = jnp.maximum(start, EARLY)
        slot = jnp.where(straight, held, start + i - crossing)
        code = ALONG_Z * SPAN + zs * WIDE + slot
        late = jnp.logical_not(straight) & (i < crossing)
        code = jnp.where(late, HOP_OUT * SPAN + out_base[phase * nz + zs] + i, code)
        near = HOP_IN * SPAN + in_base[phase] + i
        if phase == 1:
            hits = amount(0, me, store)
            near = jnp.where(i < hits, near, HOP_NEW * SPAN + new_base[0] + i - hits)
        code = jnp.where(zs == my_z, near, code)
        return jnp.where(store == me, own_code(phase, me, i), code)

    here = rep * S + me

    def own_hit(i, c):
        store = store_of(meta[here * plan.width + i])
        rank = ranks[here * plan.hits + i]
        for phase in range(2):
            places[phase * plan.hits + i] = place(phase, store, rank)
        return c

    lax.fori_loop(0, plan.hits, own_hit, 0)

    def own_new(i, c):
        sender = i >> 1
        rank = i & 1
        n = cnt[count_at(1, rep, me, sender)]
        first = cnt[count_at(0, rep, me, sender)] + rank
        for head in range(2):
            code = place(1, sender, first + head * n)
            arrivals[i * 2 + head] = jnp.where(rank < n, code, -1)
        return c

    lax.fori_loop(0, S * WCAP, own_new, 0)


def make_schedule(plan, meta, me, rep):
    smem = pl.BlockSpec(memory_space=pltpu.SMEM)
    S, nz, reps = plan.stores, plan.nz, plan.reps
    ints = lambda *shape: jax.ShapeDtypeStruct(shape, jnp.int32)
    room = lambda n: pltpu.SMEM((n,), jnp.int32)
    return pl.pallas_call(
        functools.partial(schedule_kernel, plan),
        out_shape=(
            ints(2 * nz * WIDE),
            ints(2 * plan.long_in),
            ints(plan.new_units),
            ints(2 * plan.long_out),
            ints(2 * plan.hits),
            ints(S * WCAP * 2),
            ints(1),
        ),
        in_specs=[smem, smem],
        out_specs=(smem,) * 7,
        scratch_shapes=[
            room(reps * 2 * S * S),
            room(reps * 2 * S * S * (plan.cap + 1)),
            room(reps * S * plan.hits),
            room(reps * 2 * nz * nz * NY),
            room(reps * 2 * nz * NY),
            room(2),
            room(1),
            room(2 * nz),
        ],
        name="schedule",
    )(jnp.stack([me, rep]), meta)


def for_source(code, sources, act):
    kind = code >> SPAN_BITS
    slot = code & (SPAN - 1)
    for source, ref in sources.items():
        if source == ALONG_Z:
            z = slot >> WIDE_BITS
            at = slot & (WIDE - 1)
            ends = [first for first, _ in ref[1:]] + [WIDE]
            for (first, part), end in zip(ref, ends):

                @pl.when((code >= 0) & (kind == source) & (at >= first) & (at < end))
                def _():
                    act(part.at[z, at - first])
        else:

            @pl.when((code >= 0) & (kind == source))
            def _():
                act(ref.at[slot])


def pick_kernel(names, firsts, lines, first, table, *refs):
    ins, (out, sem) = refs[: len(names)], refs[len(names) :]
    sources = {}
    for name, start, ref in zip(names, firsts, ins):
        if name == ALONG_Z:
            sources.setdefault(name, []).append((start, ref))
        else:
            sources[name] = ref
    slots = out.shape[1]
    for start in (True, False):
        for line in range(lines):

            def one(i, c):
                code = table[first + line * WIDE + i]
                dst = out.at[line, i]
                if start:
                    for_source(
                        code, sources, lambda src: pltpu.make_async_copy(src, dst, sem).start()
                    )
                else:

                    @pl.when(code >= 0)
                    def _():
                        pltpu.make_async_copy(dst, dst, sem).wait()

                return c

            lax.fori_loop(0, slots, one, 0)


def pick(table, lines, first, slots, sources, unit, dtype):
    smem = pl.BlockSpec(memory_space=pltpu.SMEM)
    far = pl.BlockSpec(memory_space=pl.ANY)
    names = [s[0] for s in sources]
    firsts = [s[1] for s in sources]
    size = lines * slots * math.prod(unit) * 2
    return pl.pallas_call(
        functools.partial(pick_kernel, names, firsts, lines, first),
        out_shape=jax.ShapeDtypeStruct((lines, slots) + unit, dtype),
        in_specs=[smem] + [far] * len(sources),
        out_specs=pl.BlockSpec(memory_space=pltpu.VMEM),
        scratch_shapes=[pltpu.SemaphoreType.DMA],
        compiler_params=pltpu.CompilerParams(vmem_limit_bytes=32 * 1024 * 1024),
        cost_estimate=pl.CostEstimate(flops=0, bytes_accessed=3 * size, transcendentals=0),
        name="pick",
    )(table, *[s[2] for s in sources])


ROWS = 256


def attend_kernel(
    plan, head, sessions, group, names, firsts, places, hit_counts, lengths, arrivals, *refs
):
    last = arrivals is not None
    refs = list(refs)
    queries, fresh_near = refs[:2]
    ins = refs[2 : 2 + len(names)]
    refs = refs[2 + len(names) :]
    if last:
        done, (out, written) = refs[: plan.ses], refs[plan.ses : plan.ses + 2]
        refs = refs[plan.ses + 2 :]
        held, vals, scores, weights, mixed, zero, kv_sem, out_sem = refs
    else:
        mixed, held, vals, scores, weights, kv_sem = refs
    sources = {}
    for name, start, ref in zip(names, firsts, ins):
        if name == ALONG_Z:
            sources.setdefault(name, []).append((start, ref))
        else:
            sources[name] = ref
    tokens, heads, dim = queries.shape
    block = fresh_near.shape[2]
    new_len = tokens // len(sessions)
    new_blocks = new_len // block
    pre = new_blocks * block
    scale = math.log2(math.e) / math.sqrt(dim)

    def fetch(s):
        def one(j, c):
            dst = held.at[s, j]
            for_source(
                places[(head * plan.ses + s) * plan.hit_len + j],
                sources,
                lambda src: pltpu.make_async_copy(src, dst, kv_sem.at[s]).start(),
            )
            return c

        lax.fori_loop(0, hit_counts[s], one, 0)

    def await_fetch(s):
        def one(j, c):
            dst = held.at[s, j]
            pltpu.make_async_copy(dst, dst, kv_sem.at[s]).wait()
            return c

        lax.fori_loop(0, hit_counts[s], one, 0)

    for s in sessions:
        fetch(s)

    if last:
        zero[...] = jnp.zeros(zero.shape, zero.dtype)

        def put_written(start):
            def one(i, c):
                dst = written.at[i >> 2, (i >> 1) & 1, i & 1]
                code = arrivals[i]
                if start:
                    for_source(
                        code,
                        sources,
                        lambda src: pltpu.make_async_copy(src, dst, out_sem.at[0]).start(),
                    )

                    @pl.when(code < 0)
                    def _():
                        pltpu.make_async_copy(zero, dst, out_sem.at[0]).start()
                else:
                    pltpu.make_async_copy(zero, dst, out_sem.at[0]).wait()
                return c

            lax.fori_loop(0, plan.stores * WCAP * 2, one, 0)

        put_written(True)

    vals[:, dim:] = jnp.ones((vals.shape[0], vals.shape[1] - dim), vals.dtype)
    step_tokens = ROWS // group
    assert ROWS % group == 0 and new_len % (2 * step_tokens) == 0 and new_blocks % 2 == 0 and plan.hit_len % 2 == 0

    for at_session, s in enumerate(sessions):
        await_fetch(s)
        used = hit_counts[s]
        for b in range(new_blocks):
            vals[pl.ds(b * block, block), :dim] = fresh_near[(s * new_blocks + b) * 2 + head, 1]
        for j in range(plan.hit_len):

            @pl.when(j < used)
            def _():
                vals[pl.ds(pre + j * block, block), :dim] = held[s, j, 1]

            @pl.when(j >= used)
            def _():
                vals[pl.ds(pre + j * block, block), :dim] = jnp.zeros((block, dim), vals.dtype)

        def two_tiles(u, c, pairs, s=s, used=used, at_session=at_session):
            width = pre + 2 * pairs * block
            lane = lax.broadcasted_iota(jnp.int32, (ROWS, block), 1)

            def begin(part):
                rt = u * 2 + part
                here = pl.ds(at_session * new_len + rt * step_tokens, step_tokens)
                q = queries[here].astype(jnp.float32)[:, head * group : (head + 1) * group, :]
                token = rt * step_tokens + lax.broadcasted_iota(
                    jnp.int32, (step_tokens, group, block), 0
                ).reshape(ROWS, block)
                return here, q.reshape(ROWS, dim).astype(jnp.bfloat16), token

            def score(part, q, token, i, tops):
                if i < new_blocks // 2:
                    keys = [fresh_near[(s * new_blocks + 2 * i + b) * 2 + head, 0] for b in range(2)]
                else:
                    j = 2 * i - new_blocks
                    keys = [held[s, j, 0], held[s, j + 1, 0]]
                both = lax.dot_general(
                    q,
                    jnp.concatenate(keys, axis=0),
                    (((1,), (1,)), ((), ())),
                    preferred_element_type=jnp.float32,
                )
                halves = [both[:, :block], both[:, block:]]
                if i < new_blocks // 2:
                    halves = [
                        jnp.where((2 * i + b) * block + lane <= token, halves[b], -jnp.inf)
                        for b in range(2)
                    ]
                elif i == width // (2 * block) - 1:
                    halves[1] = jnp.where(used < 2 * pairs, -jnp.inf, halves[1])
                for b in range(2):
                    at = (2 * i + b) * block
                    scores[part, :, at : at + block] = halves[b]
                top = jnp.maximum(halves[0], halves[1])
                return top if tops is None else jnp.maximum(tops, top)

            def weigh(part, peak, i):
                for b in range(2):
                    at = (2 * i + b) * block
                    x = scores[part, :, at : at + block] * scale - peak
                    weights[part, :, at : at + block] = jnp.exp2(x).astype(jnp.bfloat16)

            def finish(part, here, token):
                both = jnp.dot(
                    weights[part, :, :width], vals[:width, :], preferred_element_type=jnp.float32
                )
                result = both[:, :dim] / both[:, dim:]
                result = jnp.where(token < lengths[s], result, 0.0)
                mixed[here] = result.reshape(step_tokens, group, dim)

            def peak_of(tops):
                return jnp.max(tops, axis=1, keepdims=True) * scale

            chunks = range(width // (2 * block))
            here0, q0, token0 = begin(0)
            here1, q1, token1 = begin(1)
            tops0, tops1 = None, None
            for i in chunks:
                tops0 = score(0, q0, token0, i, tops0)
            peak0 = peak_of(tops0)
            for i in chunks:
                tops1 = score(1, q1, token1, i, tops1)
                weigh(0, peak0, i)
            peak1 = peak_of(tops1)
            finish(0, here0, token0)
            for i in chunks:
                weigh(1, peak1, i)
            finish(1, here1, token1)
            return c

        need = (used + 1) >> 1
        for pairs in range(1, plan.hit_len // 2 + 1):
            if pairs < plan.hit_len // 4:
                continue

            @pl.when(need == pairs)
            def _():
                lax.fori_loop(
                    0,
                    new_len // (2 * step_tokens),
                    functools.partial(two_tiles, pairs=pairs),
                    0,
                )

        if last:
            span = pl.ds(s * new_len, new_len)
            out[span] = jnp.concatenate([done[s][...], mixed[span]], axis=1).astype(jnp.bfloat16)
    if last:
        put_written(False)


def attend(
    plan, head, sessions, queries, fresh, sources, places, counts, lengths, arrivals=None, done=None
):
    smem = pl.BlockSpec(memory_space=pltpu.SMEM)
    near = pl.BlockSpec(memory_space=pltpu.VMEM)
    far = pl.BlockSpec(memory_space=pl.ANY)
    tokens, heads, dim = queries.shape
    group = heads // 2
    unit = fresh.shape[1:]
    block = unit[1]
    new_len = tokens // plan.ses
    rows = plan.hit_len * block + new_len
    last = done is not None
    names = [x[0] for x in sources]
    firsts = [x[1] for x in sources]
    kernel = functools.partial(attend_kernel, plan, head, sessions, group, names, firsts)
    scratch = [
        pltpu.VMEM((plan.ses, plan.hit_len) + unit, jnp.bfloat16),
        pltpu.VMEM((rows, 2 * dim), jnp.bfloat16),
        pltpu.VMEM((2, ROWS, rows), jnp.float32),
        pltpu.VMEM((2, ROWS, rows), jnp.bfloat16),
    ]
    mine = len(sessions) * new_len
    partial_out = jax.ShapeDtypeStruct((mine, group, dim), jnp.float32)
    arrays = [x[2] for x in sources]
    if last:
        call = dict(
            out_shape=(
                jax.ShapeDtypeStruct(queries.shape, jnp.bfloat16),
                jax.ShapeDtypeStruct((plan.stores, WCAP, 2) + unit, jnp.bfloat16),
            ),
            in_specs=[smem] * 4 + [near, near] + [far] * len(sources) + [near] * plan.ses,
            out_specs=(near, far),
            scratch_shapes=scratch
            + [
                pltpu.VMEM(partial_out.shape, jnp.float32),
                pltpu.VMEM(unit, jnp.bfloat16),
                pltpu.SemaphoreType.DMA((plan.ses,)),
                pltpu.SemaphoreType.DMA((1,)),
            ],
        )
        args = [places, counts, lengths, arrivals, queries, fresh] + arrays + list(done)
        body = kernel
    else:
        assert len(sessions) == 1
        part = pl.BlockSpec((new_len, heads, dim), lambda i: (sessions[0], 0, 0))
        call = dict(
            grid=(1,),
            out_shape=partial_out,
            in_specs=[smem] * 3 + [part, near] + [far] * len(sources),
            out_specs=near,
            scratch_shapes=scratch + [pltpu.SemaphoreType.DMA((plan.ses,))],
        )
        args = [places, counts, lengths, queries, fresh] + arrays
        body = lambda p, c, n, *refs: kernel(p, c, n, None, *refs)
    return pl.pallas_call(
        body,
        compiler_params=pltpu.CompilerParams(vmem_limit_bytes=40 * 1024 * 1024),
        cost_estimate=pl.CostEstimate(
            flops=4 * mine * group * rows * dim,
            bytes_accessed=8 * 1024 * 1024,
            transcendentals=mine * group * rows,
        ),
        name="attend",
        **call,
    )(*args)


def project(hidden, kv_weight, local_kv):
    part = jnp.einsum("ta,abhd->hbtd", hidden, kv_weight, preferred_element_type=jnp.float32)
    mine = lax.axis_index("tp")
    tp = lax.axis_size("tp")
    projected = lax.dynamic_slice_in_dim(part, mine * local_kv, local_kv, 0)
    for away in range(1, tp):
        other = lax.dynamic_slice_in_dim(part, ((mine + away) % tp) * local_kv, local_kv, 0)
        projected = projected + lax.ppermute(
            other, "tp", [(i, (i + away) % tp) for i in range(tp)]
        )
    return projected


def new_rows(projected, hit_counts, new_lengths, block_len):
    local_kv, _, tokens, dim = projected.shape
    ses_count = hit_counts.shape[0]
    new_len = tokens // ses_count
    within = jnp.arange(tokens) % new_len
    start_pos = jnp.repeat(hit_counts, new_len, total_repeat_length=tokens)
    live_len = jnp.repeat(new_lengths, new_len, total_repeat_length=tokens)
    positions = (start_pos * block_len + within).astype(jnp.float32)
    rotated = rotate(projected[:, 0], positions)
    fresh = jnp.stack([rotated, projected[:, 1]], axis=1).astype(jnp.bfloat16)
    fresh = jnp.where((within < live_len)[None, None, :, None], fresh, jnp.zeros((), jnp.bfloat16))
    fresh = fresh.reshape(local_kv, 2, tokens // block_len, block_len, dim)
    fresh = jnp.transpose(fresh, (2, 0, 1, 3, 4))
    return fresh.reshape((-1,) + fresh.shape[2:])


def along_z(plan, units):
    columns = [[z * NY + y for z in range(plan.nz)] for y in range(NY)]
    return lax.all_to_all(
        units, "store", split_axis=0, concat_axis=0, axis_index_groups=columns, tiled=True
    )


def over_y(plan, units):
    return lax.ppermute(units[0], "store", [(s, s ^ 1) for s in range(plan.stores)])


def run(plan, size, args):
    hidden, queries, kv_weight, kv_pool, hit_counts, new_lengths, tables = args
    z_out, in_out, new_out, out_out, places, arrivals = tables
    pool_rows, local_kv, _, block_len, dim = kv_pool.shape
    unit = kv_pool.shape[2:]
    pool = kv_pool.reshape((pool_rows * local_kv,) + unit)
    take = functools.partial(pick, unit=unit, dtype=kv_pool.dtype)
    z_second = plan.nz * WIDE
    (c0, in0, out0), (c1, in1, out1) = size

    early = along_z(plan, take(z_out, plan.nz, 0, EARLY, [(POOL, 0, pool)]))
    hop0 = over_y(plan, take(in_out, 1, 0, in0, [(POOL, 0, pool)]))
    sent1 = take(in_out, 1, plan.long_in, in1, [(POOL, 0, pool)])
    hop1 = over_y(plan, sent1)
    hop0, _ = lax.optimization_barrier((hop0, sent1))
    late = along_z(
        plan, take(z_out, plan.nz, EARLY, c0 - EARLY, [(POOL, 0, pool), (HOP_IN, 0, hop0)])
    )
    projected = project(hidden, kv_weight, local_kv)
    fresh = new_rows(projected, hit_counts, new_lengths, block_len)
    hop_new = over_y(plan, take(new_out, 1, 0, plan.new_units, [(FRESH, 0, fresh)]))
    ready1 = [(POOL, 0, pool), (FRESH, 0, fresh), (HOP_IN, 0, hop1), (HOP_NEW, 0, hop_new)]
    second = along_z(plan, take(z_out, plan.nz, z_second, c1, ready1))
    came0 = [(ALONG_Z, 0, early), (ALONG_Z, EARLY, late)]
    back0 = over_y(plan, take(out_out, 1, 0, out0, came0))
    sources0 = [(POOL, 0, pool), (HOP_IN, 0, hop0), (HOP_OUT, 0, back0)] + came0
    done = [
        attend(plan, 0, [s], queries, fresh, sources0, places, hit_counts, new_lengths)
        for s in range(plan.ses)
    ]
    *first, second = lax.optimization_barrier((*done[:-1], second))
    done[:-1] = first
    came1 = [(ALONG_Z, 0, second)]
    back1 = over_y(plan, take(out_out, 1, plan.long_out, out1, came1))
    return attend(
        plan,
        1,
        list(range(plan.ses)),
        queries,
        fresh,
        ready1 + [(HOP_OUT, 0, back1)] + came1,
        places,
        hit_counts,
        new_lengths,
        arrivals,
        done,
    )


def local(hidden, queries, kv_weight, kv_pool, hit_ids, hit_counts, new_lengths, dest_store):
    reps = lax.axis_size("rep")
    store_count = lax.axis_size("store")
    ses_count, hit_len = hit_ids.shape
    pool_rows, local_kv, _, block_len, _ = kv_pool.shape
    per_dev = hidden.shape[0] // block_len
    assert local_kv == 2 and store_count % NY == 0
    plan = Plan(reps, store_count, ses_count, hit_len, per_dev, pool_rows)
    me = lax.axis_index("store").astype(jnp.int32)
    rep = lax.axis_index("rep").astype(jnp.int32)

    mine = jnp.concatenate([hit_ids.reshape(-1), hit_counts, dest_store.reshape(-1)])
    meta = lax.all_to_all(
        jnp.broadcast_to(mine[None], (reps * store_count, plan.width)),
        ("rep", "store"),
        split_axis=0,
        concat_axis=0,
        tiled=True,
    )
    *tables, chosen = make_schedule(plan, meta.reshape(-1), me, rep)
    args = (hidden, queries, kv_weight, kv_pool, hit_counts, new_lengths, tables)
    branches = [functools.partial(run, plan, size) for size in plan.classes]
    attention, written = lax.switch(chosen[0], branches, args)
    return attention, written[None]


def solution(mesh):
    placed = (
        P(("rep", "store"), "tp"),
        P(("rep", "store"), "tp", None),
        P("tp", None, None, None),
        P(("rep", "store"), "tp", None, None, None),
        P(("rep", "store"), None),
        P(("rep", "store")),
        P(("rep", "store")),
        P(("rep", "store"), None),
    )
    return jax.shard_map(
        local,
        mesh=mesh,
        in_specs=placed,
        out_specs=(
            P(("rep", "store"), "tp", None),
            P(("rep", "store"), None, None, "tp", None, None, None),
        ),
        check_vma=False,
    )
```

```python
import functools
import math

import jax
import jax.numpy as jnp
from jax import lax
from jax.experimental import pallas as pl
from jax.experimental.pallas import tpu as pltpu
from jax.sharding import PartitionSpec as P

NY = 2
WCAP = 2
EARLY = 5
SPLIT = 7

theta_base = 500000.0

SPAN_BITS, WIDE_BITS = 16, 5
SPAN = 1 << SPAN_BITS
WIDE = 1 << WIDE_BITS
POOL, FRESH, HOP_IN, HOP_NEW, HOP_SAME, ALONG_Z, HOP_OUT = range(7)


def rotate(keys, positions):
    half = keys.shape[-1] // 2
    steps = jnp.arange(half, dtype=jnp.float32)
    inverse = jnp.exp(steps * (-2.0 * math.log(theta_base) / keys.shape[-1]))
    angles = positions[:, None] * inverse[None, :]
    cosine = jnp.cos(angles)
    sine = jnp.sin(angles)
    first = keys[..., :half]
    second = keys[..., half:]
    return jnp.concatenate(
        [first * cosine - second * sine, second * cosine + first * sine], axis=-1
    )


class Plan:
    def __init__(self, reps, store_count, ses_count, hit_len, per_dev, pool_rows):
        self.reps = reps
        self.stores = store_count
        self.nz = store_count // NY
        self.ses = ses_count
        self.hit_len = hit_len
        self.hits = ses_count * hit_len
        self.per_dev = per_dev
        self.pool_rows = pool_rows
        self.cap = 2 * ((self.hits + store_count - 1) // store_count)
        self.line = hit_len + 1 + per_dev // ses_count
        self.width = ses_count * self.line
        nz, cap = self.nz, self.cap
        both = cap + 2 * WCAP
        self.most = (
            (max(2 * cap, EARLY + cap), (nz - 1) * cap, (nz - 1) * cap),
            (max(2 * both, SPLIT + both), (nz - 1) * cap, (nz - 1) * both),
        )
        wanted = (
            ((10, 9, 15), (13, 15, 9)),
            ((11, 10, 15), (14, 17, 10)),
            ((12, 11, 17), (15, 18, 11)),
            ((13, 13, 18), (17, 21, 13)),
            self.most,
        )
        self.long_in = max(m[1] for m in self.most)
        self.long_out = max(m[2] for m in self.most)
        self.new_units = 2 * per_dev
        assert max(m[0] for m in self.most) <= WIDE
        self.factor = -(-SPAN // pool_rows)
        ids = range(store_count * pool_rows)
        assert all((i * self.factor) >> SPAN_BITS == i // pool_rows for i in ids)
        self.classes = [
            tuple(
                tuple(min(a, b) for a, b in zip(size, most))
                for size, most in zip(sizes, self.most)
            )
            for sizes in wanted
        ]


def schedule_kernel(
    plan, me_ref, meta, z_out, in_out, new_out, same_out, out_out, places, arrivals, chosen,
    cnt, rows, ranks, over, hop_out_sum, new_base, out_base
):
    S, nz, cap = plan.stores, plan.nz, plan.cap
    me = me_ref[0]
    rep = me_ref[1]
    my_z = me >> 1
    my_y = me & 1
    stride = cap + 1

    def count_at(kind, group, dst, src):
        return ((group * 2 + kind) * S + dst) * S + src

    def units(phase, group, dst, src):
        n = cnt[count_at(0, group, dst, src)]
        return n if phase == 0 else n + 2 * cnt[count_at(1, group, dst, src)]

    def over_at(phase, group, z, zp, ys):
        return (((group * 2 + phase) * nz + z) * nz + zp) * NY + ys

    def store_of(block):
        return (block * plan.factor) >> SPAN_BITS

    def zero(ref, n, value=0):
        def put(i, c):
            for k in range(8):
                ref[i * 8 + k] = jnp.int32(value)
            return c

        lax.fori_loop(0, n // 8, put, 0)
        for k in range(n - n % 8, n):
            ref[k] = jnp.int32(value)

    zero(cnt, plan.reps * 2 * S * S)
    zero(hop_out_sum, plan.reps * 2 * nz * NY)
    zero(z_out, 2 * nz * WIDE, -1)
    zero(in_out, 2 * plan.long_in, -1)
    zero(new_out, plan.new_units, -1)
    zero(same_out, 2 * plan.cap, -1)
    zero(out_out, 2 * plan.long_out, -1)

    def scan(group, d):
        g = group * S + d
        base = g * plan.width
        for t in range(plan.ses):
            line = base + t * plan.line
            used = meta[line + plan.hit_len]
            for j in range(plan.hit_len):
                block = meta[line + j]
                store = store_of(block)
                at = count_at(0, group, d, store)
                rank = cnt[at]
                rows[at * stride + jnp.minimum(rank, cap)] = block - store * plan.pool_rows
                ranks[g * plan.hits + t * plan.hit_len + j] = rank
                cnt[at] = rank + (j < used).astype(jnp.int32)
        for j in range(plan.per_dev):
            t, k = divmod(j, plan.per_dev // plan.ses)
            dest = meta[base + t * plan.line + plan.hit_len + 1 + k]
            at = count_at(1, group, dest, d)
            rank = cnt[at]
            rows[at * stride + jnp.minimum(rank, cap)] = j
            cnt[at] = rank + 1

    def scan_group(group, c):
        def one(d, c):
            scan(group, d)
            return c

        return lax.fori_loop(0, S, one, c)

    lax.fori_loop(0, plan.reps, scan_group, 0)

    none = jnp.int32(0)

    def balance(group, z, c):
        c = list(c)
        for phase in range(2):
            longest, most_in = c[2 * phase], c[2 * phase + 1]
            going = [none, none]
            for zp in range(nz):
                a = [
                    [units(phase, group, zp * NY + yd, z * NY + ys) for yd in range(NY)]
                    for ys in range(NY)
                ]
                half = (a[0][0] + a[0][1] + a[1][0] + a[1][1] + 1) >> 1
                if phase == 0:
                    excess = [a[y][y] + a[y][1 - y] - half for y in range(NY)]
                    first = [
                        a[y][1 - y] - jnp.minimum(jnp.maximum(excess[y], 0), a[y][1 - y])
                        for y in range(NY)
                    ]
                else:
                    excess = [a[y][y] + a[1 - y][y] - half for y in range(NY)]
                    first = [
                        jnp.minimum(jnp.maximum(excess[1 - y], 0), a[y][1 - y]) for y in range(NY)
                    ]
                away = zp != z
                for y in range(NY):
                    over[over_at(phase, group, z, zp, y)] = first[y]
                    later = a[1 - y][y] - first[1 - y]
                    own = a[y][y] + first[y]
                    start = jnp.maximum(own, EARLY) if phase == 0 else own
                    hop = later
                    if phase == 1:
                        hits = units(0, group, zp * NY + y, z * NY + 1 - y)
                        hop = jnp.maximum(hits - first[1 - y], 0)
                    end = jnp.where(hop > 0, start + hop, own)
                    if phase == 1:
                        new_hop = later - hop
                        end = jnp.where(new_hop > 0, jnp.maximum(end, SPLIT) + new_hop, end)
                    longest = jnp.where(away, jnp.maximum(longest, end), longest)
                    going[1 - y] = going[1 - y] + jnp.where(away, hop, 0)
                    at = ((group * 2 + phase) * nz + zp) * NY + y
                    hop_out_sum[at] = hop_out_sum[at] + jnp.where(away, first[y], 0)
            c[2 * phase] = longest
            c[2 * phase + 1] = jnp.maximum(most_in, jnp.maximum(going[0], going[1]))
        return tuple(c)

    need = lax.fori_loop(
        0,
        plan.reps,
        lambda group, c: lax.fori_loop(0, nz, functools.partial(balance, group), c),
        (none,) * 4,
    )
    out_need = []
    for phase in range(2):

        def top(group, c, phase=phase):
            for i in range(nz * NY):
                c = jnp.maximum(c, hop_out_sum[(group * 2 + phase) * nz * NY + i])
            return c

        out_need.append(lax.fori_loop(0, plan.reps, top, none))
    needs = ((need[0], need[1], out_need[0]), (need[2], need[3], out_need[1]))
    pick = jnp.int32(len(plan.classes) - 1)
    for k in reversed(range(len(plan.classes) - 1)):
        fits = jnp.bool_(True)
        for phase in range(2):
            for n, size in zip(needs[phase], plan.classes[k][phase]):
                fits = fits & (n <= size)
        pick = jnp.where(fits, jnp.int32(k), pick)
    chosen[0] = pick

    def amount(phase, dst, src):
        return units(phase, rep, dst, src)

    def first_of(phase, z, zp, ys):
        return over[over_at(phase, rep, z, zp, ys)]

    def own_code(phase, dst, i):
        hit_at = count_at(0, rep, dst, me)
        hit = rows[hit_at * stride + jnp.minimum(i, cap)]
        code = POOL * SPAN + hit * 2 + phase
        if phase == 0:
            return code
        new_at = count_at(1, rep, dst, me)
        n = cnt[new_at]
        k = i - cnt[hit_at]
        head = (k >= n).astype(jnp.int32)
        new = rows[new_at * stride + jnp.clip(k - head * n, 0, cap)]
        return jnp.where(k >= 0, FRESH * SPAN + new * 2 + head, code)

    def fill(ref, start, n, code_of):
        def put(i, c):
            ref[start + i] = code_of(i)
            return c

        lax.fori_loop(0, n, put, 0)

    other = my_z * NY + 1 - my_y
    for phase in range(2):
        in_first, out_first = phase * plan.long_in, phase * plan.long_out

        def each(zp, c, phase=phase, in_first=in_first, out_first=out_first):
            mine, theirs, new_mine, new_theirs, out_mine, out_theirs = c
            away = (zp != my_z).astype(jnp.int32)
            over_there = zp * NY + 1 - my_y
            along = zp * NY + my_y
            first = first_of(phase, my_z, zp, my_y)
            hits = amount(0, over_there, me)
            n = jnp.maximum(hits - first, 0) * away
            fill(in_out, in_first + mine, n, lambda i: own_code(phase, over_there, first + i))
            their_first = first_of(phase, my_z, zp, 1 - my_y)
            their_hits = amount(0, along, other)
            later = jnp.maximum(their_hits - their_first, 0) * away
            new_n, new_later = 0, 0
            if phase == 1:
                skip = jnp.maximum(first, hits)
                new_n = (amount(1, over_there, me) - skip) * away
                fill(new_out, new_mine, new_n, lambda i: own_code(1, over_there, skip + i))
                new_later = amount(1, along, other) - jnp.maximum(their_first, their_hits)
                new_later = new_later * away
            row = (phase * nz + zp) * WIDE
            own = amount(phase, along, me)
            fill(z_out, row, first * away, lambda i: own_code(phase, over_there, i))
            fill(z_out, row + first, own * away, lambda i: own_code(phase, along, i))
            start = first + own
            if phase == 0:
                start = jnp.maximum(start, EARLY)
            fill(z_out, row + start, later, lambda i: HOP_IN * SPAN + theirs + i)
            if phase == 1:
                fill(
                    z_out,
                    row + jnp.maximum(start + later, SPLIT),
                    new_later,
                    lambda i: HOP_NEW * SPAN + new_theirs + i,
                )
            out_n = first_of(phase, zp, my_z, my_y) * away
            fill(
                out_out, out_first + out_mine, out_n, lambda i: ALONG_Z * SPAN + zp * WIDE + i
            )
            out_base[phase * nz + zp] = out_theirs
            out_later = first_of(phase, zp, my_z, 1 - my_y) * away
            return (
                mine + n,
                theirs + later,
                new_mine + new_n,
                new_theirs + new_later,
                out_mine + out_n,
                out_theirs + out_later,
            )

        _, _, new_mine, new_theirs, _, _ = lax.fori_loop(0, nz, each, (none,) * 6)
        hits = amount(0, other, me)
        fill(same_out, phase * cap, hits, lambda i, p=phase: own_code(p, other, i))
        if phase == 1:
            fill(new_out, new_mine, amount(1, other, me) - hits, lambda i: own_code(1, other, hits + i))
            new_base[0] = new_theirs

    def place(phase, store, i):
        zs = store >> 1
        straight = (store & 1) == my_y
        first = first_of(phase, zs, my_z, my_y)
        held = first + i
        crossing = first_of(phase, zs, my_z, 1 - my_y)
        start = first + amount(phase, me, zs * NY + my_y)
        if phase == 0:
            start = jnp.maximum(start, EARLY)
        slot = start + i - crossing
        if phase == 1:
            hits = amount(0, me, store)
            new_start = jnp.maximum(start + jnp.maximum(hits - crossing, 0), SPLIT)
            slot = jnp.where(i < hits, slot, new_start + i - jnp.maximum(hits, crossing))
        slot = jnp.where(straight, held, slot)
        code = ALONG_Z * SPAN + zs * WIDE + slot
        late = jnp.logical_not(straight) & (i < crossing)
        code = jnp.where(late, HOP_OUT * SPAN + out_base[phase * nz + zs] + i, code)
        near = HOP_SAME * SPAN + phase * cap + i
        if phase == 1:
            near = jnp.where(i < hits, near, HOP_NEW * SPAN + new_base[0] + i - hits)
        code = jnp.where(zs == my_z, near, code)
        return jnp.where(store == me, own_code(phase, me, i), code)

    here = rep * S + me

    for t in range(plan.ses):

        def own_hit(j, c, t=t):
            store = store_of(meta[here * plan.width + t * plan.line + j])
            i = t * plan.hit_len + j
            rank = ranks[here * plan.hits + i]
            for phase in range(2):
                places[phase * plan.hits + i] = place(phase, store, rank)
            return c

        lax.fori_loop(0, plan.hit_len, own_hit, 0)

    def own_new(i, c):
        sender = i >> 1
        rank = i & 1
        n = cnt[count_at(1, rep, me, sender)]
        first = cnt[count_at(0, rep, me, sender)] + rank
        for head in range(2):
            code = place(1, sender, first + head * n)
            arrivals[i * 2 + head] = jnp.where(rank < n, code, -1)
        return c

    lax.fori_loop(0, S * WCAP, own_new, 0)


def make_schedule(plan, meta, me, rep):
    smem = pl.BlockSpec(memory_space=pltpu.SMEM)
    S, nz, reps = plan.stores, plan.nz, plan.reps
    ints = lambda *shape: jax.ShapeDtypeStruct(shape, jnp.int32)
    room = lambda n: pltpu.SMEM((n,), jnp.int32)
    return pl.pallas_call(
        functools.partial(schedule_kernel, plan),
        out_shape=(
            ints(2 * nz * WIDE),
            ints(2 * plan.long_in),
            ints(plan.new_units),
            ints(2 * plan.cap),
            ints(2 * plan.long_out),
            ints(2 * plan.hits),
            ints(S * WCAP * 2),
            ints(1),
        ),
        in_specs=[smem, smem],
        out_specs=(smem,) * 8,
        scratch_shapes=[
            room(reps * 2 * S * S),
            room(reps * 2 * S * S * (plan.cap + 1)),
            room(reps * S * plan.hits),
            room(reps * 2 * nz * nz * NY),
            room(reps * 2 * nz * NY),
            room(1),
            room(2 * nz),
        ],
        name="schedule",
    )(jnp.stack([me, rep]), meta)


def for_source(code, sources, act):
    kind = code >> SPAN_BITS
    slot = code & (SPAN - 1)
    for source, ref in sources.items():
        if source == ALONG_Z:
            z = slot >> WIDE_BITS
            at = slot & (WIDE - 1)
            ends = [first for first, _ in ref[1:]] + [WIDE]
            for (first, part), end in zip(ref, ends):

                @pl.when((code >= 0) & (kind == source) & (at >= first) & (at < end))
                def _():
                    act(part.at[z, at - first])
        else:

            @pl.when((code >= 0) & (kind == source))
            def _():
                act(ref.at[slot])


def pick_kernel(names, firsts, lines, first, table, *refs):
    ins, (out, sem) = refs[: len(names)], refs[len(names) :]
    sources = {}
    for name, start, ref in zip(names, firsts, ins):
        if name == ALONG_Z:
            sources.setdefault(name, []).append((start, ref))
        else:
            sources[name] = ref
    slots = out.shape[1]
    for start in (True, False):
        for line in range(lines):

            def one(i, c):
                code = table[first + line * WIDE + i]
                dst = out.at[line, i]
                if start:
                    for_source(
                        code, sources, lambda src: pltpu.make_async_copy(src, dst, sem).start()
                    )
                else:

                    @pl.when(code >= 0)
                    def _():
                        pltpu.make_async_copy(dst, dst, sem).wait()

                return c

            lax.fori_loop(0, slots, one, 0)


def pick(table, lines, first, slots, sources, unit, dtype):
    smem = pl.BlockSpec(memory_space=pltpu.SMEM)
    far = pl.BlockSpec(memory_space=pl.ANY)
    names = [s[0] for s in sources]
    firsts = [s[1] for s in sources]
    size = lines * slots * math.prod(unit) * 2
    return pl.pallas_call(
        functools.partial(pick_kernel, names, firsts, lines, first),
        out_shape=jax.ShapeDtypeStruct((lines, slots) + unit, dtype),
        in_specs=[smem] + [far] * len(sources),
        out_specs=pl.BlockSpec(memory_space=pltpu.VMEM),
        scratch_shapes=[pltpu.SemaphoreType.DMA],
        compiler_params=pltpu.CompilerParams(vmem_limit_bytes=32 * 1024 * 1024),
        cost_estimate=pl.CostEstimate(flops=0, bytes_accessed=3 * size, transcendentals=0),
        name="pick",
    )(table, *[s[2] for s in sources])


ROWS = 256


def attend_kernel(
    plan, head, sessions, group, names, firsts, places, hit_counts, lengths, arrivals, *refs
):
    last = arrivals is not None
    refs = list(refs)
    queries, fresh_near = refs[:2]
    ins = refs[2 : 2 + len(names)]
    refs = refs[2 + len(names) :]
    if last:
        done, (out, written) = refs[: plan.ses], refs[plan.ses : plan.ses + 2]
        refs = refs[plan.ses + 2 :]
        held, vals, scores, weights, mixed, zero, kv_sem, out_sem = refs
    else:
        mixed, held, vals, scores, weights, kv_sem = refs
    sources = {}
    for name, start, ref in zip(names, firsts, ins):
        if name == ALONG_Z:
            sources.setdefault(name, []).append((start, ref))
        else:
            sources[name] = ref
    tokens, heads, dim = queries.shape
    block = fresh_near.shape[2]
    new_len = tokens // len(sessions)
    new_blocks = new_len // block
    pre = new_blocks * block
    scale = math.log2(math.e) / math.sqrt(dim)

    def fetch(s):
        def one(j, c):
            dst = held.at[s, j]
            for_source(
                places[(head * plan.ses + s) * plan.hit_len + j],
                sources,
                lambda src: pltpu.make_async_copy(src, dst, kv_sem.at[s]).start(),
            )
            return c

        lax.fori_loop(0, hit_counts[s], one, 0)

    def await_fetch(s):
        def one(j, c):
            dst = held.at[s, j]
            pltpu.make_async_copy(dst, dst, kv_sem.at[s]).wait()
            return c

        lax.fori_loop(0, hit_counts[s], one, 0)

    for s in sessions:
        fetch(s)

    if last:
        zero[...] = jnp.zeros(zero.shape, zero.dtype)

        def put_written(start):
            def one(i, c):
                dst = written.at[i >> 2, (i >> 1) & 1, i & 1]
                code = arrivals[i]
                if start:
                    for_source(
                        code,
                        sources,
                        lambda src: pltpu.make_async_copy(src, dst, out_sem.at[0]).start(),
                    )

                    @pl.when(code < 0)
                    def _():
                        pltpu.make_async_copy(zero, dst, out_sem.at[0]).start()
                else:
                    pltpu.make_async_copy(zero, dst, out_sem.at[0]).wait()
                return c

            lax.fori_loop(0, plan.stores * WCAP * 2, one, 0)

        put_written(True)

    vals[:, dim:] = jnp.ones((vals.shape[0], vals.shape[1] - dim), vals.dtype)
    step_tokens = ROWS // group
    assert ROWS % group == 0 and new_len % (2 * step_tokens) == 0 and new_blocks % 2 == 0 and plan.hit_len % 2 == 0

    def session(s, c):
        at_session = s - sessions[0]
        await_fetch(s)
        used = hit_counts[s]
        for b in range(new_blocks):
            vals[pl.ds(b * block, block), :dim] = fresh_near[(s * new_blocks + b) * 2 + head, 1]
        for j in range(plan.hit_len):

            @pl.when(j < used)
            def _():
                vals[pl.ds(pre + j * block, block), :dim] = held[s, j, 1]

            @pl.when(j >= used)
            def _():
                vals[pl.ds(pre + j * block, block), :dim] = jnp.zeros((block, dim), vals.dtype)

        def two_tiles(u, c, pairs, low):
            width = pre + 2 * pairs * block
            lane = lax.broadcasted_iota(jnp.int32, (ROWS, block), 1)

            def begin(part):
                rt = u * 2 + part
                here = pl.ds(at_session * new_len + rt * step_tokens, step_tokens)
                q = queries[here].astype(jnp.float32)[:, head * group : (head + 1) * group, :]
                token = rt * step_tokens + lax.broadcasted_iota(
                    jnp.int32, (step_tokens, group, block), 0
                ).reshape(ROWS, block)
                return here, q.reshape(ROWS, dim).astype(jnp.bfloat16), token

            def score(part, q, token, i, tops):
                if i < new_blocks // 2:
                    keys = [fresh_near[(s * new_blocks + 2 * i + b) * 2 + head, 0] for b in range(2)]
                else:
                    j = 2 * i - new_blocks
                    keys = [held[s, j, 0], held[s, j + 1, 0]]
                both = lax.dot_general(
                    q,
                    jnp.concatenate(keys, axis=0),
                    (((1,), (1,)), ((), ())),
                    preferred_element_type=jnp.float32,
                )
                halves = [both[:, :block], both[:, block:]]
                if i < new_blocks // 2:
                    halves = [
                        jnp.where((2 * i + b) * block + lane <= token, halves[b], -jnp.inf)
                        for b in range(2)
                    ]
                else:
                    for b in range(2):
                        if j + b >= low:
                            halves[b] = jnp.where(j + b < used, halves[b], -jnp.inf)
                for b in range(2):
                    at = (2 * i + b) * block
                    scores[part, :, at : at + block] = halves[b]
                top = jnp.maximum(halves[0], halves[1])
                return top if tops is None else jnp.maximum(tops, top)

            def weigh(part, peak, i):
                for b in range(2):
                    at = (2 * i + b) * block
                    x = scores[part, :, at : at + block] * scale - peak
                    weights[part, :, at : at + block] = jnp.exp2(x).astype(jnp.bfloat16)

            def finish(part, here, token):
                both = jnp.dot(
                    weights[part, :, :width], vals[:width, :], preferred_element_type=jnp.float32
                )
                result = both[:, :dim] / both[:, dim:]
                result = jnp.where(token < lengths[s], result, 0.0)
                mixed[here] = result.reshape(step_tokens, group, dim)

            def peak_of(tops):
                return jnp.max(tops, axis=1, keepdims=True) * scale

            chunks = range(width // (2 * block))
            here0, q0, token0 = begin(0)
            here1, q1, token1 = begin(1)
            tops0, tops1 = None, None
            for i in chunks:
                tops0 = score(0, q0, token0, i, tops0)
            peak0 = peak_of(tops0)
            for i in chunks:
                tops1 = score(1, q1, token1, i, tops1)
                weigh(0, peak0, i)
            peak1 = peak_of(tops1)
            finish(0, here0, token0)
            for i in chunks:
                weigh(1, peak1, i)
            finish(1, here1, token1)
            return c

        low = plan.hit_len // 2
        for pairs in range(plan.hit_len // 4 + 1, plan.hit_len // 2 + 1):

            @pl.when((used >= low) & (used <= 2 * pairs))
            def _():
                lax.fori_loop(
                    0,
                    new_len // (2 * step_tokens),
                    functools.partial(two_tiles, pairs=pairs, low=low),
                    0,
                )

            low = 2 * pairs + 1

        if last:
            span = pl.ds(pl.multiple_of(at_session * new_len, new_len), new_len)
            for k in range(plan.ses):

                @pl.when(s == k)
                def _():
                    whole = jnp.concatenate([done[k][...], mixed[span]], axis=1)
                    out[span] = whole.astype(jnp.bfloat16)

        return c

    lax.fori_loop(sessions[0], sessions[-1] + 1, session, 0)
    if last:
        put_written(False)


def attend(
    plan, head, sessions, queries, fresh, sources, places, counts, lengths, arrivals=None, done=None
):
    smem = pl.BlockSpec(memory_space=pltpu.SMEM)
    near = pl.BlockSpec(memory_space=pltpu.VMEM)
    far = pl.BlockSpec(memory_space=pl.ANY)
    tokens, heads, dim = queries.shape
    group = heads // 2
    unit = fresh.shape[1:]
    block = unit[1]
    new_len = tokens // plan.ses
    rows = plan.hit_len * block + new_len
    last = done is not None
    names = [x[0] for x in sources]
    firsts = [x[1] for x in sources]
    kernel = functools.partial(attend_kernel, plan, head, sessions, group, names, firsts)
    scratch = [
        pltpu.VMEM((plan.ses, plan.hit_len) + unit, jnp.bfloat16),
        pltpu.VMEM((rows, 2 * dim), jnp.bfloat16),
        pltpu.VMEM((2, ROWS, rows), jnp.float32),
        pltpu.VMEM((2, ROWS, rows), jnp.bfloat16),
    ]
    mine = len(sessions) * new_len
    partial_out = jax.ShapeDtypeStruct((mine, group, dim), jnp.float32)
    arrays = [x[2] for x in sources]
    if last:
        call = dict(
            out_shape=(
                jax.ShapeDtypeStruct(queries.shape, jnp.bfloat16),
                jax.ShapeDtypeStruct((plan.stores, WCAP, 2) + unit, jnp.bfloat16),
            ),
            in_specs=[smem] * 4 + [near, near] + [far] * len(sources) + [near] * plan.ses,
            out_specs=(near, far),
            scratch_shapes=scratch
            + [
                pltpu.VMEM(partial_out.shape, jnp.float32),
                pltpu.VMEM(unit, jnp.bfloat16),
                pltpu.SemaphoreType.DMA((plan.ses,)),
                pltpu.SemaphoreType.DMA((1,)),
            ],
        )
        args = [places, counts, lengths, arrivals, queries, fresh] + arrays + list(done)
        body = kernel
    else:
        assert len(sessions) == 1
        part = pl.BlockSpec((new_len, heads, dim), lambda i: (sessions[0], 0, 0))
        call = dict(
            grid=(1,),
            out_shape=partial_out,
            in_specs=[smem] * 3 + [part, near] + [far] * len(sources),
            out_specs=near,
            scratch_shapes=scratch + [pltpu.SemaphoreType.DMA((plan.ses,))],
        )
        args = [places, counts, lengths, queries, fresh] + arrays
        body = lambda p, c, n, *refs: kernel(p, c, n, None, *refs)
    return pl.pallas_call(
        body,
        compiler_params=pltpu.CompilerParams(vmem_limit_bytes=40 * 1024 * 1024),
        cost_estimate=pl.CostEstimate(
            flops=4 * mine * group * rows * dim,
            bytes_accessed=8 * 1024 * 1024,
            transcendentals=mine * group * rows,
        ),
        name="attend",
        **call,
    )(*args)


def project(hidden, kv_weight, local_kv):
    part = jnp.einsum("ta,abhd->hbtd", hidden, kv_weight, preferred_element_type=jnp.float32)
    mine = lax.axis_index("tp")
    tp = lax.axis_size("tp")
    projected = lax.dynamic_slice_in_dim(part, mine * local_kv, local_kv, 0)
    for away in range(1, tp):
        other = lax.dynamic_slice_in_dim(part, ((mine + away) % tp) * local_kv, local_kv, 0)
        projected = projected + lax.ppermute(
            other, "tp", [(i, (i + away) % tp) for i in range(tp)]
        )
    return projected


def new_rows(projected, hit_counts, new_lengths, block_len):
    local_kv, _, tokens, dim = projected.shape
    ses_count = hit_counts.shape[0]
    new_len = tokens // ses_count
    within = jnp.arange(tokens) % new_len
    start_pos = jnp.repeat(hit_counts, new_len, total_repeat_length=tokens)
    live_len = jnp.repeat(new_lengths, new_len, total_repeat_length=tokens)
    positions = (start_pos * block_len + within).astype(jnp.float32)
    rotated = rotate(projected[:, 0], positions)
    fresh = jnp.stack([rotated, projected[:, 1]], axis=1).astype(jnp.bfloat16)
    fresh = jnp.where((within < live_len)[None, None, :, None], fresh, jnp.zeros((), jnp.bfloat16))
    fresh = fresh.reshape(local_kv, 2, tokens // block_len, block_len, dim)
    fresh = jnp.transpose(fresh, (2, 0, 1, 3, 4))
    return fresh.reshape((-1,) + fresh.shape[2:])


def along_z(plan, units):
    columns = [[z * NY + y for z in range(plan.nz)] for y in range(NY)]
    return lax.all_to_all(
        units, "store", split_axis=0, concat_axis=0, axis_index_groups=columns, tiled=True
    )


def over_y(plan, units):
    return lax.ppermute(units[0], "store", [(s, s ^ 1) for s in range(plan.stores)])


def run(plan, size, args):
    hidden, queries, kv_weight, kv_pool, hit_counts, new_lengths, tables = args
    z_out, in_out, new_out, same_out, out_out, places, arrivals = tables
    pool_rows, local_kv, _, block_len, dim = kv_pool.shape
    unit = kv_pool.shape[2:]
    pool = kv_pool.reshape((pool_rows * local_kv,) + unit)
    take = functools.partial(pick, unit=unit, dtype=kv_pool.dtype)
    z_second = plan.nz * WIDE
    (c0, in0, out0), (c1, in1, out1) = size

    early = along_z(plan, take(z_out, plan.nz, 0, EARLY, [(POOL, 0, pool)]))
    hop0 = over_y(plan, take(in_out, 1, 0, in0, [(POOL, 0, pool)]))
    sent1 = take(in_out, 1, plan.long_in, in1, [(POOL, 0, pool)])
    hop1 = over_y(plan, sent1)
    hop0, _ = lax.optimization_barrier((hop0, sent1))
    late = along_z(
        plan, take(z_out, plan.nz, EARLY, c0 - EARLY, [(POOL, 0, pool), (HOP_IN, 0, hop0)])
    )
    projected = project(hidden, kv_weight, local_kv)
    fresh = new_rows(projected, hit_counts, new_lengths, block_len)
    sent_new = take(new_out, 1, 0, plan.new_units, [(FRESH, 0, fresh)])
    hop_new = over_y(plan, sent_new)
    ready1 = [(POOL, 0, pool), (FRESH, 0, fresh), (HOP_IN, 0, hop1)]
    second = along_z(plan, take(z_out, plan.nz, z_second, SPLIT, ready1))
    ready1.append((HOP_NEW, 0, hop_new))
    third = along_z(plan, take(z_out, plan.nz, z_second + SPLIT, c1 - SPLIT, ready1))
    later_pool, _ = lax.optimization_barrier((pool, sent_new))
    same = over_y(plan, take(same_out, 1, 0, 2 * plan.cap, [(POOL, 0, later_pool)]))
    ready1.append((HOP_SAME, 0, same))
    came0 = [(ALONG_Z, 0, early), (ALONG_Z, EARLY, late)]
    back0 = over_y(plan, take(out_out, 1, 0, out0, came0))
    sources0 = [(POOL, 0, pool), (HOP_SAME, 0, same), (HOP_OUT, 0, back0)] + came0
    done = [
        attend(plan, 0, [s], queries, fresh, sources0, places, hit_counts, new_lengths)
        for s in range(plan.ses)
    ]
    *first, third = lax.optimization_barrier((*done[:-1], third))
    done[:-1] = first
    came1 = [(ALONG_Z, 0, second), (ALONG_Z, SPLIT, third)]
    back1 = over_y(plan, take(out_out, 1, plan.long_out, out1, came1))
    ready1 = [source for source in ready1 if source[0] != HOP_IN]
    return attend(
        plan,
        1,
        list(range(plan.ses)),
        queries,
        fresh,
        ready1 + [(HOP_OUT, 0, back1)] + came1,
        places,
        hit_counts,
        new_lengths,
        arrivals,
        done,
    )


def local(hidden, queries, kv_weight, kv_pool, hit_ids, hit_counts, new_lengths, dest_store):
    reps = lax.axis_size("rep")
    store_count = lax.axis_size("store")
    ses_count, hit_len = hit_ids.shape
    pool_rows, local_kv, _, block_len, _ = kv_pool.shape
    per_dev = hidden.shape[0] // block_len
    assert local_kv == 2 and store_count % NY == 0
    plan = Plan(reps, store_count, ses_count, hit_len, per_dev, pool_rows)
    me = lax.axis_index("store").astype(jnp.int32)
    rep = lax.axis_index("rep").astype(jnp.int32)

    mine = jnp.concatenate([hit_ids, hit_counts[:, None], dest_store], axis=1)
    meta = lax.all_to_all(
        jnp.broadcast_to(mine[None], (reps * store_count,) + mine.shape),
        ("rep", "store"),
        split_axis=0,
        concat_axis=0,
    )
    *tables, chosen = make_schedule(plan, meta.reshape(-1), me, rep)
    args = (hidden, queries, kv_weight, kv_pool, hit_counts, new_lengths, tables)
    branches = [functools.partial(run, plan, size) for size in plan.classes]
    attention, written = lax.switch(chosen[0], branches, args)
    return attention, written[None]


def solution(mesh):
    placed = (
        P(("rep", "store"), "tp"),
        P(("rep", "store"), "tp", None),
        P("tp", None, None, None),
        P(("rep", "store"), "tp", None, None, None),
        P(("rep", "store"), None),
        P(("rep", "store")),
        P(("rep", "store")),
        P(("rep", "store"), None),
    )
    return jax.shard_map(
        local,
        mesh=mesh,
        in_specs=placed,
        out_specs=(
            P(("rep", "store"), "tp", None),
            P(("rep", "store"), None, None, "tp", None, None, None),
        ),
        check_vma=False,
    )
```

```python
import functools
import math

import jax
import jax.numpy as jnp
from jax import lax
from jax.experimental import pallas as pl
from jax.experimental.pallas import tpu as pltpu
from jax.sharding import PartitionSpec as P

NY = 2
WCAP = 2
EARLY = 5

theta_base = 500000.0

SPAN_BITS, WIDE_BITS = 16, 5
SPAN = 1 << SPAN_BITS
WIDE = 1 << WIDE_BITS
POOL, FRESH, HOP_IN, HOP_NEW, HOP_SAME, ALONG_Z, HOP_OUT = range(7)


def rotate(keys, positions):
    half = keys.shape[-1] // 2
    steps = jnp.arange(half, dtype=jnp.float32)
    inverse = jnp.exp(steps * (-2.0 * math.log(theta_base) / keys.shape[-1]))
    angles = positions[:, None] * inverse[None, :]
    cosine = jnp.cos(angles)
    sine = jnp.sin(angles)
    first = keys[..., :half]
    second = keys[..., half:]
    return jnp.concatenate(
        [first * cosine - second * sine, second * cosine + first * sine], axis=-1
    )


class Plan:
    def __init__(self, reps, store_count, ses_count, hit_len, per_dev, pool_rows):
        self.reps = reps
        self.stores = store_count
        self.nz = store_count // NY
        self.ses = ses_count
        self.hit_len = hit_len
        self.hits = ses_count * hit_len
        self.per_dev = per_dev
        self.pool_rows = pool_rows
        self.cap = 2 * ((self.hits + store_count - 1) // store_count)
        self.line = hit_len + 1 + per_dev // ses_count
        self.width = ses_count * self.line
        nz, cap = self.nz, self.cap
        both = cap + 2 * WCAP
        self.most = (
            (max(2 * cap, EARLY + cap), (nz - 1) * cap, (nz - 1) * cap),
            (2 * both, (nz - 1) * cap, (nz - 1) * both),
        )
        wanted = (
            ((10, 9, 15), (13, 15, 9)),
            ((11, 10, 15), (14, 17, 10)),
            ((12, 11, 17), (15, 18, 11)),
            ((13, 13, 18), (17, 21, 13)),
            self.most,
        )
        self.long_in = max(m[1] for m in self.most)
        self.only_y = 2 * cap
        self.long_out = max(self.only_y + self.most[0][2], self.most[1][2])
        self.new_units = 2 * per_dev
        assert max(m[0] for m in self.most) <= WIDE
        self.factor = -(-SPAN // pool_rows)
        ids = range(store_count * pool_rows)
        assert all((i * self.factor) >> SPAN_BITS == i // pool_rows for i in ids)
        self.classes = [
            tuple(
                tuple(min(a, b) for a, b in zip(size, most))
                for size, most in zip(sizes, self.most)
            )
            for sizes in wanted
        ]


def schedule_kernel(
    plan, me_ref, meta, z_out, in_out, new_out, out_out, places, arrivals, chosen,
    cnt, rows, ranks, over, hop_out_sum, new_base, out_base
):
    S, nz, cap = plan.stores, plan.nz, plan.cap
    me = me_ref[0]
    rep = me_ref[1]
    my_z = me >> 1
    my_y = me & 1
    stride = cap + 1

    def count_at(kind, group, dst, src):
        return ((group * 2 + kind) * S + dst) * S + src

    def units(phase, group, dst, src):
        n = cnt[count_at(0, group, dst, src)]
        return n if phase == 0 else n + 2 * cnt[count_at(1, group, dst, src)]

    def over_at(phase, group, z, zp, ys):
        return (((group * 2 + phase) * nz + z) * nz + zp) * NY + ys

    def store_of(block):
        return (block * plan.factor) >> SPAN_BITS

    def zero(ref, n, value=0):
        def put(i, c):
            for k in range(8):
                ref[i * 8 + k] = jnp.int32(value)
            return c

        lax.fori_loop(0, n // 8, put, 0)
        for k in range(n - n % 8, n):
            ref[k] = jnp.int32(value)

    zero(cnt, plan.reps * 2 * S * S)
    zero(hop_out_sum, plan.reps * 2 * nz * NY)
    zero(z_out, 2 * nz * WIDE, -1)
    zero(in_out, 2 * plan.long_in, -1)
    zero(new_out, plan.new_units, -1)
    zero(out_out, 2 * plan.long_out, -1)

    def scan(group, d):
        g = group * S + d
        base = g * plan.width
        for t in range(plan.ses):
            line = base + t * plan.line
            used = meta[line + plan.hit_len]
            for j in range(plan.hit_len):
                block = meta[line + j]
                store = store_of(block)
                at = count_at(0, group, d, store)
                rank = cnt[at]
                rows[at * stride + jnp.minimum(rank, cap)] = block - store * plan.pool_rows
                ranks[g * plan.hits + t * plan.hit_len + j] = rank
                cnt[at] = rank + (j < used).astype(jnp.int32)
        for j in range(plan.per_dev):
            t, k = divmod(j, plan.per_dev // plan.ses)
            dest = meta[base + t * plan.line + plan.hit_len + 1 + k]
            at = count_at(1, group, dest, d)
            rank = cnt[at]
            rows[at * stride + jnp.minimum(rank, cap)] = j
            cnt[at] = rank + 1

    def scan_group(group, c):
        def one(d, c):
            scan(group, d)
            return c

        return lax.fori_loop(0, S, one, c)

    lax.fori_loop(0, plan.reps, scan_group, 0)

    none = jnp.int32(0)

    def balance(group, z, c):
        c = list(c)
        for phase in range(2):
            longest, most_in = c[2 * phase], c[2 * phase + 1]
            going = [none, none]
            for zp in range(nz):
                a = [
                    [units(phase, group, zp * NY + yd, z * NY + ys) for yd in range(NY)]
                    for ys in range(NY)
                ]
                half = (a[0][0] + a[0][1] + a[1][0] + a[1][1] + 1) >> 1
                if phase == 0:
                    excess = [a[y][y] + a[y][1 - y] - half for y in range(NY)]
                    first = [
                        a[y][1 - y] - jnp.minimum(jnp.maximum(excess[y], 0), a[y][1 - y])
                        for y in range(NY)
                    ]
                else:
                    excess = [a[y][y] + a[1 - y][y] - half for y in range(NY)]
                    first = [
                        jnp.minimum(jnp.maximum(excess[1 - y], 0), a[y][1 - y]) for y in range(NY)
                    ]
                away = zp != z
                for y in range(NY):
                    over[over_at(phase, group, z, zp, y)] = first[y]
                    later = a[1 - y][y] - first[1 - y]
                    own = a[y][y] + first[y]
                    start = jnp.maximum(own, EARLY) if phase == 0 else own
                    hop = later
                    if phase == 1:
                        hits = units(0, group, zp * NY + y, z * NY + 1 - y)
                        hop = jnp.maximum(hits - first[1 - y], 0)
                    end = jnp.where(hop > 0, start + hop, own)
                    if phase == 1:
                        new_hop = later - hop
                        end = end + new_hop
                    longest = jnp.where(away, jnp.maximum(longest, end), longest)
                    going[1 - y] = going[1 - y] + jnp.where(away, hop, 0)
                    at = ((group * 2 + phase) * nz + zp) * NY + y
                    hop_out_sum[at] = hop_out_sum[at] + jnp.where(away, first[y], 0)
            c[2 * phase] = longest
            c[2 * phase + 1] = jnp.maximum(most_in, jnp.maximum(going[0], going[1]))
        return tuple(c)

    need = lax.fori_loop(
        0,
        plan.reps,
        lambda group, c: lax.fori_loop(0, nz, functools.partial(balance, group), c),
        (none,) * 4,
    )
    out_need = []
    for phase in range(2):

        def top(group, c, phase=phase):
            for i in range(nz * NY):
                c = jnp.maximum(c, hop_out_sum[(group * 2 + phase) * nz * NY + i])
            return c

        out_need.append(lax.fori_loop(0, plan.reps, top, none))
    needs = ((need[0], need[1], out_need[0]), (need[2], need[3], out_need[1]))
    pick = jnp.int32(len(plan.classes) - 1)
    for k in reversed(range(len(plan.classes) - 1)):
        fits = jnp.bool_(True)
        for phase in range(2):
            for n, size in zip(needs[phase], plan.classes[k][phase]):
                fits = fits & (n <= size)
        pick = jnp.where(fits, jnp.int32(k), pick)
    chosen[0] = pick

    def amount(phase, dst, src):
        return units(phase, rep, dst, src)

    def first_of(phase, z, zp, ys):
        return over[over_at(phase, rep, z, zp, ys)]

    def own_code(phase, dst, i):
        hit_at = count_at(0, rep, dst, me)
        hit = rows[hit_at * stride + jnp.minimum(i, cap)]
        code = POOL * SPAN + hit * 2 + phase
        if phase == 0:
            return code
        new_at = count_at(1, rep, dst, me)
        n = cnt[new_at]
        k = i - cnt[hit_at]
        head = (k >= n).astype(jnp.int32)
        new = rows[new_at * stride + jnp.clip(k - head * n, 0, cap)]
        return jnp.where(k >= 0, FRESH * SPAN + new * 2 + head, code)

    def fill(ref, start, n, code_of):
        def put(i, c):
            ref[start + i] = code_of(i)
            return c

        lax.fori_loop(0, n, put, 0)

    other = my_z * NY + 1 - my_y
    for phase in range(2):
        in_first = phase * plan.long_in
        out_first = plan.long_out if phase == 1 else plan.only_y

        def each(zp, c, phase=phase, in_first=in_first, out_first=out_first):
            mine, theirs, new_mine, new_theirs, out_mine, out_theirs = c
            away = (zp != my_z).astype(jnp.int32)
            over_there = zp * NY + 1 - my_y
            along = zp * NY + my_y
            first = first_of(phase, my_z, zp, my_y)
            hits = amount(0, over_there, me)
            n = jnp.maximum(hits - first, 0) * away
            fill(in_out, in_first + mine, n, lambda i: own_code(phase, over_there, first + i))
            their_first = first_of(phase, my_z, zp, 1 - my_y)
            their_hits = amount(0, along, other)
            later = jnp.maximum(their_hits - their_first, 0) * away
            new_n, new_later = 0, 0
            if phase == 1:
                skip = jnp.maximum(first, hits)
                new_n = (amount(1, over_there, me) - skip) * away
                fill(new_out, new_mine, new_n, lambda i: own_code(1, over_there, skip + i))
                new_later = amount(1, along, other) - jnp.maximum(their_first, their_hits)
                new_later = new_later * away
            row = (phase * nz + zp) * WIDE
            own = amount(phase, along, me)
            fill(z_out, row, first * away, lambda i: own_code(phase, over_there, i))
            fill(z_out, row + first, own * away, lambda i: own_code(phase, along, i))
            start = first + own
            if phase == 0:
                start = jnp.maximum(start, EARLY)
            fill(z_out, row + start, later, lambda i: HOP_IN * SPAN + theirs + i)
            if phase == 1:
                fill(
                    z_out,
                    row + start + later,
                    new_later,
                    lambda i: HOP_NEW * SPAN + new_theirs + i,
                )
            out_n = first_of(phase, zp, my_z, my_y) * away
            fill(
                out_out, out_first + out_mine, out_n, lambda i: ALONG_Z * SPAN + zp * WIDE + i
            )
            out_base[phase * nz + zp] = out_theirs
            out_later = first_of(phase, zp, my_z, 1 - my_y) * away
            return (
                mine + n,
                theirs + later,
                new_mine + new_n,
                new_theirs + new_later,
                out_mine + out_n,
                out_theirs + out_later,
            )

        _, _, new_mine, new_theirs, _, _ = lax.fori_loop(0, nz, each, (none,) * 6)
        hits = amount(0, other, me)
        fill(out_out, phase * cap, hits, lambda i, p=phase: own_code(p, other, i))
        if phase == 1:
            fill(new_out, new_mine, amount(1, other, me) - hits, lambda i: own_code(1, other, hits + i))
            new_base[0] = new_theirs

    def place(phase, store, i):
        zs = store >> 1
        straight = (store & 1) == my_y
        first = first_of(phase, zs, my_z, my_y)
        held = first + i
        crossing = first_of(phase, zs, my_z, 1 - my_y)
        start = first + amount(phase, me, zs * NY + my_y)
        if phase == 0:
            start = jnp.maximum(start, EARLY)
        slot = start + i - crossing
        if phase == 1:
            hits = amount(0, me, store)
            new_start = start + jnp.maximum(hits - crossing, 0)
            slot = jnp.where(i < hits, slot, new_start + i - jnp.maximum(hits, crossing))
        slot = jnp.where(straight, held, slot)
        code = ALONG_Z * SPAN + zs * WIDE + slot
        late = jnp.logical_not(straight) & (i < crossing)
        back = HOP_OUT * SPAN + (plan.only_y if phase == 0 else 0) + out_base[phase * nz + zs]
        code = jnp.where(late, back + i, code)
        near = HOP_SAME * SPAN + phase * cap + i
        if phase == 1:
            near = jnp.where(i < hits, near, HOP_NEW * SPAN + new_base[0] + i - hits)
        code = jnp.where(zs == my_z, near, code)
        return jnp.where(store == me, own_code(phase, me, i), code)

    here = rep * S + me

    for t in range(plan.ses):

        def own_hit(j, c, t=t):
            store = store_of(meta[here * plan.width + t * plan.line + j])
            i = t * plan.hit_len + j
            rank = ranks[here * plan.hits + i]
            for phase in range(2):
                places[phase * plan.hits + i] = place(phase, store, rank)
            return c

        lax.fori_loop(0, plan.hit_len, own_hit, 0)

    def own_new(i, c):
        sender = i >> 1
        rank = i & 1
        n = cnt[count_at(1, rep, me, sender)]
        first = cnt[count_at(0, rep, me, sender)] + rank
        for head in range(2):
            code = place(1, sender, first + head * n)
            arrivals[i * 2 + head] = jnp.where(rank < n, code, -1)
        return c

    lax.fori_loop(0, S * WCAP, own_new, 0)


def make_schedule(plan, meta, me, rep):
    smem = pl.BlockSpec(memory_space=pltpu.SMEM)
    S, nz, reps = plan.stores, plan.nz, plan.reps
    ints = lambda *shape: jax.ShapeDtypeStruct(shape, jnp.int32)
    room = lambda n: pltpu.SMEM((n,), jnp.int32)
    return pl.pallas_call(
        functools.partial(schedule_kernel, plan),
        out_shape=(
            ints(2 * nz * WIDE),
            ints(2 * plan.long_in),
            ints(plan.new_units),
            ints(2 * plan.long_out),
            ints(2 * plan.hits),
            ints(S * WCAP * 2),
            ints(1),
        ),
        in_specs=[smem, smem],
        out_specs=(smem,) * 7,
        scratch_shapes=[
            room(reps * 2 * S * S),
            room(reps * 2 * S * S * (plan.cap + 1)),
            room(reps * S * plan.hits),
            room(reps * 2 * nz * nz * NY),
            room(reps * 2 * nz * NY),
            room(1),
            room(2 * nz),
        ],
        name="schedule",
    )(jnp.stack([me, rep]), meta)


def for_source(code, sources, act):
    kind = code >> SPAN_BITS
    slot = code & (SPAN - 1)
    for source, ref in sources.items():
        if source == ALONG_Z:
            z = slot >> WIDE_BITS
            at = slot & (WIDE - 1)
            ends = [first for first, _ in ref[1:]] + [WIDE]
            for (first, part), end in zip(ref, ends):

                @pl.when((code >= 0) & (kind == source) & (at >= first) & (at < end))
                def _():
                    act(part.at[z, at - first])
        else:

            @pl.when((code >= 0) & (kind == source))
            def _():
                act(ref.at[slot])


def pick_kernel(names, firsts, lines, first, table, *refs):
    ins, (out, sem) = refs[: len(names)], refs[len(names) :]
    sources = {}
    for name, start, ref in zip(names, firsts, ins):
        if name == ALONG_Z:
            sources.setdefault(name, []).append((start, ref))
        else:
            sources[name] = ref
    slots = out.shape[1]
    for start in (True, False):
        for line in range(lines):

            def one(i, c):
                code = table[first + line * WIDE + i]
                dst = out.at[line, i]
                if start:
                    for_source(
                        code, sources, lambda src: pltpu.make_async_copy(src, dst, sem).start()
                    )
                else:

                    @pl.when(code >= 0)
                    def _():
                        pltpu.make_async_copy(dst, dst, sem).wait()

                return c

            lax.fori_loop(0, slots, one, 0)


def pick(table, lines, first, slots, sources, unit, dtype):
    smem = pl.BlockSpec(memory_space=pltpu.SMEM)
    far = pl.BlockSpec(memory_space=pl.ANY)
    names = [s[0] for s in sources]
    firsts = [s[1] for s in sources]
    size = lines * slots * math.prod(unit) * 2
    return pl.pallas_call(
        functools.partial(pick_kernel, names, firsts, lines, first),
        out_shape=jax.ShapeDtypeStruct((lines, slots) + unit, dtype),
        in_specs=[smem] + [far] * len(sources),
        out_specs=pl.BlockSpec(memory_space=pltpu.VMEM),
        scratch_shapes=[pltpu.SemaphoreType.DMA],
        compiler_params=pltpu.CompilerParams(vmem_limit_bytes=32 * 1024 * 1024),
        cost_estimate=pl.CostEstimate(flops=0, bytes_accessed=3 * size, transcendentals=0),
        name="pick",
    )(table, *[s[2] for s in sources])


ROWS = 256


def attend_kernel(
    plan, head, sessions, group, names, firsts, places, hit_counts, lengths, arrivals, *refs
):
    last = arrivals is not None
    refs = list(refs)
    queries, fresh_near = refs[:2]
    ins = refs[2 : 2 + len(names)]
    refs = refs[2 + len(names) :]
    if last:
        done, (out, written) = refs[: plan.ses], refs[plan.ses : plan.ses + 2]
        refs = refs[plan.ses + 2 :]
        held, vals, scores, weights, mixed, zero, kv_sem, out_sem = refs
    else:
        mixed, held, vals, scores, weights, kv_sem = refs
    sources = {}
    for name, start, ref in zip(names, firsts, ins):
        if name == ALONG_Z:
            sources.setdefault(name, []).append((start, ref))
        else:
            sources[name] = ref
    tokens, heads, dim = queries.shape
    block = fresh_near.shape[2]
    new_len = tokens // len(sessions)
    new_blocks = new_len // block
    pre = new_blocks * block
    scale = math.log2(math.e) / math.sqrt(dim)

    def fetch(s):
        def one(j, c):
            dst = held.at[s, j]
            for_source(
                places[(head * plan.ses + s) * plan.hit_len + j],
                sources,
                lambda src: pltpu.make_async_copy(src, dst, kv_sem.at[s]).start(),
            )
            return c

        lax.fori_loop(0, hit_counts[s], one, 0)

    def await_fetch(s):
        def one(j, c):
            dst = held.at[s, j]
            pltpu.make_async_copy(dst, dst, kv_sem.at[s]).wait()
            return c

        lax.fori_loop(0, hit_counts[s], one, 0)

    for s in sessions:
        fetch(s)

    if last:
        zero[...] = jnp.zeros(zero.shape, zero.dtype)

        def put_written(start):
            def one(i, c):
                dst = written.at[i >> 2, (i >> 1) & 1, i & 1]
                code = arrivals[i]
                if start:
                    for_source(
                        code,
                        sources,
                        lambda src: pltpu.make_async_copy(src, dst, out_sem.at[0]).start(),
                    )

                    @pl.when(code < 0)
                    def _():
                        pltpu.make_async_copy(zero, dst, out_sem.at[0]).start()
                else:
                    pltpu.make_async_copy(zero, dst, out_sem.at[0]).wait()
                return c

            lax.fori_loop(0, plan.stores * WCAP * 2, one, 0)

        put_written(True)

    vals[:, dim:] = jnp.ones((vals.shape[0], vals.shape[1] - dim), vals.dtype)
    step_tokens = ROWS // group
    assert ROWS % group == 0 and new_len % (2 * step_tokens) == 0 and new_blocks % 2 == 0 and plan.hit_len % 2 == 0

    def session(s, c):
        at_session = s - sessions[0]
        await_fetch(s)
        used = hit_counts[s]
        for b in range(new_blocks):
            vals[pl.ds(b * block, block), :dim] = fresh_near[(s * new_blocks + b) * 2 + head, 1]
        for j in range(plan.hit_len):

            @pl.when(j < used)
            def _():
                vals[pl.ds(pre + j * block, block), :dim] = held[s, j, 1]

            @pl.when(j >= used)
            def _():
                vals[pl.ds(pre + j * block, block), :dim] = jnp.zeros((block, dim), vals.dtype)

        def two_tiles(u, c, pairs, low):
            width = pre + 2 * pairs * block
            lane = lax.broadcasted_iota(jnp.int32, (ROWS, block), 1)

            def begin(part):
                rt = u * 2 + part
                here = pl.ds(at_session * new_len + rt * step_tokens, step_tokens)
                q = queries[here].astype(jnp.float32)[:, head * group : (head + 1) * group, :]
                token = rt * step_tokens + lax.broadcasted_iota(
                    jnp.int32, (step_tokens, group, block), 0
                ).reshape(ROWS, block)
                return here, q.reshape(ROWS, dim).astype(jnp.bfloat16), token

            def score(part, q, token, i, tops):
                if i < new_blocks // 2:
                    keys = [fresh_near[(s * new_blocks + 2 * i + b) * 2 + head, 0] for b in range(2)]
                else:
                    j = 2 * i - new_blocks
                    keys = [held[s, j, 0], held[s, j + 1, 0]]
                both = lax.dot_general(
                    q,
                    jnp.concatenate(keys, axis=0),
                    (((1,), (1,)), ((), ())),
                    preferred_element_type=jnp.float32,
                )
                halves = [both[:, :block], both[:, block:]]
                if i < new_blocks // 2:
                    halves = [
                        jnp.where((2 * i + b) * block + lane <= token, halves[b], -jnp.inf)
                        for b in range(2)
                    ]
                else:
                    for b in range(2):
                        if j + b >= low:
                            halves[b] = jnp.where(j + b < used, halves[b], -jnp.inf)
                for b in range(2):
                    at = (2 * i + b) * block
                    scores[part, :, at : at + block] = halves[b]
                top = jnp.maximum(halves[0], halves[1])
                return top if tops is None else jnp.maximum(tops, top)

            def weigh(part, peak, i):
                for b in range(2):
                    at = (2 * i + b) * block
                    x = scores[part, :, at : at + block] * scale - peak
                    weights[part, :, at : at + block] = jnp.exp2(x).astype(jnp.bfloat16)

            def finish(part, here, token):
                both = jnp.dot(
                    weights[part, :, :width], vals[:width, :], preferred_element_type=jnp.float32
                )
                result = both[:, :dim] / both[:, dim:]
                result = jnp.where(token < lengths[s], result, 0.0)
                mixed[here] = result.reshape(step_tokens, group, dim)

            def peak_of(tops):
                return jnp.max(tops, axis=1, keepdims=True) * scale

            chunks = range(width // (2 * block))
            here0, q0, token0 = begin(0)
            here1, q1, token1 = begin(1)
            tops0, tops1 = None, None
            for i in chunks:
                tops0 = score(0, q0, token0, i, tops0)
            peak0 = peak_of(tops0)
            for i in chunks:
                tops1 = score(1, q1, token1, i, tops1)
                weigh(0, peak0, i)
            peak1 = peak_of(tops1)
            finish(0, here0, token0)
            for i in chunks:
                weigh(1, peak1, i)
            finish(1, here1, token1)
            return c

        low = plan.hit_len // 2
        for pairs in range(plan.hit_len // 4 + 1, plan.hit_len // 2 + 1):

            @pl.when((used >= low) & (used <= 2 * pairs))
            def _():
                lax.fori_loop(
                    0,
                    new_len // (2 * step_tokens),
                    functools.partial(two_tiles, pairs=pairs, low=low),
                    0,
                )

            low = 2 * pairs + 1

        if last:
            span = pl.ds(pl.multiple_of(at_session * new_len, new_len), new_len)
            for k in range(plan.ses):

                @pl.when(s == k)
                def _():
                    whole = jnp.concatenate([done[k][...], mixed[span]], axis=1)
                    out[span] = whole.astype(jnp.bfloat16)

        return c

    lax.fori_loop(sessions[0], sessions[-1] + 1, session, 0)
    if last:
        put_written(False)


def attend(
    plan, head, sessions, queries, fresh, sources, places, counts, lengths, arrivals=None, done=None
):
    smem = pl.BlockSpec(memory_space=pltpu.SMEM)
    near = pl.BlockSpec(memory_space=pltpu.VMEM)
    far = pl.BlockSpec(memory_space=pl.ANY)
    tokens, heads, dim = queries.shape
    group = heads // 2
    unit = fresh.shape[1:]
    block = unit[1]
    new_len = tokens // plan.ses
    rows = plan.hit_len * block + new_len
    last = done is not None
    names = [x[0] for x in sources]
    firsts = [x[1] for x in sources]
    kernel = functools.partial(attend_kernel, plan, head, sessions, group, names, firsts)
    scratch = [
        pltpu.VMEM((plan.ses, plan.hit_len) + unit, jnp.bfloat16),
        pltpu.VMEM((rows, 2 * dim), jnp.bfloat16),
        pltpu.VMEM((2, ROWS, rows), jnp.float32),
        pltpu.VMEM((2, ROWS, rows), jnp.bfloat16),
    ]
    mine = len(sessions) * new_len
    partial_out = jax.ShapeDtypeStruct((mine, group, dim), jnp.float32)
    arrays = [x[2] for x in sources]
    if last:
        call = dict(
            out_shape=(
                jax.ShapeDtypeStruct(queries.shape, jnp.bfloat16),
                jax.ShapeDtypeStruct((plan.stores, WCAP, 2) + unit, jnp.bfloat16),
            ),
            in_specs=[smem] * 4 + [near, near] + [far] * len(sources) + [near] * plan.ses,
            out_specs=(near, far),
            scratch_shapes=scratch
            + [
                pltpu.VMEM(partial_out.shape, jnp.float32),
                pltpu.VMEM(unit, jnp.bfloat16),
                pltpu.SemaphoreType.DMA((plan.ses,)),
                pltpu.SemaphoreType.DMA((1,)),
            ],
        )
        args = [places, counts, lengths, arrivals, queries, fresh] + arrays + list(done)
        body = kernel
    else:
        assert len(sessions) == 1
        part = pl.BlockSpec((new_len, heads, dim), lambda i: (sessions[0], 0, 0))
        call = dict(
            grid=(1,),
            out_shape=partial_out,
            in_specs=[smem] * 3 + [part, near] + [far] * len(sources),
            out_specs=near,
            scratch_shapes=scratch + [pltpu.SemaphoreType.DMA((plan.ses,))],
        )
        args = [places, counts, lengths, queries, fresh] + arrays
        body = lambda p, c, n, *refs: kernel(p, c, n, None, *refs)
    return pl.pallas_call(
        body,
        compiler_params=pltpu.CompilerParams(vmem_limit_bytes=40 * 1024 * 1024),
        cost_estimate=pl.CostEstimate(
            flops=4 * mine * group * rows * dim,
            bytes_accessed=8 * 1024 * 1024,
            transcendentals=mine * group * rows,
        ),
        name="attend",
        **call,
    )(*args)


def project(hidden, kv_weight, local_kv):
    part = jnp.einsum("ta,abhd->hbtd", hidden, kv_weight, preferred_element_type=jnp.float32)
    mine = lax.axis_index("tp")
    tp = lax.axis_size("tp")
    projected = lax.dynamic_slice_in_dim(part, mine * local_kv, local_kv, 0)
    for away in range(1, tp):
        other = lax.dynamic_slice_in_dim(part, ((mine + away) % tp) * local_kv, local_kv, 0)
        projected = projected + lax.ppermute(
            other, "tp", [(i, (i + away) % tp) for i in range(tp)]
        )
    return projected


def new_rows(projected, hit_counts, new_lengths, block_len):
    local_kv, _, tokens, dim = projected.shape
    ses_count = hit_counts.shape[0]
    new_len = tokens // ses_count
    within = jnp.arange(tokens) % new_len
    start_pos = jnp.repeat(hit_counts, new_len, total_repeat_length=tokens)
    live_len = jnp.repeat(new_lengths, new_len, total_repeat_length=tokens)
    positions = (start_pos * block_len + within).astype(jnp.float32)
    rotated = rotate(projected[:, 0], positions)
    fresh = jnp.stack([rotated, projected[:, 1]], axis=1).astype(jnp.bfloat16)
    fresh = jnp.where((within < live_len)[None, None, :, None], fresh, jnp.zeros((), jnp.bfloat16))
    fresh = fresh.reshape(local_kv, 2, tokens // block_len, block_len, dim)
    fresh = jnp.transpose(fresh, (2, 0, 1, 3, 4))
    return fresh.reshape((-1,) + fresh.shape[2:])


def along_z(plan, units):
    columns = [[z * NY + y for z in range(plan.nz)] for y in range(NY)]
    return lax.all_to_all(
        units, "store", split_axis=0, concat_axis=0, axis_index_groups=columns, tiled=True
    )


def over_y(plan, units):
    return lax.ppermute(units[0], "store", [(s, s ^ 1) for s in range(plan.stores)])


def run(plan, size, args):
    hidden, queries, kv_weight, kv_pool, hit_counts, new_lengths, tables = args
    z_out, in_out, new_out, out_out, places, arrivals = tables
    pool_rows, local_kv, _, block_len, dim = kv_pool.shape
    unit = kv_pool.shape[2:]
    pool = kv_pool.reshape((pool_rows * local_kv,) + unit)
    take = functools.partial(pick, unit=unit, dtype=kv_pool.dtype)
    z_second = plan.nz * WIDE
    (c0, in0, out0), (c1, in1, out1) = size

    early = along_z(plan, take(z_out, plan.nz, 0, EARLY, [(POOL, 0, pool)]))
    hop0 = over_y(plan, take(in_out, 1, 0, in0, [(POOL, 0, pool)]))
    sent1 = take(in_out, 1, plan.long_in, in1, [(POOL, 0, pool)])
    hop1 = over_y(plan, sent1)
    hop0, _ = lax.optimization_barrier((hop0, sent1))
    late = along_z(
        plan, take(z_out, plan.nz, EARLY, c0 - EARLY, [(POOL, 0, pool), (HOP_IN, 0, hop0)])
    )
    projected = project(hidden, kv_weight, local_kv)
    fresh = new_rows(projected, hit_counts, new_lengths, block_len)
    hop_new = over_y(plan, take(new_out, 1, 0, plan.new_units, [(FRESH, 0, fresh)]))
    ready1 = [(POOL, 0, pool), (FRESH, 0, fresh), (HOP_IN, 0, hop1), (HOP_NEW, 0, hop_new)]
    second = along_z(plan, take(z_out, plan.nz, z_second, c1, ready1))
    came0 = [(ALONG_Z, 0, early), (ALONG_Z, EARLY, late)]
    sources0 = [(POOL, 0, pool)] + came0
    back0 = over_y(plan, take(out_out, 1, 0, plan.only_y + out0, sources0))
    sources0 += [(HOP_SAME, 0, back0), (HOP_OUT, 0, back0)]
    done = [
        attend(plan, 0, [s], queries, fresh, sources0, places, hit_counts, new_lengths)
        for s in range(plan.ses)
    ]
    *first, second = lax.optimization_barrier((*done[:-1], second))
    done[:-1] = first
    came1 = [(ALONG_Z, 0, second)]
    back1 = over_y(plan, take(out_out, 1, plan.long_out, out1, came1))
    ready1 = [source for source in ready1 if source[0] != HOP_IN]
    return attend(
        plan,
        1,
        list(range(plan.ses)),
        queries,
        fresh,
        ready1 + [(HOP_SAME, 0, back0), (HOP_OUT, 0, back1)] + came1,
        places,
        hit_counts,
        new_lengths,
        arrivals,
        done,
    )


def local(hidden, queries, kv_weight, kv_pool, hit_ids, hit_counts, new_lengths, dest_store):
    reps = lax.axis_size("rep")
    store_count = lax.axis_size("store")
    ses_count, hit_len = hit_ids.shape
    pool_rows, local_kv, _, block_len, _ = kv_pool.shape
    per_dev = hidden.shape[0] // block_len
    assert local_kv == 2 and store_count % NY == 0
    plan = Plan(reps, store_count, ses_count, hit_len, per_dev, pool_rows)
    me = lax.axis_index("store").astype(jnp.int32)
    rep = lax.axis_index("rep").astype(jnp.int32)

    mine = jnp.concatenate([hit_ids, hit_counts[:, None], dest_store], axis=1)
    meta = lax.all_to_all(
        jnp.broadcast_to(mine[None], (reps * store_count,) + mine.shape),
        ("rep", "store"),
        split_axis=0,
        concat_axis=0,
    )
    *tables, chosen = make_schedule(plan, meta.reshape(-1), me, rep)
    args = (hidden, queries, kv_weight, kv_pool, hit_counts, new_lengths, tables)
    branches = [functools.partial(run, plan, size) for size in plan.classes]
    attention, written = lax.switch(chosen[0], branches, args)
    return attention, written[None]


def solution(mesh):
    placed = (
        P(("rep", "store"), "tp"),
        P(("rep", "store"), "tp", None),
        P("tp", None, None, None),
        P(("rep", "store"), "tp", None, None, None),
        P(("rep", "store"), None),
        P(("rep", "store")),
        P(("rep", "store")),
        P(("rep", "store"), None),
    )
    return jax.shard_map(
        local,
        mesh=mesh,
        in_specs=placed,
        out_specs=(
            P(("rep", "store"), "tp", None),
            P(("rep", "store"), None, None, "tp", None, None, None),
        ),
        check_vma=False,
    )
```

```python
import functools
import math

import jax
import jax.numpy as jnp
from jax import lax
from jax.experimental import pallas as pl
from jax.experimental.pallas import tpu as pltpu
from jax.sharding import PartitionSpec as P

NY = 2
WCAP = 2
EARLY = 5

theta_base = 500000.0

SPAN_BITS, WIDE_BITS = 16, 5
SPAN = 1 << SPAN_BITS
WIDE = 1 << WIDE_BITS
POOL, FRESH, HOP_IN, HOP_NEW, HOP_SAME, ALONG_Z, HOP_OUT = range(7)


def rotate(keys, positions):
    half = keys.shape[-1] // 2
    steps = jnp.arange(half, dtype=jnp.float32)
    inverse = jnp.exp(steps * (-2.0 * math.log(theta_base) / keys.shape[-1]))
    angles = positions[:, None] * inverse[None, :]
    cosine = jnp.cos(angles)
    sine = jnp.sin(angles)
    first = keys[..., :half]
    second = keys[..., half:]
    return jnp.concatenate(
        [first * cosine - second * sine, second * cosine + first * sine], axis=-1
    )


class Plan:
    def __init__(self, reps, store_count, ses_count, hit_len, per_dev, pool_rows):
        self.reps = reps
        self.stores = store_count
        self.nz = store_count // NY
        self.ses = ses_count
        self.hit_len = hit_len
        self.hits = ses_count * hit_len
        self.per_dev = per_dev
        self.pool_rows = pool_rows
        self.cap = 2 * ((self.hits + store_count - 1) // store_count)
        self.line = hit_len + 1 + per_dev // ses_count
        self.width = ses_count * self.line
        nz, cap = self.nz, self.cap
        both = cap + 2 * WCAP
        self.most = (
            (max(2 * cap, EARLY + cap), (nz - 1) * cap, (nz - 1) * cap, max(2 * cap, EARLY + cap)),
            (2 * both, (nz - 1) * cap, (nz - 1) * both, 2 * both),
        )
        wanted = (
            ((11, 10, 15, 10), (14, 17, 10, 12)),
            ((12, 11, 17, 11), (15, 18, 11, 13)),
            ((13, 13, 18, 12), (17, 21, 13, 15)),
            self.most,
        )
        self.long_in = max(m[1] for m in self.most)
        self.only_y = 2 * cap
        self.long_out = max(self.only_y + self.most[0][2], self.most[1][2])
        self.new_units = 2 * per_dev
        assert max(m[0] for m in self.most) <= WIDE
        self.factor = -(-SPAN // pool_rows)
        ids = range(store_count * pool_rows)
        assert all((i * self.factor) >> SPAN_BITS == i // pool_rows for i in ids)
        self.classes = [
            tuple(
                tuple(min(a, b) for a, b in zip(size, most))
                for size, most in zip(sizes, self.most)
            )
            for sizes in wanted
        ]


def schedule_kernel(
    plan, me_ref, meta, z_out, in_out, new_out, out_out, places, arrivals, chosen,
    cnt, rows, ranks, over, hop_out_sum, new_base, out_base
):
    S, nz, cap = plan.stores, plan.nz, plan.cap
    me = me_ref[0]
    rep = me_ref[1]
    my_z = me >> 1
    my_y = me & 1
    stride = cap + 1

    def count_at(kind, group, dst, src):
        return ((group * 2 + kind) * S + dst) * S + src

    def units(phase, group, dst, src):
        n = cnt[count_at(0, group, dst, src)]
        return n if phase == 0 else n + 2 * cnt[count_at(1, group, dst, src)]

    def over_at(phase, group, z, zp, ys):
        return (((group * 2 + phase) * nz + z) * nz + zp) * NY + ys

    def store_of(block):
        return (block * plan.factor) >> SPAN_BITS

    def zero(ref, n, value=0):
        def put(i, c):
            for k in range(8):
                ref[i * 8 + k] = jnp.int32(value)
            return c

        lax.fori_loop(0, n // 8, put, 0)
        for k in range(n - n % 8, n):
            ref[k] = jnp.int32(value)

    zero(cnt, plan.reps * 2 * S * S)
    zero(hop_out_sum, plan.reps * 2 * nz * NY)
    zero(z_out, 2 * nz * WIDE, -1)
    zero(in_out, 2 * plan.long_in, -1)
    zero(new_out, plan.new_units, -1)
    zero(out_out, 2 * plan.long_out, -1)

    def scan(group, d):
        g = group * S + d
        base = g * plan.width
        for t in range(plan.ses):
            line = base + t * plan.line
            used = meta[line + plan.hit_len]
            for j in range(plan.hit_len):
                block = meta[line + j]
                store = store_of(block)
                at = count_at(0, group, d, store)
                rank = cnt[at]
                rows[at * stride + jnp.minimum(rank, cap)] = block - store * plan.pool_rows
                ranks[g * plan.hits + t * plan.hit_len + j] = rank
                cnt[at] = rank + (j < used).astype(jnp.int32)
        for j in range(plan.per_dev):
            t, k = divmod(j, plan.per_dev // plan.ses)
            dest = meta[base + t * plan.line + plan.hit_len + 1 + k]
            at = count_at(1, group, dest, d)
            rank = cnt[at]
            rows[at * stride + jnp.minimum(rank, cap)] = j
            cnt[at] = rank + 1

    def scan_group(group, c):
        def one(d, c):
            scan(group, d)
            return c

        return lax.fori_loop(0, S, one, c)

    lax.fori_loop(0, plan.reps, scan_group, 0)

    none = jnp.int32(0)

    def balance(group, z, c):
        c = list(c)
        for phase in range(2):
            longest, most_in, longest_far = c[3 * phase : 3 * phase + 3]
            going = [none, none]
            for zp in range(nz):
                a = [
                    [units(phase, group, zp * NY + yd, z * NY + ys) for yd in range(NY)]
                    for ys in range(NY)
                ]
                half = (a[0][0] + a[0][1] + a[1][0] + a[1][1] + 1) >> 1
                if phase == 0:
                    excess = [a[y][y] + a[y][1 - y] - half for y in range(NY)]
                    first = [
                        a[y][1 - y] - jnp.minimum(jnp.maximum(excess[y], 0), a[y][1 - y])
                        for y in range(NY)
                    ]
                else:
                    excess = [a[y][y] + a[1 - y][y] - half for y in range(NY)]
                    first = [
                        jnp.minimum(jnp.maximum(excess[1 - y], 0), a[y][1 - y]) for y in range(NY)
                    ]
                away = zp != z
                far = jnp.abs(zp - z) == nz - 1
                for y in range(NY):
                    over[over_at(phase, group, z, zp, y)] = first[y]
                    later = a[1 - y][y] - first[1 - y]
                    own = a[y][y] + first[y]
                    start = jnp.maximum(own, EARLY) if phase == 0 else own
                    hop = later
                    if phase == 1:
                        hits = units(0, group, zp * NY + y, z * NY + 1 - y)
                        hop = jnp.maximum(hits - first[1 - y], 0)
                    end = jnp.where(hop > 0, start + hop, own)
                    if phase == 1:
                        new_hop = later - hop
                        end = end + new_hop
                    longest = jnp.where(
                        away & jnp.logical_not(far), jnp.maximum(longest, end), longest
                    )
                    longest_far = jnp.where(far, jnp.maximum(longest_far, end), longest_far)
                    going[1 - y] = going[1 - y] + jnp.where(away, hop, 0)
                    at = ((group * 2 + phase) * nz + zp) * NY + y
                    hop_out_sum[at] = hop_out_sum[at] + jnp.where(away, first[y], 0)
            c[3 * phase] = longest
            c[3 * phase + 1] = jnp.maximum(most_in, jnp.maximum(going[0], going[1]))
            c[3 * phase + 2] = longest_far
        return tuple(c)

    need = lax.fori_loop(
        0,
        plan.reps,
        lambda group, c: lax.fori_loop(0, nz, functools.partial(balance, group), c),
        (none,) * 6,
    )
    out_need = []
    for phase in range(2):

        def top(group, c, phase=phase):
            for i in range(nz * NY):
                c = jnp.maximum(c, hop_out_sum[(group * 2 + phase) * nz * NY + i])
            return c

        out_need.append(lax.fori_loop(0, plan.reps, top, none))
    needs = [(*need[3 * p : 3 * p + 2], out_need[p], need[3 * p + 2]) for p in range(2)]
    pick = jnp.int32(len(plan.classes) - 1)
    for k in reversed(range(len(plan.classes) - 1)):
        fits = jnp.bool_(True)
        for phase in range(2):
            for n, size in zip(needs[phase], plan.classes[k][phase]):
                fits = fits & (n <= size)
        pick = jnp.where(fits, jnp.int32(k), pick)
    chosen[0] = pick

    def way(z):
        return z - my_z + nz - 1

    def amount(phase, dst, src):
        return units(phase, rep, dst, src)

    def first_of(phase, z, zp, ys):
        return over[over_at(phase, rep, z, zp, ys)]

    def own_code(phase, dst, i):
        hit_at = count_at(0, rep, dst, me)
        hit = rows[hit_at * stride + jnp.minimum(i, cap)]
        code = POOL * SPAN + hit * 2 + phase
        if phase == 0:
            return code
        new_at = count_at(1, rep, dst, me)
        n = cnt[new_at]
        k = i - cnt[hit_at]
        head = (k >= n).astype(jnp.int32)
        new = rows[new_at * stride + jnp.clip(k - head * n, 0, cap)]
        return jnp.where(k >= 0, FRESH * SPAN + new * 2 + head, code)

    def fill(ref, start, n, code_of):
        def put(i, c):
            ref[start + i] = code_of(i)
            return c

        lax.fori_loop(0, n, put, 0)

    other = my_z * NY + 1 - my_y
    for phase in range(2):
        in_first = phase * plan.long_in
        out_first = plan.long_out if phase == 1 else plan.only_y

        def each(zp, c, phase=phase, in_first=in_first, out_first=out_first):
            mine, theirs, new_mine, new_theirs, out_mine, out_theirs = c
            away = (zp != my_z).astype(jnp.int32)
            over_there = zp * NY + 1 - my_y
            along = zp * NY + my_y
            first = first_of(phase, my_z, zp, my_y)
            hits = amount(0, over_there, me)
            n = jnp.maximum(hits - first, 0) * away
            fill(in_out, in_first + mine, n, lambda i: own_code(phase, over_there, first + i))
            their_first = first_of(phase, my_z, zp, 1 - my_y)
            their_hits = amount(0, along, other)
            later = jnp.maximum(their_hits - their_first, 0) * away
            new_n, new_later = 0, 0
            if phase == 1:
                skip = jnp.maximum(first, hits)
                new_n = (amount(1, over_there, me) - skip) * away
                fill(new_out, new_mine, new_n, lambda i: own_code(1, over_there, skip + i))
                new_later = amount(1, along, other) - jnp.maximum(their_first, their_hits)
                new_later = new_later * away
            row = (phase * nz + zp) * WIDE
            own = amount(phase, along, me)
            fill(z_out, row, first * away, lambda i: own_code(phase, over_there, i))
            fill(z_out, row + first, own * away, lambda i: own_code(phase, along, i))
            start = first + own
            if phase == 0:
                start = jnp.maximum(start, EARLY)
            fill(z_out, row + start, later, lambda i: HOP_IN * SPAN + theirs + i)
            if phase == 1:
                fill(
                    z_out,
                    row + start + later,
                    new_later,
                    lambda i: HOP_NEW * SPAN + new_theirs + i,
                )
            out_n = first_of(phase, zp, my_z, my_y) * away
            fill(
                out_out, out_first + out_mine, out_n, lambda i: ALONG_Z * SPAN + way(zp) * WIDE + i
            )
            out_base[phase * nz + zp] = out_theirs
            out_later = first_of(phase, zp, my_z, 1 - my_y) * away
            return (
                mine + n,
                theirs + later,
                new_mine + new_n,
                new_theirs + new_later,
                out_mine + out_n,
                out_theirs + out_later,
            )

        _, _, new_mine, new_theirs, _, _ = lax.fori_loop(0, nz, each, (none,) * 6)
        hits = amount(0, other, me)
        fill(out_out, phase * cap, hits, lambda i, p=phase: own_code(p, other, i))
        if phase == 1:
            fill(new_out, new_mine, amount(1, other, me) - hits, lambda i: own_code(1, other, hits + i))
            new_base[0] = new_theirs

    def place(phase, store, i):
        zs = store >> 1
        straight = (store & 1) == my_y
        first = first_of(phase, zs, my_z, my_y)
        held = first + i
        crossing = first_of(phase, zs, my_z, 1 - my_y)
        start = first + amount(phase, me, zs * NY + my_y)
        if phase == 0:
            start = jnp.maximum(start, EARLY)
        slot = start + i - crossing
        if phase == 1:
            hits = amount(0, me, store)
            new_start = start + jnp.maximum(hits - crossing, 0)
            slot = jnp.where(i < hits, slot, new_start + i - jnp.maximum(hits, crossing))
        slot = jnp.where(straight, held, slot)
        code = ALONG_Z * SPAN + way(zs) * WIDE + slot
        late = jnp.logical_not(straight) & (i < crossing)
        back = HOP_OUT * SPAN + (plan.only_y if phase == 0 else 0) + out_base[phase * nz + zs]
        code = jnp.where(late, back + i, code)
        near = HOP_SAME * SPAN + phase * cap + i
        if phase == 1:
            near = jnp.where(i < hits, near, HOP_NEW * SPAN + new_base[0] + i - hits)
        code = jnp.where(zs == my_z, near, code)
        return jnp.where(store == me, own_code(phase, me, i), code)

    here = rep * S + me

    for t in range(plan.ses):

        def own_hit(j, c, t=t):
            store = store_of(meta[here * plan.width + t * plan.line + j])
            i = t * plan.hit_len + j
            rank = ranks[here * plan.hits + i]
            for phase in range(2):
                places[phase * plan.hits + i] = place(phase, store, rank)
            return c

        lax.fori_loop(0, plan.hit_len, own_hit, 0)

    def own_new(i, c):
        sender = i >> 1
        rank = i & 1
        n = cnt[count_at(1, rep, me, sender)]
        first = cnt[count_at(0, rep, me, sender)] + rank
        for head in range(2):
            code = place(1, sender, first + head * n)
            arrivals[i * 2 + head] = jnp.where(rank < n, code, -1)
        return c

    lax.fori_loop(0, S * WCAP, own_new, 0)


def make_schedule(plan, meta, me, rep):
    smem = pl.BlockSpec(memory_space=pltpu.SMEM)
    S, nz, reps = plan.stores, plan.nz, plan.reps
    ints = lambda *shape: jax.ShapeDtypeStruct(shape, jnp.int32)
    room = lambda n: pltpu.SMEM((n,), jnp.int32)
    return pl.pallas_call(
        functools.partial(schedule_kernel, plan),
        out_shape=(
            ints(2 * nz * WIDE),
            ints(2 * plan.long_in),
            ints(plan.new_units),
            ints(2 * plan.long_out),
            ints(2 * plan.hits),
            ints(S * WCAP * 2),
            ints(1),
        ),
        in_specs=[smem, smem],
        out_specs=(smem,) * 7,
        scratch_shapes=[
            room(reps * 2 * S * S),
            room(reps * 2 * S * S * (plan.cap + 1)),
            room(reps * S * plan.hits),
            room(reps * 2 * nz * nz * NY),
            room(reps * 2 * nz * NY),
            room(1),
            room(2 * nz),
        ],
        name="schedule",
    )(jnp.stack([me, rep]), meta)


def group_sources(keys, refs):
    sources = {}
    for key, ref in zip(keys, refs):
        if isinstance(key, tuple):
            sources.setdefault(key[0], []).append((*key[1:], ref))
        else:
            sources[key] = ref
    return sources


def for_source(code, sources, act):
    kind = code >> SPAN_BITS
    slot = code & (SPAN - 1)
    for source, ref in sources.items():

        @pl.when((code >= 0) & (kind == source))
        def _():
            if source != ALONG_Z:
                act(ref.at[slot])
                return
            way = slot >> WIDE_BITS
            at = slot & (WIDE - 1)
            for this_way, first, slots, part in ref:

                @pl.when((way == this_way) & (at >= first) & (at < first + slots))
                def _():
                    act(part.at[at - first])


def pick_kernel(nz, keys, shifts, first, me, table, *refs):
    sources = group_sources(keys, refs)
    outs, sem = refs[len(keys) : -1], refs[-1]
    my_z = me[0] >> 1
    for start in (True, False):
        for out, shift in zip(outs, shifts):
            line = 0 if shift is None else my_z + shift

            def one(i, c):
                code = table[first + line * WIDE + i]
                dst = out.at[i]
                if start:
                    for_source(
                        code, sources, lambda src: pltpu.make_async_copy(src, dst, sem).start()
                    )
                else:

                    @pl.when(code >= 0)
                    def _():
                        pltpu.make_async_copy(dst, dst, sem).wait()

                return c

            if shift is None:
                lax.fori_loop(0, out.shape[0], one, 0)
            else:

                @pl.when((line >= 0) & (line < nz))
                def _():
                    lax.fori_loop(0, out.shape[0], one, 0)


def pick(plan, me, table, first, slots, sources):
    smem = pl.BlockSpec(memory_space=pltpu.SMEM)
    far = pl.BlockSpec(memory_space=pl.ANY)
    keys = [key for key, _ in sources]
    arrays = [array for _, array in sources]
    unit, dtype = arrays[0].shape[1:], arrays[0].dtype
    size = sum(slots.values()) * math.prod(unit) * 2
    return pl.pallas_call(
        functools.partial(pick_kernel, plan.nz, keys, list(slots), first),
        out_shape=tuple(jax.ShapeDtypeStruct((n,) + unit, dtype) for n in slots.values()),
        in_specs=[smem, smem] + [far] * len(sources),
        out_specs=(pl.BlockSpec(memory_space=pltpu.VMEM),) * len(slots),
        scratch_shapes=[pltpu.SemaphoreType.DMA],
        compiler_params=pltpu.CompilerParams(vmem_limit_bytes=32 * 1024 * 1024),
        cost_estimate=pl.CostEstimate(flops=0, bytes_accessed=3 * size, transcendentals=0),
        name="pick",
    )(me, table, *arrays)


ROWS = 256


def attend_kernel(
    plan, head, sessions, group, names, places, hit_counts, lengths, arrivals, *refs
):
    last = arrivals is not None
    refs = list(refs)
    queries, fresh_near = refs[:2]
    ins = refs[2 : 2 + len(names)]
    refs = refs[2 + len(names) :]
    if last:
        done, (out, written) = refs[: plan.ses], refs[plan.ses : plan.ses + 2]
        refs = refs[plan.ses + 2 :]
        held, vals, scores, weights, mixed, zero, kv_sem, out_sem = refs
    else:
        mixed, held, vals, scores, weights, kv_sem = refs
    sources = group_sources(names, ins)
    tokens, heads, dim = queries.shape
    block = fresh_near.shape[2]
    new_len = tokens // len(sessions)
    new_blocks = new_len // block
    pre = new_blocks * block
    scale = math.log2(math.e) / math.sqrt(dim)

    def fetch(s):
        def one(j, c):
            dst = held.at[s, j]
            for_source(
                places[(head * plan.ses + s) * plan.hit_len + j],
                sources,
                lambda src: pltpu.make_async_copy(src, dst, kv_sem.at[s]).start(),
            )
            return c

        lax.fori_loop(0, hit_counts[s], one, 0)

    def await_fetch(s):
        def one(j, c):
            dst = held.at[s, j]
            pltpu.make_async_copy(dst, dst, kv_sem.at[s]).wait()
            return c

        lax.fori_loop(0, hit_counts[s], one, 0)

    for s in sessions:
        fetch(s)

    if last:
        zero[...] = jnp.zeros(zero.shape, zero.dtype)

        def put_written(start):
            def one(i, c):
                dst = written.at[i >> 2, (i >> 1) & 1, i & 1]
                code = arrivals[i]
                if start:
                    for_source(
                        code,
                        sources,
                        lambda src: pltpu.make_async_copy(src, dst, out_sem.at[0]).start(),
                    )

                    @pl.when(code < 0)
                    def _():
                        pltpu.make_async_copy(zero, dst, out_sem.at[0]).start()
                else:
                    pltpu.make_async_copy(zero, dst, out_sem.at[0]).wait()
                return c

            lax.fori_loop(0, plan.stores * WCAP * 2, one, 0)

        put_written(True)

    vals[:, dim:] = jnp.ones((vals.shape[0], vals.shape[1] - dim), vals.dtype)
    step_tokens = ROWS // group
    assert ROWS % group == 0 and new_len % (2 * step_tokens) == 0 and new_blocks % 2 == 0 and plan.hit_len % 2 == 0

    def session(s, c):
        at_session = s - sessions[0]
        await_fetch(s)
        used = hit_counts[s]
        for b in range(new_blocks):
            vals[pl.ds(b * block, block), :dim] = fresh_near[(s * new_blocks + b) * 2 + head, 1]
        for j in range(plan.hit_len):

            @pl.when(j < used)
            def _():
                vals[pl.ds(pre + j * block, block), :dim] = held[s, j, 1]

            @pl.when(j >= used)
            def _():
                vals[pl.ds(pre + j * block, block), :dim] = jnp.zeros((block, dim), vals.dtype)

        def two_tiles(u, c, pairs, low):
            width = pre + 2 * pairs * block
            lane = lax.broadcasted_iota(jnp.int32, (ROWS, block), 1)

            def begin(part):
                rt = u * 2 + part
                here = pl.ds(at_session * new_len + rt * step_tokens, step_tokens)
                q = queries[here].astype(jnp.float32)[:, head * group : (head + 1) * group, :]
                token = rt * step_tokens + lax.broadcasted_iota(
                    jnp.int32, (step_tokens, group, block), 0
                ).reshape(ROWS, block)
                return here, q.reshape(ROWS, dim).astype(jnp.bfloat16), token

            def score(part, q, token, i, tops):
                if i < new_blocks // 2:
                    keys = [fresh_near[(s * new_blocks + 2 * i + b) * 2 + head, 0] for b in range(2)]
                else:
                    j = 2 * i - new_blocks
                    keys = [held[s, j, 0], held[s, j + 1, 0]]
                both = lax.dot_general(
                    q,
                    jnp.concatenate(keys, axis=0),
                    (((1,), (1,)), ((), ())),
                    preferred_element_type=jnp.float32,
                )
                halves = [both[:, :block], both[:, block:]]
                if i < new_blocks // 2:
                    halves = [
                        jnp.where((2 * i + b) * block + lane <= token, halves[b], -jnp.inf)
                        for b in range(2)
                    ]
                else:
                    for b in range(2):
                        if j + b >= low:
                            halves[b] = jnp.where(j + b < used, halves[b], -jnp.inf)
                for b in range(2):
                    at = (2 * i + b) * block
                    scores[part, :, at : at + block] = halves[b]
                top = jnp.maximum(halves[0], halves[1])
                return top if tops is None else jnp.maximum(tops, top)

            def weigh(part, peak, i):
                for b in range(2):
                    at = (2 * i + b) * block
                    x = scores[part, :, at : at + block] * scale - peak
                    weights[part, :, at : at + block] = jnp.exp2(x).astype(jnp.bfloat16)

            def finish(part, here, token):
                both = jnp.dot(
                    weights[part, :, :width], vals[:width, :], preferred_element_type=jnp.float32
                )
                result = both[:, :dim] / both[:, dim:]
                result = jnp.where(token < lengths[s], result, 0.0)
                mixed[here] = result.reshape(step_tokens, group, dim)

            def peak_of(tops):
                return jnp.max(tops, axis=1, keepdims=True) * scale

            chunks = range(width // (2 * block))
            here0, q0, token0 = begin(0)
            here1, q1, token1 = begin(1)
            tops0, tops1 = None, None
            for i in chunks:
                tops0 = score(0, q0, token0, i, tops0)
            peak0 = peak_of(tops0)
            for i in chunks:
                tops1 = score(1, q1, token1, i, tops1)
                weigh(0, peak0, i)
            peak1 = peak_of(tops1)
            finish(0, here0, token0)
            for i in chunks:
                weigh(1, peak1, i)
            finish(1, here1, token1)
            return c

        low = plan.hit_len // 2
        for pairs in range(plan.hit_len // 4 + 1, plan.hit_len // 2 + 1):

            @pl.when((used >= low) & (used <= 2 * pairs))
            def _():
                lax.fori_loop(
                    0,
                    new_len // (2 * step_tokens),
                    functools.partial(two_tiles, pairs=pairs, low=low),
                    0,
                )

            low = 2 * pairs + 1

        if last:
            span = pl.ds(pl.multiple_of(at_session * new_len, new_len), new_len)
            for k in range(plan.ses):

                @pl.when(s == k)
                def _():
                    whole = jnp.concatenate([done[k][...], mixed[span]], axis=1)
                    out[span] = whole.astype(jnp.bfloat16)

        return c

    lax.fori_loop(sessions[0], sessions[-1] + 1, session, 0)
    if last:
        put_written(False)


def attend(
    plan, head, sessions, queries, fresh, sources, places, counts, lengths, arrivals=None, done=None
):
    smem = pl.BlockSpec(memory_space=pltpu.SMEM)
    near = pl.BlockSpec(memory_space=pltpu.VMEM)
    far = pl.BlockSpec(memory_space=pl.ANY)
    tokens, heads, dim = queries.shape
    group = heads // 2
    unit = fresh.shape[1:]
    block = unit[1]
    new_len = tokens // plan.ses
    rows = plan.hit_len * block + new_len
    last = done is not None
    names = [x[0] for x in sources]
    kernel = functools.partial(attend_kernel, plan, head, sessions, group, names)
    scratch = [
        pltpu.VMEM((plan.ses, plan.hit_len) + unit, jnp.bfloat16),
        pltpu.VMEM((rows, 2 * dim), jnp.bfloat16),
        pltpu.VMEM((2, ROWS, rows), jnp.float32),
        pltpu.VMEM((2, ROWS, rows), jnp.bfloat16),
    ]
    mine = len(sessions) * new_len
    partial_out = jax.ShapeDtypeStruct((mine, group, dim), jnp.float32)
    arrays = [x[1] for x in sources]
    if last:
        call = dict(
            out_shape=(
                jax.ShapeDtypeStruct(queries.shape, jnp.bfloat16),
                jax.ShapeDtypeStruct((plan.stores, WCAP, 2) + unit, jnp.bfloat16),
            ),
            in_specs=[smem] * 4 + [near, near] + [far] * len(sources) + [near] * plan.ses,
            out_specs=(near, far),
            scratch_shapes=scratch
            + [
                pltpu.VMEM(partial_out.shape, jnp.float32),
                pltpu.VMEM(unit, jnp.bfloat16),
                pltpu.SemaphoreType.DMA((plan.ses,)),
                pltpu.SemaphoreType.DMA((1,)),
            ],
        )
        args = [places, counts, lengths, arrivals, queries, fresh] + arrays + list(done)
        body = kernel
    else:
        assert len(sessions) == 1
        part = pl.BlockSpec((new_len, heads, dim), lambda i: (sessions[0], 0, 0))
        call = dict(
            grid=(1,),
            out_shape=partial_out,
            in_specs=[smem] * 3 + [part, near] + [far] * len(sources),
            out_specs=near,
            scratch_shapes=scratch + [pltpu.SemaphoreType.DMA((plan.ses,))],
        )
        args = [places, counts, lengths, queries, fresh] + arrays
        body = lambda p, c, n, *refs: kernel(p, c, n, None, *refs)
    return pl.pallas_call(
        body,
        compiler_params=pltpu.CompilerParams(vmem_limit_bytes=40 * 1024 * 1024),
        cost_estimate=pl.CostEstimate(
            flops=4 * mine * group * rows * dim,
            bytes_accessed=8 * 1024 * 1024,
            transcendentals=mine * group * rows,
        ),
        name="attend",
        **call,
    )(*args)


def project(hidden, kv_weight, local_kv):
    part = jnp.einsum("ta,abhd->hbtd", hidden, kv_weight, preferred_element_type=jnp.float32)
    mine = lax.axis_index("tp")
    tp = lax.axis_size("tp")
    projected = lax.dynamic_slice_in_dim(part, mine * local_kv, local_kv, 0)
    for away in range(1, tp):
        other = lax.dynamic_slice_in_dim(part, ((mine + away) % tp) * local_kv, local_kv, 0)
        projected = projected + lax.ppermute(
            other, "tp", [(i, (i + away) % tp) for i in range(tp)]
        )
    return projected


def new_rows(projected, hit_counts, new_lengths, block_len):
    local_kv, _, tokens, dim = projected.shape
    ses_count = hit_counts.shape[0]
    new_len = tokens // ses_count
    within = jnp.arange(tokens) % new_len
    start_pos = jnp.repeat(hit_counts, new_len, total_repeat_length=tokens)
    live_len = jnp.repeat(new_lengths, new_len, total_repeat_length=tokens)
    positions = (start_pos * block_len + within).astype(jnp.float32)
    rotated = rotate(projected[:, 0], positions)
    fresh = jnp.stack([rotated, projected[:, 1]], axis=1).astype(jnp.bfloat16)
    fresh = jnp.where((within < live_len)[None, None, :, None], fresh, jnp.zeros((), jnp.bfloat16))
    fresh = fresh.reshape(local_kv, 2, tokens // block_len, block_len, dim)
    fresh = jnp.transpose(fresh, (2, 0, 1, 3, 4))
    return fresh.reshape((-1,) + fresh.shape[2:])


def along_z(plan, first, units):
    came = []
    for shift, part in units.items():
        pairs = [(s, s + NY * shift) for s in range(plan.stores)]
        pairs = [(a, b) for a, b in pairs if 0 <= b < plan.stores]
        key = (ALONG_Z, plan.nz - 1 - shift, first, part.shape[0])
        came.append((key, lax.ppermute(part, "store", pairs)))
    return came


def over_y(plan, units):
    return lax.ppermute(units, "store", [(s, s ^ 1) for s in range(plan.stores)])


def run(plan, size, args):
    hidden, queries, kv_weight, kv_pool, hit_counts, new_lengths, me, tables = args
    z_out, in_out, new_out, out_out, places, arrivals = tables
    pool_rows, local_kv, _, block_len, dim = kv_pool.shape
    pool = kv_pool.reshape((pool_rows * local_kv,) + kv_pool.shape[2:])
    z_second = plan.nz * WIDE
    (c0, in0, out0, far0), (c1, in1, out1, far1) = size
    shifts = [sign * d for d in range(plan.nz - 1, 0, -1) for sign in (1, -1)]

    def line(table, first, n, sources):
        return pick(plan, me, table, first, {None: n}, sources)[0]

    def lines(first, at, near, far, sources):
        slots = {k: far if abs(k) == plan.nz - 1 else near for k in shifts}
        parts = pick(plan, me, z_out, first, slots, sources)
        return along_z(plan, at, dict(zip(shifts, parts)))

    early = lines(0, 0, EARLY, EARLY, [(POOL, pool)])
    hop0 = over_y(plan, line(in_out, 0, in0, [(POOL, pool)]))
    sent1 = line(in_out, plan.long_in, in1, [(POOL, pool)])
    hop1 = over_y(plan, sent1)
    hop0, _ = lax.optimization_barrier((hop0, sent1))
    late = lines(EARLY, EARLY, c0 - EARLY, far0 - EARLY, [(POOL, pool), (HOP_IN, hop0)])
    projected = project(hidden, kv_weight, local_kv)
    fresh = new_rows(projected, hit_counts, new_lengths, block_len)
    hop_new = over_y(plan, line(new_out, 0, plan.new_units, [(FRESH, fresh)]))
    ready1 = [(POOL, pool), (FRESH, fresh), (HOP_IN, hop1), (HOP_NEW, hop_new)]
    second = lines(z_second, 0, c1, far1, ready1)
    came0 = early + late
    sources0 = [(POOL, pool)] + came0
    back0 = over_y(plan, line(out_out, 0, plan.only_y + out0, sources0))
    sources0 += [(HOP_SAME, back0), (HOP_OUT, back0)]
    done = [
        attend(plan, 0, [s], queries, fresh, sources0, places, hit_counts, new_lengths)
        for s in range(plan.ses)
    ]
    keys = [key for key, _ in second]
    held = lax.optimization_barrier((*done[:-1], *[array for _, array in second]))
    done[:-1] = held[: plan.ses - 1]
    came1 = list(zip(keys, held[plan.ses - 1 :]))
    back1 = over_y(plan, line(out_out, plan.long_out, out1, came1))
    ready1 = [source for source in ready1 if source[0] != HOP_IN]
    return attend(
        plan,
        1,
        list(range(plan.ses)),
        queries,
        fresh,
        ready1 + [(HOP_SAME, back0), (HOP_OUT, back1)] + came1,
        places,
        hit_counts,
        new_lengths,
        arrivals,
        done,
    )


def local(hidden, queries, kv_weight, kv_pool, hit_ids, hit_counts, new_lengths, dest_store):
    reps = lax.axis_size("rep")
    store_count = lax.axis_size("store")
    ses_count, hit_len = hit_ids.shape
    pool_rows, local_kv, _, block_len, _ = kv_pool.shape
    per_dev = hidden.shape[0] // block_len
    assert local_kv == 2 and store_count % NY == 0
    plan = Plan(reps, store_count, ses_count, hit_len, per_dev, pool_rows)
    me = lax.axis_index("store").astype(jnp.int32)
    rep = lax.axis_index("rep").astype(jnp.int32)

    mine = jnp.concatenate([hit_ids, hit_counts[:, None], dest_store], axis=1)
    meta = lax.all_to_all(
        jnp.broadcast_to(mine[None], (reps * store_count,) + mine.shape),
        ("rep", "store"),
        split_axis=0,
        concat_axis=0,
    )
    *tables, chosen = make_schedule(plan, meta.reshape(-1), me, rep)
    args = (hidden, queries, kv_weight, kv_pool, hit_counts, new_lengths, me.reshape(1), tables)
    branches = [functools.partial(run, plan, size) for size in plan.classes]
    attention, written = lax.switch(chosen[0], branches, args)
    return attention, written[None]


def solution(mesh):
    placed = (
        P(("rep", "store"), "tp"),
        P(("rep", "store"), "tp", None),
        P("tp", None, None, None),
        P(("rep", "store"), "tp", None, None, None),
        P(("rep", "store"), None),
        P(("rep", "store")),
        P(("rep", "store")),
        P(("rep", "store"), None),
    )
    return jax.shard_map(
        local,
        mesh=mesh,
        in_specs=placed,
        out_specs=(
            P(("rep", "store"), "tp", None),
            P(("rep", "store"), None, None, "tp", None, None, None),
        ),
        check_vma=False,
    )
```

```python
import functools
import math

import jax
import jax.numpy as jnp
from jax import lax
from jax.experimental import pallas as pl
from jax.experimental.pallas import tpu as pltpu
from jax.sharding import PartitionSpec as P

NY = 2
WCAP = 2
EARLY = 5

theta_base = 500000.0

SPAN_BITS, WIDE_BITS = 16, 5
SPAN = 1 << SPAN_BITS
WIDE = 1 << WIDE_BITS
POOL, FRESH, HOP_IN, HOP_NEW, HOP_SAME, ALONG_Z, HOP_OUT = range(7)


def rotate(keys, positions):
    half = keys.shape[-1] // 2
    steps = jnp.arange(half, dtype=jnp.float32)
    inverse = jnp.exp(steps * (-2.0 * math.log(theta_base) / keys.shape[-1]))
    angles = positions[:, None] * inverse[None, :]
    cosine = jnp.cos(angles)
    sine = jnp.sin(angles)
    first = keys[..., :half]
    second = keys[..., half:]
    return jnp.concatenate(
        [first * cosine - second * sine, second * cosine + first * sine], axis=-1
    )


class Plan:
    def __init__(self, reps, store_count, ses_count, hit_len, per_dev, pool_rows):
        self.reps = reps
        self.stores = store_count
        self.nz = store_count // NY
        self.ses = ses_count
        self.hit_len = hit_len
        self.hits = ses_count * hit_len
        self.per_dev = per_dev
        self.pool_rows = pool_rows
        self.cap = 2 * ((self.hits + store_count - 1) // store_count)
        self.line = hit_len + 1 + per_dev // ses_count
        self.width = ses_count * self.line
        nz, cap = self.nz, self.cap
        both = cap + 2 * WCAP
        self.most = (
            (max(2 * cap, EARLY + cap), (nz - 1) * cap, (nz - 1) * cap),
            (2 * both, (nz - 1) * cap, (nz - 1) * both),
        )
        wanted = (
            ((11, 7, 18), (14, 21, 6)),
            ((12, 7, 19), (15, 21, 6)),
            ((13, 10, 20), (17, 24, 9)),
            self.most,
        )
        self.long_in = max(m[1] for m in self.most)
        self.only_y = 2 * cap
        self.long_out = max(self.only_y + self.most[0][2], self.most[1][2])
        self.new_units = 2 * per_dev
        assert max(m[0] for m in self.most) <= WIDE
        self.factor = -(-SPAN // pool_rows)
        ids = range(store_count * pool_rows)
        assert all((i * self.factor) >> SPAN_BITS == i // pool_rows for i in ids)
        self.classes = [
            tuple(
                tuple(min(a, b) for a, b in zip(size, most))
                for size, most in zip(sizes, self.most)
            )
            for sizes in wanted
        ]


def schedule_kernel(
    plan, me_ref, meta, z_out, in_out, new_out, out_out, places, arrivals, chosen,
    cnt, rows, ranks, over, hop_out_sum, new_base, out_base
):
    S, nz, cap = plan.stores, plan.nz, plan.cap
    me = me_ref[0]
    rep = me_ref[1]
    my_z = me >> 1
    my_y = me & 1
    stride = cap + 1

    def count_at(kind, group, dst, src):
        return ((group * 2 + kind) * S + dst) * S + src

    def units(phase, group, dst, src):
        n = cnt[count_at(0, group, dst, src)]
        return n if phase == 0 else n + 2 * cnt[count_at(1, group, dst, src)]

    def over_at(phase, group, z, zp, ys):
        return (((group * 2 + phase) * nz + z) * nz + zp) * NY + ys

    def store_of(block):
        return (block * plan.factor) >> SPAN_BITS

    def zero(ref, n, value=0):
        def put(i, c):
            for k in range(8):
                ref[i * 8 + k] = jnp.int32(value)
            return c

        lax.fori_loop(0, n // 8, put, 0)
        for k in range(n - n % 8, n):
            ref[k] = jnp.int32(value)

    zero(cnt, plan.reps * 2 * S * S)
    zero(hop_out_sum, plan.reps * 2 * nz * NY)
    zero(z_out, 2 * nz * WIDE, -1)
    zero(in_out, 2 * plan.long_in, -1)
    zero(new_out, plan.new_units, -1)
    zero(out_out, 2 * plan.long_out, -1)

    def scan(group, d):
        g = group * S + d
        base = g * plan.width
        for t in range(plan.ses):
            line = base + t * plan.line
            used = meta[line + plan.hit_len]
            for j in range(plan.hit_len):
                block = meta[line + j]
                store = store_of(block)
                at = count_at(0, group, d, store)
                rank = cnt[at]
                rows[at * stride + jnp.minimum(rank, cap)] = block - store * plan.pool_rows
                ranks[g * plan.hits + t * plan.hit_len + j] = rank
                cnt[at] = rank + (j < used).astype(jnp.int32)
        for j in range(plan.per_dev):
            t, k = divmod(j, plan.per_dev // plan.ses)
            dest = meta[base + t * plan.line + plan.hit_len + 1 + k]
            at = count_at(1, group, dest, d)
            rank = cnt[at]
            rows[at * stride + jnp.minimum(rank, cap)] = j
            cnt[at] = rank + 1

    def scan_group(group, c):
        def one(d, c):
            scan(group, d)
            return c

        return lax.fori_loop(0, S, one, c)

    lax.fori_loop(0, plan.reps, scan_group, 0)

    none = jnp.int32(0)

    def balance(group, z, c):
        c = list(c)
        for phase in range(2):
            longest, most_in = c[2 * phase], c[2 * phase + 1]
            going = [none, none]
            for zp in range(nz):
                a = [
                    [units(phase, group, zp * NY + yd, z * NY + ys) for yd in range(NY)]
                    for ys in range(NY)
                ]
                half = (a[0][0] + a[0][1] + a[1][0] + a[1][1] + 1) >> 1
                half = jnp.maximum(half, plan.classes[0][phase][0])
                if phase == 0:
                    excess = [a[y][y] + a[y][1 - y] - half for y in range(NY)]
                    first = [
                        a[y][1 - y] - jnp.minimum(jnp.maximum(excess[y], 0), a[y][1 - y])
                        for y in range(NY)
                    ]
                else:
                    excess = [a[y][y] + a[1 - y][y] - half for y in range(NY)]
                    first = [
                        jnp.minimum(jnp.maximum(excess[1 - y], 0), a[y][1 - y]) for y in range(NY)
                    ]
                away = zp != z
                for y in range(NY):
                    over[over_at(phase, group, z, zp, y)] = first[y]
                    later = a[1 - y][y] - first[1 - y]
                    own = a[y][y] + first[y]
                    start = jnp.maximum(own, EARLY) if phase == 0 else own
                    hop = later
                    if phase == 1:
                        hits = units(0, group, zp * NY + y, z * NY + 1 - y)
                        hop = jnp.maximum(hits - first[1 - y], 0)
                    end = jnp.where(hop > 0, start + hop, own)
                    if phase == 1:
                        new_hop = later - hop
                        end = end + new_hop
                    longest = jnp.where(away, jnp.maximum(longest, end), longest)
                    going[1 - y] = going[1 - y] + jnp.where(away, hop, 0)
                    at = ((group * 2 + phase) * nz + zp) * NY + y
                    hop_out_sum[at] = hop_out_sum[at] + jnp.where(away, first[y], 0)
            c[2 * phase] = longest
            c[2 * phase + 1] = jnp.maximum(most_in, jnp.maximum(going[0], going[1]))
        return tuple(c)

    need = lax.fori_loop(
        0,
        plan.reps,
        lambda group, c: lax.fori_loop(0, nz, functools.partial(balance, group), c),
        (none,) * 4,
    )
    out_need = []
    for phase in range(2):

        def top(group, c, phase=phase):
            for i in range(nz * NY):
                c = jnp.maximum(c, hop_out_sum[(group * 2 + phase) * nz * NY + i])
            return c

        out_need.append(lax.fori_loop(0, plan.reps, top, none))
    needs = ((need[0], need[1], out_need[0]), (need[2], need[3], out_need[1]))
    pick = jnp.int32(len(plan.classes) - 1)
    for k in reversed(range(len(plan.classes) - 1)):
        fits = jnp.bool_(True)
        for phase in range(2):
            for n, size in zip(needs[phase], plan.classes[k][phase]):
                fits = fits & (n <= size)
        pick = jnp.where(fits, jnp.int32(k), pick)
    chosen[0] = pick

    def amount(phase, dst, src):
        return units(phase, rep, dst, src)

    def first_of(phase, z, zp, ys):
        return over[over_at(phase, rep, z, zp, ys)]

    def own_code(phase, dst, i):
        hit_at = count_at(0, rep, dst, me)
        hit = rows[hit_at * stride + jnp.minimum(i, cap)]
        code = POOL * SPAN + hit * 2 + phase
        if phase == 0:
            return code
        new_at = count_at(1, rep, dst, me)
        n = cnt[new_at]
        k = i - cnt[hit_at]
        head = (k >= n).astype(jnp.int32)
        new = rows[new_at * stride + jnp.clip(k - head * n, 0, cap)]
        return jnp.where(k >= 0, FRESH * SPAN + new * 2 + head, code)

    def fill(ref, start, n, code_of):
        def put(i, c):
            ref[start + i] = code_of(i)
            return c

        lax.fori_loop(0, n, put, 0)

    other = my_z * NY + 1 - my_y
    for phase in range(2):
        in_first = phase * plan.long_in
        out_first = plan.long_out if phase == 1 else plan.only_y

        def each(zp, c, phase=phase, in_first=in_first, out_first=out_first):
            mine, theirs, new_mine, new_theirs, out_mine, out_theirs = c
            away = (zp != my_z).astype(jnp.int32)
            over_there = zp * NY + 1 - my_y
            along = zp * NY + my_y
            first = first_of(phase, my_z, zp, my_y)
            hits = amount(0, over_there, me)
            n = jnp.maximum(hits - first, 0) * away
            fill(in_out, in_first + mine, n, lambda i: own_code(phase, over_there, first + i))
            their_first = first_of(phase, my_z, zp, 1 - my_y)
            their_hits = amount(0, along, other)
            later = jnp.maximum(their_hits - their_first, 0) * away
            new_n, new_later = 0, 0
            if phase == 1:
                skip = jnp.maximum(first, hits)
                new_n = (amount(1, over_there, me) - skip) * away
                fill(new_out, new_mine, new_n, lambda i: own_code(1, over_there, skip + i))
                new_later = amount(1, along, other) - jnp.maximum(their_first, their_hits)
                new_later = new_later * away
            row = (phase * nz + zp) * WIDE
            own = amount(phase, along, me)
            fill(z_out, row, first * away, lambda i: own_code(phase, over_there, i))
            fill(z_out, row + first, own * away, lambda i: own_code(phase, along, i))
            start = first + own
            if phase == 0:
                start = jnp.maximum(start, EARLY)
            fill(z_out, row + start, later, lambda i: HOP_IN * SPAN + theirs + i)
            if phase == 1:
                fill(
                    z_out,
                    row + start + later,
                    new_later,
                    lambda i: HOP_NEW * SPAN + new_theirs + i,
                )
            out_n = first_of(phase, zp, my_z, my_y) * away
            fill(
                out_out, out_first + out_mine, out_n, lambda i: ALONG_Z * SPAN + zp * WIDE + i
            )
            out_base[phase * nz + zp] = out_theirs
            out_later = first_of(phase, zp, my_z, 1 - my_y) * away
            return (
                mine + n,
                theirs + later,
                new_mine + new_n,
                new_theirs + new_later,
                out_mine + out_n,
                out_theirs + out_later,
            )

        _, _, new_mine, new_theirs, _, _ = lax.fori_loop(0, nz, each, (none,) * 6)
        hits = amount(0, other, me)
        fill(out_out, phase * cap, hits, lambda i, p=phase: own_code(p, other, i))
        if phase == 1:
            fill(new_out, new_mine, amount(1, other, me) - hits, lambda i: own_code(1, other, hits + i))
            new_base[0] = new_theirs

    def place(phase, store, i):
        zs = store >> 1
        straight = (store & 1) == my_y
        first = first_of(phase, zs, my_z, my_y)
        held = first + i
        crossing = first_of(phase, zs, my_z, 1 - my_y)
        start = first + amount(phase, me, zs * NY + my_y)
        if phase == 0:
            start = jnp.maximum(start, EARLY)
        slot = start + i - crossing
        if phase == 1:
            hits = amount(0, me, store)
            new_start = start + jnp.maximum(hits - crossing, 0)
            slot = jnp.where(i < hits, slot, new_start + i - jnp.maximum(hits, crossing))
        slot = jnp.where(straight, held, slot)
        code = ALONG_Z * SPAN + zs * WIDE + slot
        late = jnp.logical_not(straight) & (i < crossing)
        back = HOP_OUT * SPAN + (plan.only_y if phase == 0 else 0) + out_base[phase * nz + zs]
        code = jnp.where(late, back + i, code)
        near = HOP_SAME * SPAN + phase * cap + i
        if phase == 1:
            near = jnp.where(i < hits, near, HOP_NEW * SPAN + new_base[0] + i - hits)
        code = jnp.where(zs == my_z, near, code)
        return jnp.where(store == me, own_code(phase, me, i), code)

    here = rep * S + me

    for t in range(plan.ses):

        def own_hit(j, c, t=t):
            store = store_of(meta[here * plan.width + t * plan.line + j])
            i = t * plan.hit_len + j
            rank = ranks[here * plan.hits + i]
            for phase in range(2):
                places[phase * plan.hits + i] = place(phase, store, rank)
            return c

        lax.fori_loop(0, plan.hit_len, own_hit, 0)

    def own_new(i, c):
        sender = i >> 1
        rank = i & 1
        n = cnt[count_at(1, rep, me, sender)]
        first = cnt[count_at(0, rep, me, sender)] + rank
        for head in range(2):
            code = place(1, sender, first + head * n)
            arrivals[i * 2 + head] = jnp.where(rank < n, code, -1)
        return c

    lax.fori_loop(0, S * WCAP, own_new, 0)


def make_schedule(plan, meta, me, rep):
    smem = pl.BlockSpec(memory_space=pltpu.SMEM)
    S, nz, reps = plan.stores, plan.nz, plan.reps
    ints = lambda *shape: jax.ShapeDtypeStruct(shape, jnp.int32)
    room = lambda n: pltpu.SMEM((n,), jnp.int32)
    return pl.pallas_call(
        functools.partial(schedule_kernel, plan),
        out_shape=(
            ints(2 * nz * WIDE),
            ints(2 * plan.long_in),
            ints(plan.new_units),
            ints(2 * plan.long_out),
            ints(2 * plan.hits),
            ints(S * WCAP * 2),
            ints(1),
        ),
        in_specs=[smem, smem],
        out_specs=(smem,) * 7,
        scratch_shapes=[
            room(reps * 2 * S * S),
            room(reps * 2 * S * S * (plan.cap + 1)),
            room(reps * S * plan.hits),
            room(reps * 2 * nz * nz * NY),
            room(reps * 2 * nz * NY),
            room(1),
            room(2 * nz),
        ],
        name="schedule",
    )(jnp.stack([me, rep]), meta)


def for_source(code, sources, act):
    kind = code >> SPAN_BITS
    slot = code & (SPAN - 1)
    for source, ref in sources.items():
        if source == ALONG_Z:
            z = slot >> WIDE_BITS
            at = slot & (WIDE - 1)
            ends = [first for first, _ in ref[1:]] + [WIDE]
            for (first, part), end in zip(ref, ends):

                @pl.when((code >= 0) & (kind == source) & (at >= first) & (at < end))
                def _():
                    act(part.at[z, at - first])
        else:

            @pl.when((code >= 0) & (kind == source))
            def _():
                act(ref.at[slot])


def pick_kernel(names, firsts, lines, first, table, *refs):
    ins, (out, sem) = refs[: len(names)], refs[len(names) :]
    sources = {}
    for name, start, ref in zip(names, firsts, ins):
        if name == ALONG_Z:
            sources.setdefault(name, []).append((start, ref))
        else:
            sources[name] = ref
    slots = out.shape[1]
    for start in (True, False):
        for line in range(lines):

            def one(i, c):
                code = table[first + line * WIDE + i]
                dst = out.at[line, i]
                if start:
                    for_source(
                        code, sources, lambda src: pltpu.make_async_copy(src, dst, sem).start()
                    )
                else:

                    @pl.when(code >= 0)
                    def _():
                        pltpu.make_async_copy(dst, dst, sem).wait()

                return c

            lax.fori_loop(0, slots, one, 0)


def pick(table, lines, first, slots, sources, unit, dtype):
    smem = pl.BlockSpec(memory_space=pltpu.SMEM)
    far = pl.BlockSpec(memory_space=pl.ANY)
    names = [s[0] for s in sources]
    firsts = [s[1] for s in sources]
    size = lines * slots * math.prod(unit) * 2
    return pl.pallas_call(
        functools.partial(pick_kernel, names, firsts, lines, first),
        out_shape=jax.ShapeDtypeStruct((lines, slots) + unit, dtype),
        in_specs=[smem] + [far] * len(sources),
        out_specs=pl.BlockSpec(memory_space=pltpu.VMEM),
        scratch_shapes=[pltpu.SemaphoreType.DMA],
        compiler_params=pltpu.CompilerParams(vmem_limit_bytes=32 * 1024 * 1024),
        cost_estimate=pl.CostEstimate(flops=0, bytes_accessed=3 * size, transcendentals=0),
        name="pick",
    )(table, *[s[2] for s in sources])


ROWS = 256


def attend_kernel(
    plan, head, sessions, group, names, firsts, places, hit_counts, lengths, arrivals, *refs
):
    last = arrivals is not None
    refs = list(refs)
    queries, fresh_near = refs[:2]
    ins = refs[2 : 2 + len(names)]
    refs = refs[2 + len(names) :]
    if last:
        done, (out, written) = refs[: plan.ses], refs[plan.ses : plan.ses + 2]
        refs = refs[plan.ses + 2 :]
        held, vals, scores, weights, mixed, zero, kv_sem, out_sem = refs
    else:
        mixed, held, vals, scores, weights, kv_sem = refs
    sources = {}
    for name, start, ref in zip(names, firsts, ins):
        if name == ALONG_Z:
            sources.setdefault(name, []).append((start, ref))
        else:
            sources[name] = ref
    tokens, heads, dim = queries.shape
    block = fresh_near.shape[2]
    new_len = tokens // len(sessions)
    new_blocks = new_len // block
    pre = new_blocks * block
    scale = math.log2(math.e) / math.sqrt(dim)

    def fetch(s):
        def one(j, c):
            dst = held.at[s, j]
            for_source(
                places[(head * plan.ses + s) * plan.hit_len + j],
                sources,
                lambda src: pltpu.make_async_copy(src, dst, kv_sem.at[s]).start(),
            )
            return c

        lax.fori_loop(0, hit_counts[s], one, 0)

    def await_fetch(s):
        def one(j, c):
            dst = held.at[s, j]
            pltpu.make_async_copy(dst, dst, kv_sem.at[s]).wait()
            return c

        lax.fori_loop(0, hit_counts[s], one, 0)

    for s in sessions:
        fetch(s)

    if last:
        zero[...] = jnp.zeros(zero.shape, zero.dtype)

        def put_written(start):
            def one(i, c):
                dst = written.at[i >> 2, (i >> 1) & 1, i & 1]
                code = arrivals[i]
                if start:
                    for_source(
                        code,
                        sources,
                        lambda src: pltpu.make_async_copy(src, dst, out_sem.at[0]).start(),
                    )

                    @pl.when(code < 0)
                    def _():
                        pltpu.make_async_copy(zero, dst, out_sem.at[0]).start()
                else:
                    pltpu.make_async_copy(zero, dst, out_sem.at[0]).wait()
                return c

            lax.fori_loop(0, plan.stores * WCAP * 2, one, 0)

        put_written(True)

    vals[:, dim:] = jnp.ones((vals.shape[0], vals.shape[1] - dim), vals.dtype)
    step_tokens = ROWS // group
    assert ROWS % group == 0 and new_len % (2 * step_tokens) == 0 and new_blocks % 2 == 0 and plan.hit_len % 2 == 0

    def session(s, c):
        at_session = s - sessions[0]
        await_fetch(s)
        used = hit_counts[s]
        for b in range(new_blocks):
            vals[pl.ds(b * block, block), :dim] = fresh_near[(s * new_blocks + b) * 2 + head, 1]
        for j in range(plan.hit_len):

            @pl.when(j < used)
            def _():
                vals[pl.ds(pre + j * block, block), :dim] = held[s, j, 1]

            @pl.when(j >= used)
            def _():
                vals[pl.ds(pre + j * block, block), :dim] = jnp.zeros((block, dim), vals.dtype)

        def two_tiles(u, c, pairs, low):
            width = pre + 2 * pairs * block
            lane = lax.broadcasted_iota(jnp.int32, (ROWS, block), 1)

            def begin(part):
                rt = u * 2 + part
                here = pl.ds(at_session * new_len + rt * step_tokens, step_tokens)
                q = queries[here].astype(jnp.float32)[:, head * group : (head + 1) * group, :]
                token = rt * step_tokens + lax.broadcasted_iota(
                    jnp.int32, (step_tokens, group, block), 0
                ).reshape(ROWS, block)
                return here, q.reshape(ROWS, dim).astype(jnp.bfloat16), token

            def score(part, q, token, i, tops):
                if i < new_blocks // 2:
                    keys = [fresh_near[(s * new_blocks + 2 * i + b) * 2 + head, 0] for b in range(2)]
                else:
                    j = 2 * i - new_blocks
                    keys = [held[s, j, 0], held[s, j + 1, 0]]
                both = lax.dot_general(
                    q,
                    jnp.concatenate(keys, axis=0),
                    (((1,), (1,)), ((), ())),
                    preferred_element_type=jnp.float32,
                )
                halves = [both[:, :block], both[:, block:]]
                if i < new_blocks // 2:
                    halves = [
                        jnp.where((2 * i + b) * block + lane <= token, halves[b], -jnp.inf)
                        for b in range(2)
                    ]
                else:
                    for b in range(2):
                        if j + b >= low:
                            halves[b] = jnp.where(j + b < used, halves[b], -jnp.inf)
                for b in range(2):
                    at = (2 * i + b) * block
                    scores[part, :, at : at + block] = halves[b]
                top = jnp.maximum(halves[0], halves[1])
                return top if tops is None else jnp.maximum(tops, top)

            def weigh(part, peak, i):
                for b in range(2):
                    at = (2 * i + b) * block
                    x = scores[part, :, at : at + block] * scale - peak
                    weights[part, :, at : at + block] = jnp.exp2(x).astype(jnp.bfloat16)

            def finish(part, here, token):
                both = jnp.dot(
                    weights[part, :, :width], vals[:width, :], preferred_element_type=jnp.float32
                )
                result = both[:, :dim] / both[:, dim:]
                result = jnp.where(token < lengths[s], result, 0.0)
                mixed[here] = result.reshape(step_tokens, group, dim)

            def peak_of(tops):
                return jnp.max(tops, axis=1, keepdims=True) * scale

            chunks = range(width // (2 * block))
            here0, q0, token0 = begin(0)
            here1, q1, token1 = begin(1)
            tops0, tops1 = None, None
            for i in chunks:
                tops0 = score(0, q0, token0, i, tops0)
            peak0 = peak_of(tops0)
            for i in chunks:
                tops1 = score(1, q1, token1, i, tops1)
                weigh(0, peak0, i)
            peak1 = peak_of(tops1)
            finish(0, here0, token0)
            for i in chunks:
                weigh(1, peak1, i)
            finish(1, here1, token1)
            return c

        low = plan.hit_len // 2
        for pairs in range(plan.hit_len // 4 + 1, plan.hit_len // 2 + 1):

            @pl.when((used >= low) & (used <= 2 * pairs))
            def _():
                lax.fori_loop(
                    0,
                    new_len // (2 * step_tokens),
                    functools.partial(two_tiles, pairs=pairs, low=low),
                    0,
                )

            low = 2 * pairs + 1

        if last:
            span = pl.ds(pl.multiple_of(at_session * new_len, new_len), new_len)
            for k in range(plan.ses):

                @pl.when(s == k)
                def _():
                    whole = jnp.concatenate([done[k][...], mixed[span]], axis=1)
                    out[span] = whole.astype(jnp.bfloat16)

        return c

    lax.fori_loop(sessions[0], sessions[-1] + 1, session, 0)
    if last:
        put_written(False)


def attend(
    plan, head, sessions, queries, fresh, sources, places, counts, lengths, arrivals=None, done=None
):
    smem = pl.BlockSpec(memory_space=pltpu.SMEM)
    near = pl.BlockSpec(memory_space=pltpu.VMEM)
    far = pl.BlockSpec(memory_space=pl.ANY)
    tokens, heads, dim = queries.shape
    group = heads // 2
    unit = fresh.shape[1:]
    block = unit[1]
    new_len = tokens // plan.ses
    rows = plan.hit_len * block + new_len
    last = done is not None
    names = [x[0] for x in sources]
    firsts = [x[1] for x in sources]
    kernel = functools.partial(attend_kernel, plan, head, sessions, group, names, firsts)
    scratch = [
        pltpu.VMEM((plan.ses, plan.hit_len) + unit, jnp.bfloat16),
        pltpu.VMEM((rows, 2 * dim), jnp.bfloat16),
        pltpu.VMEM((2, ROWS, rows), jnp.float32),
        pltpu.VMEM((2, ROWS, rows), jnp.bfloat16),
    ]
    mine = len(sessions) * new_len
    partial_out = jax.ShapeDtypeStruct((mine, group, dim), jnp.float32)
    arrays = [x[2] for x in sources]
    if last:
        call = dict(
            out_shape=(
                jax.ShapeDtypeStruct(queries.shape, jnp.bfloat16),
                jax.ShapeDtypeStruct((plan.stores, WCAP, 2) + unit, jnp.bfloat16),
            ),
            in_specs=[smem] * 4 + [near, near] + [far] * len(sources) + [near] * plan.ses,
            out_specs=(near, far),
            scratch_shapes=scratch
            + [
                pltpu.VMEM(partial_out.shape, jnp.float32),
                pltpu.VMEM(unit, jnp.bfloat16),
                pltpu.SemaphoreType.DMA((plan.ses,)),
                pltpu.SemaphoreType.DMA((1,)),
            ],
        )
        args = [places, counts, lengths, arrivals, queries, fresh] + arrays + list(done)
        body = kernel
    else:
        assert len(sessions) == 1
        part = pl.BlockSpec((new_len, heads, dim), lambda i: (sessions[0], 0, 0))
        call = dict(
            grid=(1,),
            out_shape=partial_out,
            in_specs=[smem] * 3 + [part, near] + [far] * len(sources),
            out_specs=near,
            scratch_shapes=scratch + [pltpu.SemaphoreType.DMA((plan.ses,))],
        )
        args = [places, counts, lengths, queries, fresh] + arrays
        body = lambda p, c, n, *refs: kernel(p, c, n, None, *refs)
    return pl.pallas_call(
        body,
        compiler_params=pltpu.CompilerParams(vmem_limit_bytes=40 * 1024 * 1024),
        cost_estimate=pl.CostEstimate(
            flops=4 * mine * group * rows * dim,
            bytes_accessed=8 * 1024 * 1024,
            transcendentals=mine * group * rows,
        ),
        name="attend",
        **call,
    )(*args)


def project(hidden, kv_weight, local_kv):
    part = jnp.einsum("ta,abhd->hbtd", hidden, kv_weight, preferred_element_type=jnp.float32)
    mine = lax.axis_index("tp")
    tp = lax.axis_size("tp")
    projected = lax.dynamic_slice_in_dim(part, mine * local_kv, local_kv, 0)
    for away in range(1, tp):
        other = lax.dynamic_slice_in_dim(part, ((mine + away) % tp) * local_kv, local_kv, 0)
        projected = projected + lax.ppermute(
            other, "tp", [(i, (i + away) % tp) for i in range(tp)]
        )
    return projected


def new_rows(projected, hit_counts, new_lengths, block_len):
    local_kv, _, tokens, dim = projected.shape
    ses_count = hit_counts.shape[0]
    new_len = tokens // ses_count
    within = jnp.arange(tokens) % new_len
    start_pos = jnp.repeat(hit_counts, new_len, total_repeat_length=tokens)
    live_len = jnp.repeat(new_lengths, new_len, total_repeat_length=tokens)
    positions = (start_pos * block_len + within).astype(jnp.float32)
    rotated = rotate(projected[:, 0], positions)
    fresh = jnp.stack([rotated, projected[:, 1]], axis=1).astype(jnp.bfloat16)
    fresh = jnp.where((within < live_len)[None, None, :, None], fresh, jnp.zeros((), jnp.bfloat16))
    fresh = fresh.reshape(local_kv, 2, tokens // block_len, block_len, dim)
    fresh = jnp.transpose(fresh, (2, 0, 1, 3, 4))
    return fresh.reshape((-1,) + fresh.shape[2:])


def along_z(plan, units):
    columns = [[z * NY + y for z in range(plan.nz)] for y in range(NY)]
    return lax.all_to_all(
        units, "store", split_axis=0, concat_axis=0, axis_index_groups=columns, tiled=True
    )


def over_y(plan, units):
    return lax.ppermute(units[0], "store", [(s, s ^ 1) for s in range(plan.stores)])


def run(plan, size, args):
    hidden, queries, kv_weight, kv_pool, hit_counts, new_lengths, tables = args
    z_out, in_out, new_out, out_out, places, arrivals = tables
    pool_rows, local_kv, _, block_len, dim = kv_pool.shape
    unit = kv_pool.shape[2:]
    pool = kv_pool.reshape((pool_rows * local_kv,) + unit)
    take = functools.partial(pick, unit=unit, dtype=kv_pool.dtype)
    z_second = plan.nz * WIDE
    (c0, in0, out0), (c1, in1, out1) = size

    early = along_z(plan, take(z_out, plan.nz, 0, EARLY, [(POOL, 0, pool)]))
    hop0 = over_y(plan, take(in_out, 1, 0, in0, [(POOL, 0, pool)]))
    sent1 = take(in_out, 1, plan.long_in, in1, [(POOL, 0, pool)])
    hop1 = over_y(plan, sent1)
    hop0, _ = lax.optimization_barrier((hop0, sent1))
    late = along_z(
        plan, take(z_out, plan.nz, EARLY, c0 - EARLY, [(POOL, 0, pool), (HOP_IN, 0, hop0)])
    )
    projected = project(hidden, kv_weight, local_kv)
    fresh = new_rows(projected, hit_counts, new_lengths, block_len)
    hop_new = over_y(plan, take(new_out, 1, 0, plan.new_units, [(FRESH, 0, fresh)]))
    ready1 = [(POOL, 0, pool), (FRESH, 0, fresh), (HOP_IN, 0, hop1), (HOP_NEW, 0, hop_new)]
    second = along_z(plan, take(z_out, plan.nz, z_second, c1, ready1))
    came0 = [(ALONG_Z, 0, early), (ALONG_Z, EARLY, late)]
    sources0 = [(POOL, 0, pool)] + came0
    back0 = over_y(plan, take(out_out, 1, 0, plan.only_y + out0, sources0))
    sources0 += [(HOP_SAME, 0, back0), (HOP_OUT, 0, back0)]
    done = [
        attend(plan, 0, [s], queries, fresh, sources0, places, hit_counts, new_lengths)
        for s in range(plan.ses)
    ]
    *first, second = lax.optimization_barrier((*done[:-1], second))
    done[:-1] = first
    came1 = [(ALONG_Z, 0, second)]
    back1 = over_y(plan, take(out_out, 1, plan.long_out, out1, came1))
    ready1 = [source for source in ready1 if source[0] != HOP_IN]
    return attend(
        plan,
        1,
        list(range(plan.ses)),
        queries,
        fresh,
        ready1 + [(HOP_SAME, 0, back0), (HOP_OUT, 0, back1)] + came1,
        places,
        hit_counts,
        new_lengths,
        arrivals,
        done,
    )


def local(hidden, queries, kv_weight, kv_pool, hit_ids, hit_counts, new_lengths, dest_store):
    reps = lax.axis_size("rep")
    store_count = lax.axis_size("store")
    ses_count, hit_len = hit_ids.shape
    pool_rows, local_kv, _, block_len, _ = kv_pool.shape
    per_dev = hidden.shape[0] // block_len
    assert local_kv == 2 and store_count % NY == 0
    plan = Plan(reps, store_count, ses_count, hit_len, per_dev, pool_rows)
    me = lax.axis_index("store").astype(jnp.int32)
    rep = lax.axis_index("rep").astype(jnp.int32)

    mine = jnp.concatenate([hit_ids, hit_counts[:, None], dest_store], axis=1)
    meta = lax.all_to_all(
        jnp.broadcast_to(mine[None], (reps * store_count,) + mine.shape),
        ("rep", "store"),
        split_axis=0,
        concat_axis=0,
    )
    *tables, chosen = make_schedule(plan, meta.reshape(-1), me, rep)
    args = (hidden, queries, kv_weight, kv_pool, hit_counts, new_lengths, tables)
    branches = [functools.partial(run, plan, size) for size in plan.classes]
    attention, written = lax.switch(chosen[0], branches, args)
    return attention, written[None]


def solution(mesh):
    placed = (
        P(("rep", "store"), "tp"),
        P(("rep", "store"), "tp", None),
        P("tp", None, None, None),
        P(("rep", "store"), "tp", None, None, None),
        P(("rep", "store"), None),
        P(("rep", "store")),
        P(("rep", "store")),
        P(("rep", "store"), None),
    )
    return jax.shard_map(
        local,
        mesh=mesh,
        in_specs=placed,
        out_specs=(
            P(("rep", "store"), "tp", None),
            P(("rep", "store"), None, None, "tp", None, None, None),
        ),
        check_vma=False,
    )
```

```python
import functools
import math

import jax
import jax.numpy as jnp
from jax import lax
from jax.experimental import pallas as pl
from jax.experimental.pallas import tpu as pltpu
from jax.sharding import PartitionSpec as P

NY = 2
WCAP = 2
EARLY = 5

theta_base = 500000.0

SPAN_BITS, WIDE_BITS = 16, 5
SPAN = 1 << SPAN_BITS
WIDE = 1 << WIDE_BITS
POOL, FRESH, HOP_IN, HOP_NEW, HOP_SAME, ALONG_Z, HOP_OUT = range(7)


def rotate(keys, positions):
    half = keys.shape[-1] // 2
    steps = jnp.arange(half, dtype=jnp.float32)
    inverse = jnp.exp(steps * (-2.0 * math.log(theta_base) / keys.shape[-1]))
    angles = positions[:, None] * inverse[None, :]
    cosine = jnp.cos(angles)
    sine = jnp.sin(angles)
    first = keys[..., :half]
    second = keys[..., half:]
    return jnp.concatenate(
        [first * cosine - second * sine, second * cosine + first * sine], axis=-1
    )


class Plan:
    def __init__(self, reps, store_count, ses_count, hit_len, per_dev, pool_rows):
        self.reps = reps
        self.stores = store_count
        self.nz = store_count // NY
        self.ses = ses_count
        self.hit_len = hit_len
        self.hits = ses_count * hit_len
        self.per_dev = per_dev
        self.pool_rows = pool_rows
        self.cap = 2 * ((self.hits + store_count - 1) // store_count)
        self.line = hit_len + 1 + per_dev // ses_count
        self.width = ses_count * self.line
        nz, cap = self.nz, self.cap
        both = cap + 2 * WCAP
        self.most = (
            (max(2 * cap, EARLY + cap), (nz - 1) * cap, (nz - 1) * cap),
            (2 * both, (nz - 1) * cap, (nz - 1) * both),
        )
        wanted = (
            ((11, 10, 16), (14, 17, 10)),
            ((12, 11, 17), (15, 18, 11)),
            ((13, 13, 18), (17, 21, 13)),
            self.most,
        )
        self.long_in = max(m[1] for m in self.most)
        self.only_y = 2 * cap
        self.long_out = max(self.only_y + self.most[0][2], self.most[1][2])
        self.new_units = 2 * per_dev
        assert max(m[0] for m in self.most) <= WIDE
        self.factor = -(-SPAN // pool_rows)
        ids = range(store_count * pool_rows)
        assert all((i * self.factor) >> SPAN_BITS == i // pool_rows for i in ids)
        self.classes = [
            tuple(
                tuple(min(a, b) for a, b in zip(size, most))
                for size, most in zip(sizes, self.most)
            )
            for sizes in wanted
        ]


def schedule_kernel(
    plan, me_ref, meta, z_out, in_out, new_out, out_out, places, arrivals, chosen,
    cnt, rows, ranks, over, hop_out_sum, new_base, out_base
):
    S, nz, cap = plan.stores, plan.nz, plan.cap
    me = me_ref[0]
    rep = me_ref[1]
    my_z = me >> 1
    my_y = me & 1
    stride = cap + 1

    def count_at(kind, group, dst, src):
        return ((group * 2 + kind) * S + dst) * S + src

    def units(phase, group, dst, src):
        n = cnt[count_at(0, group, dst, src)]
        return n if phase == 0 else n + 2 * cnt[count_at(1, group, dst, src)]

    def over_at(phase, group, z, zp, ys):
        return (((group * 2 + phase) * nz + z) * nz + zp) * NY + ys

    def store_of(block):
        return (block * plan.factor) >> SPAN_BITS

    def zero(ref, n, value=0):
        def put(i, c):
            for k in range(8):
                ref[i * 8 + k] = jnp.int32(value)
            return c

        lax.fori_loop(0, n // 8, put, 0)
        for k in range(n - n % 8, n):
            ref[k] = jnp.int32(value)

    zero(cnt, plan.reps * 2 * S * S)
    zero(hop_out_sum, plan.reps * 2 * nz * NY)
    zero(z_out, 2 * nz * WIDE, -1)
    zero(in_out, 2 * plan.long_in, -1)
    zero(new_out, plan.new_units, -1)
    zero(out_out, 2 * plan.long_out, -1)

    def scan(group, d):
        g = group * S + d
        base = g * plan.width
        for t in range(plan.ses):
            line = base + t * plan.line
            used = meta[line + plan.hit_len]
            for j in range(plan.hit_len):
                block = meta[line + j]
                store = store_of(block)
                at = count_at(0, group, d, store)
                rank = cnt[at]
                rows[at * stride + jnp.minimum(rank, cap)] = block - store * plan.pool_rows
                ranks[g * plan.hits + t * plan.hit_len + j] = rank
                cnt[at] = rank + (j < used).astype(jnp.int32)
        for j in range(plan.per_dev):
            t, k = divmod(j, plan.per_dev // plan.ses)
            dest = meta[base + t * plan.line + plan.hit_len + 1 + k]
            at = count_at(1, group, dest, d)
            rank = cnt[at]
            rows[at * stride + jnp.minimum(rank, cap)] = j
            cnt[at] = rank + 1

    def scan_group(group, c):
        def one(d, c):
            scan(group, d)
            return c

        return lax.fori_loop(0, S, one, c)

    lax.fori_loop(0, plan.reps, scan_group, 0)

    none = jnp.int32(0)

    def balance(group, z, c):
        c = list(c)
        for phase in range(2):
            longest, most_in = c[2 * phase], c[2 * phase + 1]
            going = [none, none]
            for zp in range(nz):
                a = [
                    [units(phase, group, zp * NY + yd, z * NY + ys) for yd in range(NY)]
                    for ys in range(NY)
                ]
                half = (a[0][0] + a[0][1] + a[1][0] + a[1][1] + 1) >> 1
                if phase == 0:
                    excess = [a[y][y] + a[y][1 - y] - half for y in range(NY)]
                    first = [
                        a[y][1 - y] - jnp.minimum(jnp.maximum(excess[y], 0), a[y][1 - y])
                        for y in range(NY)
                    ]
                else:
                    excess = [a[y][y] + a[1 - y][y] - half for y in range(NY)]
                    first = [
                        jnp.minimum(jnp.maximum(excess[1 - y], 0), a[y][1 - y]) for y in range(NY)
                    ]
                away = zp != z
                for y in range(NY):
                    over[over_at(phase, group, z, zp, y)] = first[y]
                    later = a[1 - y][y] - first[1 - y]
                    own = a[y][y] + first[y]
                    start = jnp.maximum(own, EARLY) if phase == 0 else own
                    hop = later
                    if phase == 1:
                        hits = units(0, group, zp * NY + y, z * NY + 1 - y)
                        hop = jnp.maximum(hits - first[1 - y], 0)
                    end = jnp.where(hop > 0, start + hop, own)
                    if phase == 1:
                        new_hop = later - hop
                        end = end + new_hop
                    longest = jnp.where(away, jnp.maximum(longest, end), longest)
                    going[1 - y] = going[1 - y] + jnp.where(away, hop, 0)
                    at = ((group * 2 + phase) * nz + zp) * NY + y
                    hop_out_sum[at] = hop_out_sum[at] + jnp.where(away, first[y], 0)
            c[2 * phase] = longest
            c[2 * phase + 1] = jnp.maximum(most_in, jnp.maximum(going[0], going[1]))
        return tuple(c)

    need = lax.fori_loop(
        0,
        plan.reps,
        lambda group, c: lax.fori_loop(0, nz, functools.partial(balance, group), c),
        (none,) * 4,
    )
    out_need = []
    for phase in range(2):

        def top(group, c, phase=phase):
            for i in range(nz * NY):
                c = jnp.maximum(c, hop_out_sum[(group * 2 + phase) * nz * NY + i])
            return c

        out_need.append(lax.fori_loop(0, plan.reps, top, none))
    needs = ((need[0], need[1], out_need[0]), (need[2], need[3], out_need[1]))
    pick = jnp.int32(len(plan.classes) - 1)
    for k in reversed(range(len(plan.classes) - 1)):
        fits = jnp.bool_(True)
        for phase in range(2):
            for n, size in zip(needs[phase], plan.classes[k][phase]):
                fits = fits & (n <= size)
        pick = jnp.where(fits, jnp.int32(k), pick)
    chosen[0] = pick

    def amount(phase, dst, src):
        return units(phase, rep, dst, src)

    def first_of(phase, z, zp, ys):
        return over[over_at(phase, rep, z, zp, ys)]

    def own_code(phase, dst, i):
        hit_at = count_at(0, rep, dst, me)
        hit = rows[hit_at * stride + jnp.minimum(i, cap)]
        code = POOL * SPAN + hit * 2 + phase
        if phase == 0:
            return code
        new_at = count_at(1, rep, dst, me)
        n = cnt[new_at]
        k = i - cnt[hit_at]
        head = (k >= n).astype(jnp.int32)
        new = rows[new_at * stride + jnp.clip(k - head * n, 0, cap)]
        return jnp.where(k >= 0, FRESH * SPAN + new * 2 + head, code)

    def fill(ref, start, n, code_of):
        def put(i, c):
            ref[start + i] = code_of(i)
            return c

        lax.fori_loop(0, n, put, 0)

    other = my_z * NY + 1 - my_y
    for phase in range(2):
        in_first = phase * plan.long_in
        out_first = plan.long_out if phase == 1 else plan.only_y

        def each(zp, c, phase=phase, in_first=in_first, out_first=out_first):
            mine, theirs, new_mine, new_theirs, out_mine, out_theirs = c
            away = (zp != my_z).astype(jnp.int32)
            over_there = zp * NY + 1 - my_y
            along = zp * NY + my_y
            first = first_of(phase, my_z, zp, my_y)
            hits = amount(0, over_there, me)
            n = jnp.maximum(hits - first, 0) * away
            fill(in_out, in_first + mine, n, lambda i: own_code(phase, over_there, first + i))
            their_first = first_of(phase, my_z, zp, 1 - my_y)
            their_hits = amount(0, along, other)
            later = jnp.maximum(their_hits - their_first, 0) * away
            new_n, new_later = 0, 0
            if phase == 1:
                skip = jnp.maximum(first, hits)
                new_n = (amount(1, over_there, me) - skip) * away
                fill(new_out, new_mine, new_n, lambda i: own_code(1, over_there, skip + i))
                new_later = amount(1, along, other) - jnp.maximum(their_first, their_hits)
                new_later = new_later * away
            row = (phase * nz + zp) * WIDE
            own = amount(phase, along, me)
            fill(z_out, row, first * away, lambda i: own_code(phase, over_there, i))
            fill(z_out, row + first, own * away, lambda i: own_code(phase, along, i))
            start = first + own
            if phase == 0:
                start = jnp.maximum(start, EARLY)
            fill(z_out, row + start, later, lambda i: HOP_IN * SPAN + theirs + i)
            if phase == 1:
                fill(
                    z_out,
                    row + start + later,
                    new_later,
                    lambda i: HOP_NEW * SPAN + new_theirs + i,
                )
            out_n = first_of(phase, zp, my_z, my_y) * away
            fill(
                out_out, out_first + out_mine, out_n, lambda i: ALONG_Z * SPAN + zp * WIDE + i
            )
            out_base[phase * nz + zp] = out_theirs
            out_later = first_of(phase, zp, my_z, 1 - my_y) * away
            return (
                mine + n,
                theirs + later,
                new_mine + new_n,
                new_theirs + new_later,
                out_mine + out_n,
                out_theirs + out_later,
            )

        _, _, new_mine, new_theirs, _, _ = lax.fori_loop(0, nz, each, (none,) * 6)
        hits = amount(0, other, me)
        fill(out_out, phase * cap, hits, lambda i, p=phase: own_code(p, other, i))
        if phase == 1:
            fill(new_out, new_mine, amount(1, other, me) - hits, lambda i: own_code(1, other, hits + i))
            new_base[0] = new_theirs

    def place(phase, store, i):
        zs = store >> 1
        straight = (store & 1) == my_y
        first = first_of(phase, zs, my_z, my_y)
        held = first + i
        crossing = first_of(phase, zs, my_z, 1 - my_y)
        start = first + amount(phase, me, zs * NY + my_y)
        if phase == 0:
            start = jnp.maximum(start, EARLY)
        slot = start + i - crossing
        if phase == 1:
            hits = amount(0, me, store)
            new_start = start + jnp.maximum(hits - crossing, 0)
            slot = jnp.where(i < hits, slot, new_start + i - jnp.maximum(hits, crossing))
        slot = jnp.where(straight, held, slot)
        code = ALONG_Z * SPAN + zs * WIDE + slot
        late = jnp.logical_not(straight) & (i < crossing)
        back = HOP_OUT * SPAN + (plan.only_y if phase == 0 else 0) + out_base[phase * nz + zs]
        code = jnp.where(late, back + i, code)
        near = HOP_SAME * SPAN + phase * cap + i
        if phase == 1:
            near = jnp.where(i < hits, near, HOP_NEW * SPAN + new_base[0] + i - hits)
        code = jnp.where(zs == my_z, near, code)
        return jnp.where(store == me, own_code(phase, me, i), code)

    here = rep * S + me

    for t in range(plan.ses):

        def own_hit(j, c, t=t):
            store = store_of(meta[here * plan.width + t * plan.line + j])
            i = t * plan.hit_len + j
            rank = ranks[here * plan.hits + i]
            for phase in range(2):
                places[phase * plan.hits + i] = place(phase, store, rank)
            return c

        lax.fori_loop(0, plan.hit_len, own_hit, 0)

    def own_new(i, c):
        sender = i >> 1
        rank = i & 1
        n = cnt[count_at(1, rep, me, sender)]
        first = cnt[count_at(0, rep, me, sender)] + rank
        for head in range(2):
            code = place(1, sender, first + head * n)
            arrivals[i * 2 + head] = jnp.where(rank < n, code, -1)
        return c

    lax.fori_loop(0, S * WCAP, own_new, 0)


def make_schedule(plan, meta, me, rep):
    smem = pl.BlockSpec(memory_space=pltpu.SMEM)
    S, nz, reps = plan.stores, plan.nz, plan.reps
    ints = lambda *shape: jax.ShapeDtypeStruct(shape, jnp.int32)
    room = lambda n: pltpu.SMEM((n,), jnp.int32)
    return pl.pallas_call(
        functools.partial(schedule_kernel, plan),
        out_shape=(
            ints(2 * nz * WIDE),
            ints(2 * plan.long_in),
            ints(plan.new_units),
            ints(2 * plan.long_out),
            ints(2 * plan.hits),
            ints(S * WCAP * 2),
            ints(1),
        ),
        in_specs=[smem, smem],
        out_specs=(smem,) * 7,
        scratch_shapes=[
            room(reps * 2 * S * S),
            room(reps * 2 * S * S * (plan.cap + 1)),
            room(reps * S * plan.hits),
            room(reps * 2 * nz * nz * NY),
            room(reps * 2 * nz * NY),
            room(1),
            room(2 * nz),
        ],
        name="schedule",
    )(jnp.stack([me, rep]), meta)


def for_source(code, sources, act):
    kind = code >> SPAN_BITS
    slot = code & (SPAN - 1)
    for source, ref in sources.items():
        if source == ALONG_Z:
            z = slot >> WIDE_BITS
            at = slot & (WIDE - 1)
            ends = [first for first, _ in ref[1:]] + [WIDE]
            for (first, part), end in zip(ref, ends):

                @pl.when((code >= 0) & (kind == source) & (at >= first) & (at < end))
                def _():
                    act(part.at[z, at - first])
        else:

            @pl.when((code >= 0) & (kind == source))
            def _():
                act(ref.at[slot])


def pick_kernel(names, firsts, lines, first, table, *refs):
    ins, (out, sem) = refs[: len(names)], refs[len(names) :]
    sources = {}
    for name, start, ref in zip(names, firsts, ins):
        if name == ALONG_Z:
            sources.setdefault(name, []).append((start, ref))
        else:
            sources[name] = ref
    slots = out.shape[1]
    for start in (True, False):
        for line in range(lines):

            def one(i, c):
                code = table[first + line * WIDE + i]
                dst = out.at[line, i]
                if start:
                    for_source(
                        code, sources, lambda src: pltpu.make_async_copy(src, dst, sem).start()
                    )
                else:

                    @pl.when(code >= 0)
                    def _():
                        pltpu.make_async_copy(dst, dst, sem).wait()

                return c

            lax.fori_loop(0, slots, one, 0)


def pick(table, lines, first, slots, sources, unit, dtype):
    smem = pl.BlockSpec(memory_space=pltpu.SMEM)
    far = pl.BlockSpec(memory_space=pl.ANY)
    names = [s[0] for s in sources]
    firsts = [s[1] for s in sources]
    size = lines * slots * math.prod(unit) * 2
    return pl.pallas_call(
        functools.partial(pick_kernel, names, firsts, lines, first),
        out_shape=jax.ShapeDtypeStruct((lines, slots) + unit, dtype),
        in_specs=[smem] + [far] * len(sources),
        out_specs=pl.BlockSpec(memory_space=pltpu.VMEM),
        scratch_shapes=[pltpu.SemaphoreType.DMA],
        compiler_params=pltpu.CompilerParams(vmem_limit_bytes=32 * 1024 * 1024),
        cost_estimate=pl.CostEstimate(flops=0, bytes_accessed=3 * size, transcendentals=0),
        name="pick",
    )(table, *[s[2] for s in sources])


ROWS = 256


def attend_kernel(
    plan, head, sessions, group, names, firsts, places, hit_counts, lengths, arrivals, *refs
):
    last = arrivals is not None
    refs = list(refs)
    queries, fresh_near = refs[:2]
    ins = refs[2 : 2 + len(names)]
    refs = refs[2 + len(names) :]
    if last:
        done, (out, written) = refs[: plan.ses], refs[plan.ses : plan.ses + 2]
        refs = refs[plan.ses + 2 :]
        held, vals, scores, weights, mixed, zero, kv_sem, out_sem = refs
    else:
        mixed, held, vals, scores, weights, kv_sem = refs
    sources = {}
    for name, start, ref in zip(names, firsts, ins):
        if name == ALONG_Z:
            sources.setdefault(name, []).append((start, ref))
        else:
            sources[name] = ref
    tokens, heads, dim = queries.shape
    block = fresh_near.shape[2]
    new_len = tokens // len(sessions)
    new_blocks = new_len // block
    pre = new_blocks * block
    scale = math.log2(math.e) / math.sqrt(dim)

    def fetch(s):
        def one(j, c):
            dst = held.at[s, j]
            for_source(
                places[(head * plan.ses + s) * plan.hit_len + j],
                sources,
                lambda src: pltpu.make_async_copy(src, dst, kv_sem.at[s]).start(),
            )
            return c

        lax.fori_loop(0, hit_counts[s], one, 0)

    def await_fetch(s):
        def one(j, c):
            dst = held.at[s, j]
            pltpu.make_async_copy(dst, dst, kv_sem.at[s]).wait()
            return c

        lax.fori_loop(0, hit_counts[s], one, 0)

    for s in sessions:
        fetch(s)

    if last:
        zero[...] = jnp.zeros(zero.shape, zero.dtype)

        def put_written(start):
            def one(i, c):
                dst = written.at[i >> 2, (i >> 1) & 1, i & 1]
                code = arrivals[i]
                if start:
                    for_source(
                        code,
                        sources,
                        lambda src: pltpu.make_async_copy(src, dst, out_sem.at[0]).start(),
                    )

                    @pl.when(code < 0)
                    def _():
                        pltpu.make_async_copy(zero, dst, out_sem.at[0]).start()
                else:
                    pltpu.make_async_copy(zero, dst, out_sem.at[0]).wait()
                return c

            lax.fori_loop(0, plan.stores * WCAP * 2, one, 0)

        put_written(True)

    vals[:, dim:] = jnp.ones((vals.shape[0], vals.shape[1] - dim), vals.dtype)
    step_tokens = ROWS // group
    assert ROWS % group == 0 and new_len % (2 * step_tokens) == 0 and new_blocks % 2 == 0 and plan.hit_len % 2 == 0

    def session(s, c):
        at_session = s - sessions[0]
        await_fetch(s)
        used = hit_counts[s]
        for b in range(new_blocks):
            vals[pl.ds(b * block, block), :dim] = fresh_near[(s * new_blocks + b) * 2 + head, 1]
        for j in range(plan.hit_len):

            @pl.when(j < used)
            def _():
                vals[pl.ds(pre + j * block, block), :dim] = held[s, j, 1]

            @pl.when(j >= used)
            def _():
                vals[pl.ds(pre + j * block, block), :dim] = jnp.zeros((block, dim), vals.dtype)

        def two_tiles(u, c, pairs, low):
            width = pre + 2 * pairs * block
            lane = lax.broadcasted_iota(jnp.int32, (ROWS, block), 1)

            def begin(part):
                rt = u * 2 + part
                here = pl.ds(at_session * new_len + rt * step_tokens, step_tokens)
                q = queries[here].astype(jnp.float32)[:, head * group : (head + 1) * group, :]
                token = rt * step_tokens + lax.broadcasted_iota(
                    jnp.int32, (step_tokens, group, block), 0
                ).reshape(ROWS, block)
                return here, q.reshape(ROWS, dim).astype(jnp.bfloat16), token

            def score(part, q, token, i, tops):
                if i < new_blocks // 2:
                    keys = [fresh_near[(s * new_blocks + 2 * i + b) * 2 + head, 0] for b in range(2)]
                else:
                    j = 2 * i - new_blocks
                    keys = [held[s, j, 0], held[s, j + 1, 0]]
                both = lax.dot_general(
                    q,
                    jnp.concatenate(keys, axis=0),
                    (((1,), (1,)), ((), ())),
                    preferred_element_type=jnp.float32,
                )
                halves = [both[:, :block], both[:, block:]]
                if i < new_blocks // 2:
                    halves = [
                        jnp.where((2 * i + b) * block + lane <= token, halves[b], -jnp.inf)
                        for b in range(2)
                    ]
                else:
                    for b in range(2):
                        if j + b >= low:
                            halves[b] = jnp.where(j + b < used, halves[b], -jnp.inf)
                for b in range(2):
                    at = (2 * i + b) * block
                    scores[part, :, at : at + block] = halves[b]
                top = jnp.maximum(halves[0], halves[1])
                return top if tops is None else jnp.maximum(tops, top)

            def weigh(part, peak, i):
                for b in range(2):
                    at = (2 * i + b) * block
                    x = scores[part, :, at : at + block] * scale - peak
                    weights[part, :, at : at + block] = jnp.exp2(x).astype(jnp.bfloat16)

            def finish(part, here, token):
                both = jnp.dot(
                    weights[part, :, :width], vals[:width, :], preferred_element_type=jnp.float32
                )
                result = both[:, :dim] / both[:, dim:]
                result = jnp.where(token < lengths[s], result, 0.0)
                mixed[here] = result.reshape(step_tokens, group, dim)

            def peak_of(tops):
                return jnp.max(tops, axis=1, keepdims=True) * scale

            chunks = range(width // (2 * block))
            here0, q0, token0 = begin(0)
            here1, q1, token1 = begin(1)
            tops0, tops1 = None, None
            for i in chunks:
                tops0 = score(0, q0, token0, i, tops0)
            peak0 = peak_of(tops0)
            for i in chunks:
                tops1 = score(1, q1, token1, i, tops1)
                weigh(0, peak0, i)
            peak1 = peak_of(tops1)
            finish(0, here0, token0)
            for i in chunks:
                weigh(1, peak1, i)
            finish(1, here1, token1)
            return c

        low = plan.hit_len // 2
        for pairs in range(plan.hit_len // 4 + 1, plan.hit_len // 2 + 1):

            @pl.when((used >= low) & (used <= 2 * pairs))
            def _():
                lax.fori_loop(
                    0,
                    new_len // (2 * step_tokens),
                    functools.partial(two_tiles, pairs=pairs, low=low),
                    0,
                )

            low = 2 * pairs + 1

        if last:
            span = pl.ds(pl.multiple_of(at_session * new_len, new_len), new_len)
            for k in range(plan.ses):

                @pl.when(s == k)
                def _():
                    whole = jnp.concatenate([done[k][...], mixed[span]], axis=1)
                    out[span] = whole.astype(jnp.bfloat16)

        return c

    lax.fori_loop(sessions[0], sessions[-1] + 1, session, 0)
    if last:
        put_written(False)


def attend(
    plan, head, sessions, queries, fresh, sources, places, counts, lengths, arrivals=None, done=None
):
    smem = pl.BlockSpec(memory_space=pltpu.SMEM)
    near = pl.BlockSpec(memory_space=pltpu.VMEM)
    far = pl.BlockSpec(memory_space=pl.ANY)
    tokens, heads, dim = queries.shape
    group = heads // 2
    unit = fresh.shape[1:]
    block = unit[1]
    new_len = tokens // plan.ses
    rows = plan.hit_len * block + new_len
    last = done is not None
    names = [x[0] for x in sources]
    firsts = [x[1] for x in sources]
    kernel = functools.partial(attend_kernel, plan, head, sessions, group, names, firsts)
    scratch = [
        pltpu.VMEM((plan.ses, plan.hit_len) + unit, jnp.bfloat16),
        pltpu.VMEM((rows, 2 * dim), jnp.bfloat16),
        pltpu.VMEM((2, ROWS, rows), jnp.float32),
        pltpu.VMEM((2, ROWS, rows), jnp.bfloat16),
    ]
    mine = len(sessions) * new_len
    partial_out = jax.ShapeDtypeStruct((mine, group, dim), jnp.float32)
    arrays = [x[2] for x in sources]
    if last:
        call = dict(
            out_shape=(
                jax.ShapeDtypeStruct(queries.shape, jnp.bfloat16),
                jax.ShapeDtypeStruct((plan.stores, WCAP, 2) + unit, jnp.bfloat16),
            ),
            in_specs=[smem] * 4 + [near, near] + [far] * len(sources) + [near] * plan.ses,
            out_specs=(near, far),
            scratch_shapes=scratch
            + [
                pltpu.VMEM(partial_out.shape, jnp.float32),
                pltpu.VMEM(unit, jnp.bfloat16),
                pltpu.SemaphoreType.DMA((plan.ses,)),
                pltpu.SemaphoreType.DMA((1,)),
            ],
        )
        args = [places, counts, lengths, arrivals, queries, fresh] + arrays + list(done)
        body = kernel
    else:
        assert len(sessions) == 1
        part = pl.BlockSpec((new_len, heads, dim), lambda i: (sessions[0], 0, 0))
        call = dict(
            grid=(1,),
            out_shape=partial_out,
            in_specs=[smem] * 3 + [part, near] + [far] * len(sources),
            out_specs=near,
            scratch_shapes=scratch + [pltpu.SemaphoreType.DMA((plan.ses,))],
        )
        args = [places, counts, lengths, queries, fresh] + arrays
        body = lambda p, c, n, *refs: kernel(p, c, n, None, *refs)
    return pl.pallas_call(
        body,
        compiler_params=pltpu.CompilerParams(vmem_limit_bytes=40 * 1024 * 1024),
        cost_estimate=pl.CostEstimate(
            flops=4 * mine * group * rows * dim,
            bytes_accessed=8 * 1024 * 1024,
            transcendentals=mine * group * rows,
        ),
        name="attend",
        **call,
    )(*args)


def project(hidden, kv_weight, local_kv):
    part = jnp.einsum("ta,abhd->hbtd", hidden, kv_weight, preferred_element_type=jnp.float32)
    mine = lax.axis_index("tp")
    tp = lax.axis_size("tp")
    projected = lax.dynamic_slice_in_dim(part, mine * local_kv, local_kv, 0)
    for away in range(1, tp):
        other = lax.dynamic_slice_in_dim(part, ((mine + away) % tp) * local_kv, local_kv, 0)
        projected = projected + lax.ppermute(
            other, "tp", [(i, (i + away) % tp) for i in range(tp)]
        )
    return projected


def new_rows(projected, hit_counts, new_lengths, block_len):
    local_kv, _, tokens, dim = projected.shape
    ses_count = hit_counts.shape[0]
    new_len = tokens // ses_count
    within = jnp.arange(tokens) % new_len
    start_pos = jnp.repeat(hit_counts, new_len, total_repeat_length=tokens)
    live_len = jnp.repeat(new_lengths, new_len, total_repeat_length=tokens)
    positions = (start_pos * block_len + within).astype(jnp.float32)
    rotated = rotate(projected[:, 0], positions)
    fresh = jnp.stack([rotated, projected[:, 1]], axis=1).astype(jnp.bfloat16)
    fresh = jnp.where((within < live_len)[None, None, :, None], fresh, jnp.zeros((), jnp.bfloat16))
    fresh = fresh.reshape(local_kv, 2, tokens // block_len, block_len, dim)
    fresh = jnp.transpose(fresh, (2, 0, 1, 3, 4))
    return fresh.reshape((-1,) + fresh.shape[2:])


def along_z(plan, units):
    columns = [[z * NY + y for z in range(plan.nz)] for y in range(NY)]
    return lax.all_to_all(
        units, "store", split_axis=0, concat_axis=0, axis_index_groups=columns, tiled=True
    )


def over_y(plan, units):
    return lax.ppermute(units[0], "store", [(s, s ^ 1) for s in range(plan.stores)])


def run(plan, size, args):
    hidden, queries, kv_weight, kv_pool, hit_counts, new_lengths, tables = args
    z_out, in_out, new_out, out_out, places, arrivals = tables
    pool_rows, local_kv, _, block_len, dim = kv_pool.shape
    unit = kv_pool.shape[2:]
    pool = kv_pool.reshape((pool_rows * local_kv,) + unit)
    take = functools.partial(pick, unit=unit, dtype=kv_pool.dtype)
    z_second = plan.nz * WIDE
    (c0, in0, out0), (c1, in1, out1) = size

    early = along_z(plan, take(z_out, plan.nz, 0, EARLY, [(POOL, 0, pool)]))
    hop0 = over_y(plan, take(in_out, 1, 0, in0, [(POOL, 0, pool)]))
    sent1 = take(in_out, 1, plan.long_in, in1, [(POOL, 0, pool)])
    hop1 = over_y(plan, sent1)
    hop0, _ = lax.optimization_barrier((hop0, sent1))
    late = along_z(
        plan, take(z_out, plan.nz, EARLY, c0 - EARLY, [(POOL, 0, pool), (HOP_IN, 0, hop0)])
    )
    projected = project(hidden, kv_weight, local_kv)
    fresh = new_rows(projected, hit_counts, new_lengths, block_len)
    hop_new = over_y(plan, take(new_out, 1, 0, plan.new_units, [(FRESH, 0, fresh)]))
    ready1 = [(POOL, 0, pool), (FRESH, 0, fresh), (HOP_IN, 0, hop1), (HOP_NEW, 0, hop_new)]
    second = along_z(plan, take(z_out, plan.nz, z_second, c1, ready1))
    came0 = [(ALONG_Z, 0, early), (ALONG_Z, EARLY, late)]
    sources0 = [(POOL, 0, pool)] + came0
    back0 = over_y(plan, take(out_out, 1, 0, plan.only_y + out0, sources0))
    sources0 += [(HOP_SAME, 0, back0), (HOP_OUT, 0, back0)]
    done = [
        attend(plan, 0, [s], queries, fresh, sources0, places, hit_counts, new_lengths)
        for s in range(plan.ses)
    ]
    *first, second = lax.optimization_barrier((*done[:-1], second))
    done[:-1] = first
    came1 = [(ALONG_Z, 0, second)]
    back1 = over_y(plan, take(out_out, 1, plan.long_out, out1, came1))
    ready1 = [source for source in ready1 if source[0] != HOP_IN]
    return attend(
        plan,
        1,
        list(range(plan.ses)),
        queries,
        fresh,
        ready1 + [(HOP_SAME, 0, back0), (HOP_OUT, 0, back1)] + came1,
        places,
        hit_counts,
        new_lengths,
        arrivals,
        done,
    )


def local(hidden, queries, kv_weight, kv_pool, hit_ids, hit_counts, new_lengths, dest_store):
    reps = lax.axis_size("rep")
    store_count = lax.axis_size("store")
    ses_count, hit_len = hit_ids.shape
    pool_rows, local_kv, _, block_len, _ = kv_pool.shape
    per_dev = hidden.shape[0] // block_len
    assert local_kv == 2 and store_count % NY == 0
    plan = Plan(reps, store_count, ses_count, hit_len, per_dev, pool_rows)
    me = lax.axis_index("store").astype(jnp.int32)
    rep = lax.axis_index("rep").astype(jnp.int32)

    mine = jnp.concatenate([hit_ids, hit_counts[:, None], dest_store], axis=1)
    meta = lax.all_to_all(
        jnp.broadcast_to(mine[None], (reps * store_count,) + mine.shape),
        ("rep", "store"),
        split_axis=0,
        concat_axis=0,
    )
    *tables, chosen = make_schedule(plan, meta.reshape(-1), me, rep)
    args = (hidden, queries, kv_weight, kv_pool, hit_counts, new_lengths, tables)
    branches = [functools.partial(run, plan, size) for size in plan.classes]
    attention, written = lax.switch(chosen[0], branches, args)
    return attention, written[None]


def solution(mesh):
    placed = (
        P(("rep", "store"), "tp"),
        P(("rep", "store"), "tp", None),
        P("tp", None, None, None),
        P(("rep", "store"), "tp", None, None, None),
        P(("rep", "store"), None),
        P(("rep", "store")),
        P(("rep", "store")),
        P(("rep", "store"), None),
    )
    return jax.shard_map(
        local,
        mesh=mesh,
        in_specs=placed,
        out_specs=(
            P(("rep", "store"), "tp", None),
            P(("rep", "store"), None, None, "tp", None, None, None),
        ),
        check_vma=False,
    )
```
